32 devices in a mesh: group: 2 (over y), resp: 4 (over z), tensor: 4 (over x, core).
Axes of the slice: x: 2, y: 2, z: 4, core: 2. Of those that a mesh axis runs over, the one named last changes fastest.
Arguments:
- queries: bfloat16 [8, 512, 8192], P(('group', 'resp'), None, 'tensor'), parts along dimension 0, may hold values from -50 to 50
- resp_keys: bfloat16 [8, 512, 1024], P(('group', 'resp'), None, 'tensor'), parts along dimension 0, may hold values from -6 to 6
- resp_values: bfloat16 [8, 512, 1024], P(('group', 'resp'), None, 'tensor'), parts along dimension 0, may hold values from -6 to 6
- prompt_keys: bfloat16 [4096, 1024], P(('group', 'resp', 'tensor')), parts along dimension 0, may hold values from -7 to 7
- prompt_values: bfloat16 [4096, 1024], P(('group', 'resp', 'tensor')), parts along dimension 0, may hold values from -6 to 6
- out_grad: bfloat16 [8, 512, 8192], P(('group', 'resp'), None, 'tensor'), parts along dimension 0, may hold values from -6 to 6
- lengths: int32 [8], P(('group', 'resp')), parts along dimension 0, may hold values from 1 to 512, 1280 in all
Outputs:
- attended: bfloat16 [8, 512, 8192], P(('group', 'resp'), None, 'tensor'), parts along dimension 0
- query_grad: bfloat16 [8, 512, 8192], P(('group', 'resp'), None, 'tensor'), parts along dimension 0
- resp_key_grad: bfloat16 [8, 512, 1024], P(('group', 'resp'), None, 'tensor'), parts along dimension 0
- resp_value_grad: bfloat16 [8, 512, 1024], P(('group', 'resp'), None, 'tensor'), parts along dimension 0
- prompt_key_grad: float32 [4096, 1024], P(('group', 'resp', 'tensor')), parts along dimension 0
- prompt_value_grad: float32 [4096, 1024], P(('group', 'resp', 'tensor')), parts along dimension 0
The draws below stay inside these ranges and needn't reach their ends.
There are 2 independent parts, one for each index of `group`. The reference program is written for one: setup_inputs(seed, part) draws one part's arguments, and reference() takes and returns one part's arrays. A program takes and returns all parts, laid end to end along the dimension named above; each array names one. Nothing has to cross between parts.
Inputs may be any that keep to these rules, and one draw needn't show every extreme that they name: For each prompt group separately, its 4 lengths sum to 1280, and one of them is exactly 512; the table lists the groups one after another.
All inputs are finite; a program needn't handle non-finite values.
Results may differ from the reference program's by a relative error of at most 0.012.
The reference program's roundings to bfloat16 on the way count: a program that leaves them out, or rounds other values in their place, can miss the bound.
Values may be sent and summed in bfloat16 or wider, within the bound.
No kernel may reach another device: no remote copies, remote signals or barrier semaphores. Data moves between devices by JAX's collectives and lax.ppermute only.
A program may use at most 64 MiB of HBM per device.

```python
import math
import jax
import jax.numpy as jnp
import numpy as np
from jax import lax

QH = 64
KVH = 8
HD = 128
PROMPT = 2048
RLEN = 512
RESPONSES = 4


def shared_keys(key, pair_share):
    key_normal = jax.random.fold_in(key, 0)
    gaussian = jnp.clip(jax.random.normal(key_normal, (PROMPT, KVH * HD), jnp.float32), -6.0, 6.0)
    raw_keys = gaussian
    row_ids = jnp.arange(PROMPT)
    follower = (row_ids % 16 == 1).astype(jnp.float32)[:, None] * pair_share
    return (1.0 - follower) * raw_keys


def draw_prompt_keys(key, part):
    base_keys = shared_keys(key, 0.0)
    return base_keys.astype(jnp.bfloat16)


def draw_queries(key, part):
    key = jax.random.fold_in(key, 23)
    key_drawn = jax.random.fold_in(key, 0)
    result = jnp.clip(2.0 * jax.random.normal(key_drawn, (RESPONSES, RLEN, QH, HD), jnp.float32), -12.0, 12.0)
    return result.reshape(RESPONSES, RLEN, QH * HD).astype(jnp.bfloat16)


def level_of(key, shape, shards, smallest, top_value):
    level = 1.0
    for axis_at, blocks in shards:
        draws = jax.random.uniform(jax.random.fold_in(jax.random.fold_in(key, 6), axis_at), (blocks,), jnp.float32, smallest / len(shards), top_value / len(shards))
        level = level * jnp.repeat(jnp.exp(draws), shape[axis_at] // blocks).reshape((-1,) + (1,) * (len(shape) - 1 - axis_at))
    return level


def profile(number_of, total, bound, skew):
    loads = [(1 << 20) // math.isqrt(rank ** skew) + 1 for rank in range(2, number_of + 1)]
    surplus, counts = total - bound - (number_of - 1), [1] * (number_of - 1)
    while surplus > 0:
        movable = [i for i in range(number_of - 1) if counts[i] < bound]
        pool, budget = sum([loads[i] for i in movable]), surplus
        for i in movable:
            extra = min(bound - counts[i], max(1, budget * loads[i] // pool), surplus)
            counts[i] = counts[i] + extra
            surplus = surplus - extra
    return np.array([bound] + counts)


def uneven_parts(stream_key, count, total, limit, slope):
    if count == 2:
        one = jax.random.randint(stream_key, (), max(1, total - limit), min(limit, total - 1) + 1)
        return jnp.stack([one, total - one])
    sizes = jnp.asarray(profile(count, total, limit, slope), jnp.int32)
    couples = (count - 1) // 2
    giver, taker = sizes[1:1 + 2 * couples:2], sizes[2:2 + 2 * couples:2]
    margin = jnp.minimum(giver - 1, limit - taker)
    moved = jax.random.randint(jax.random.fold_in(stream_key, 1), (couples,), 0, 1 << 20) % (margin + 1)
    sizes = sizes.at[1:1 + 2 * couples:2].set(giver - moved).at[2:2 + 2 * couples:2].set(taker + moved)
    return sizes[jax.random.permutation(jax.random.fold_in(stream_key, 2), count)]


def noise(stream_key, extent, spread, reach, cuts=(), kind=jnp.bfloat16):
    values = spread * jax.random.normal(stream_key, extent, jnp.float32)
    if cuts:
        values = values * level_of(stream_key, extent, cuts, -0.22, 0.18)
    return jnp.clip(values, -reach, reach).astype(kind)


def setup_inputs(seed: int = 0, part: int = 0) -> dict:
    keys = jax.random.split(jax.random.key(seed), 8)
    part_splits = jax.random.split(jax.random.fold_in(keys[7], part), 8)
    queries = draw_queries(jax.random.fold_in(jax.random.fold_in(keys[7], part), 71), part)
    resp_keys = noise(part_splits[1], (RESPONSES, RLEN, KVH * HD), 1.0, 6.0, ((0, 4), (2, 4)))
    resp_values = noise(part_splits[2], (RESPONSES, RLEN, KVH * HD), 1.0, 6.0, ((0, 4), (2, 4)))
    prompt_keys = draw_prompt_keys(jax.random.fold_in(jax.random.fold_in(keys[7], part), 71), part)
    prompt_values = noise(part_splits[4], (PROMPT, KVH * HD), 1.0, 6.0, ((0, 16),))
    out_grad = noise(part_splits[5], (RESPONSES, RLEN, QH * HD), 1.0, 6.0, ((0, 4), (2, 4)))
    lengths = uneven_parts(part_splits[6], RESPONSES, RESPONSES * 5 * RLEN // 8, RLEN, 1).astype(jnp.int32)
    return dict(queries=queries, resp_keys=resp_keys, resp_values=resp_values, prompt_keys=prompt_keys, prompt_values=prompt_values, out_grad=out_grad, lengths=lengths)


def rounded(values):
    return lax.optimization_barrier(values.astype(jnp.bfloat16)).astype(jnp.float32)


def pair_terms(query_rows, grad_rows, key_resp, value_resp, key_prompt, value_prompt, resp_length):
    factor = HD ** -0.5
    positions = jnp.arange(RLEN, dtype=jnp.int32)
    live_rows = positions < resp_length
    allowed = (positions[None, :] <= positions[:, None]) & (positions[None, :] < resp_length)
    query_wide = query_rows.astype(jnp.float32)
    key_prompt_wide = key_prompt.astype(jnp.float32)
    value_prompt_wide = value_prompt.astype(jnp.float32)
    key_resp_wide = key_resp.astype(jnp.float32)
    value_resp_wide = value_resp.astype(jnp.float32)
    score_prompt = jnp.einsum("gqd,kd->gqk", query_wide, key_prompt_wide) * factor
    score_resp = jnp.where(allowed[None], jnp.einsum("gqd,kd->gqk", query_wide, key_resp_wide) * factor, -jnp.inf)
    row_top = jnp.maximum(jnp.max(score_prompt, -1), jnp.max(score_resp, -1))
    exp_prompt = jnp.exp(score_prompt - row_top[..., None])
    exp_resp = jnp.exp(score_resp - row_top[..., None])
    row_total = jnp.sum(exp_prompt, -1) + jnp.sum(exp_resp, -1)
    frac_prompt = exp_prompt / row_total[..., None]
    frac_resp = exp_resp / row_total[..., None]
    weight_prompt = rounded(frac_prompt)
    weight_resp = rounded(frac_resp)
    mixture = jnp.einsum("gqk,kd->gqd", weight_prompt, value_prompt_wide) + jnp.einsum("gqk,kd->gqd", weight_resp, value_resp_wide)
    attended = jnp.where(live_rows[None, :, None], mixture, 0.0).astype(jnp.bfloat16)
    live_grad = jnp.where(live_rows[None, :, None], grad_rows, jnp.zeros_like(grad_rows)).astype(jnp.float32)
    row_delta = jnp.sum(live_grad * lax.optimization_barrier(attended).astype(jnp.float32), -1)
    sgrad_prompt = rounded(frac_prompt * (jnp.einsum("gqd,kd->gqk", live_grad, value_prompt_wide) - row_delta[..., None]))
    sgrad_resp = rounded(frac_resp * (jnp.einsum("gqd,kd->gqk", live_grad, value_resp_wide) - row_delta[..., None]))
    query_grad = (factor * (jnp.einsum("gqk,kd->gqd", sgrad_prompt, key_prompt_wide) + jnp.einsum("gqk,kd->gqd", sgrad_resp, key_resp_wide))).astype(jnp.bfloat16)
    key_grad_resp = factor * jnp.einsum("gqk,gqd->kd", sgrad_resp, query_wide)
    value_grad_resp = jnp.einsum("gqk,gqd->kd", weight_resp, live_grad)
    key_grad_prompt = factor * jnp.einsum("gqk,gqd->kd", sgrad_prompt, query_wide)
    value_grad_prompt = jnp.einsum("gqk,gqd->kd", weight_prompt, live_grad)
    return attended, query_grad, key_grad_resp, value_grad_resp, key_grad_prompt, value_grad_prompt


def reference(queries, resp_keys, resp_values, prompt_keys, prompt_values, out_grad, lengths):
    heads_per = QH // KVH
    query_blocks = queries.reshape(RESPONSES, RLEN, KVH, heads_per, HD).transpose(0, 2, 3, 1, 4)
    grad_blocks = out_grad.reshape(RESPONSES, RLEN, KVH, heads_per, HD).transpose(0, 2, 3, 1, 4)
    key_blocks = resp_keys.reshape(RESPONSES, RLEN, KVH, HD).transpose(0, 2, 1, 3)
    value_blocks = resp_values.reshape(RESPONSES, RLEN, KVH, HD).transpose(0, 2, 1, 3)
    prompt_key_heads = prompt_keys.reshape(PROMPT, KVH, HD).transpose(1, 0, 2)
    prompt_value_heads = prompt_values.reshape(PROMPT, KVH, HD).transpose(1, 0, 2)

    def per_response(sums, inputs):
        query_set, grad_set, key_set, value_set, resp_length = inputs

        def per_head(pieces):
            return pair_terms(pieces[0], pieces[1], pieces[2], pieces[3], pieces[4], pieces[5], resp_length)

        results = lax.map(per_head, (query_set, grad_set, key_set, value_set, prompt_key_heads, prompt_value_heads))
        new_sums = (sums[0] + results[4], sums[1] + results[5])
        return new_sums, (results[0], results[1], results[2], results[3])

    start_sums = (jnp.zeros((KVH, PROMPT, HD), jnp.float32), jnp.zeros((KVH, PROMPT, HD), jnp.float32))
    final_sums, outputs = lax.scan(per_response, start_sums, (query_blocks, grad_blocks, key_blocks, value_blocks, lengths))
    attended = outputs[0].transpose(0, 3, 1, 2, 4).reshape(RESPONSES, RLEN, QH * HD)
    query_grad = outputs[1].transpose(0, 3, 1, 2, 4).reshape(RESPONSES, RLEN, QH * HD)
    resp_key_grad = outputs[2].transpose(0, 2, 1, 3).reshape(RESPONSES, RLEN, KVH * HD).astype(jnp.bfloat16)
    resp_value_grad = outputs[3].transpose(0, 2, 1, 3).reshape(RESPONSES, RLEN, KVH * HD).astype(jnp.bfloat16)
    prompt_key_grad = final_sums[0].transpose(1, 0, 2).reshape(PROMPT, KVH * HD)
    prompt_value_grad = final_sums[1].transpose(1, 0, 2).reshape(PROMPT, KVH * HD)
    return attended, query_grad, resp_key_grad, resp_value_grad, prompt_key_grad, prompt_value_grad
```

```python
import functools
import math

import jax
import jax.numpy as jnp
from jax import lax
from jax.experimental import pallas as pl
from jax.experimental.pallas import tpu as pltpu
from jax.sharding import PartitionSpec as P

HD = 128
BF16 = jnp.bfloat16
F32 = jnp.float32


def dot(a, b):
    return jnp.dot(a, b, preferred_element_type=F32)


def attention_kernel(
    parts,
    heads_per,
    len_ref,
    q_ref,
    g_ref,
    cache_ref,
    kr_ref,
    vr_ref,
    *rest,
):
    (
        out_ref,
        dq_ref,
        dkr_ref,
        dvr_ref,
        dcache_ref,
        keys,
        values,
        keys_t,
        values_t,
        exps,
        dprobs,
        weights,
        dk_sum,
        dv_sum,
        tops,
        sums,
    ) = rest[-16:]
    rows = q_ref.shape[0]
    part_rows = cache_ref.shape[2]
    prompt_rows = parts * part_rows
    chunk = rows
    prompt_chunks = prompt_rows // chunk
    chunks = prompt_chunks + 1
    factor = HD ** (-0.5)
    factor2 = factor * math.log2(math.e)
    length = len_ref[0]
    step = pl.program_id(0)

    @pl.when(step == 0)
    def _():
        for p in range(parts):
            at = pl.ds(p * part_rows, part_rows)
            keys[at, :] = cache_ref[p, 0]
            values[at, :] = cache_ref[p, 1]
            keys_t[:, at] = cache_ref[p, 0].astype(F32).T.astype(BF16)
            values_t[:, at] = cache_ref[p, 1].astype(F32).T.astype(BF16)
        at = pl.ds(prompt_rows, rows)
        keys[at, :] = kr_ref[...]
        values[at, :] = vr_ref[...]
        keys_t[:, at] = kr_ref[...].astype(F32).T.astype(BF16)
        values_t[:, at] = vr_ref[...].astype(F32).T.astype(BF16)
        dk_sum[...] = jnp.zeros_like(dk_sum)
        dv_sum[...] = jnp.zeros_like(dv_sum)

    live_rows = lax.broadcasted_iota(jnp.int32, (rows, HD), 0) < length
    live_grad = jnp.where(live_rows, g_ref[...].astype(F32), 0.0)
    grad = live_grad.astype(BF16)
    grad_t32 = live_grad.T
    grad_t = grad_t32.astype(BF16)
    query = q_ref[...]
    query_t = query.astype(F32).T.astype(BF16)

    def first(c, masked):
        at = pl.ds(pl.multiple_of(c * chunk, chunk), chunk)
        score = dot(keys[at, :], query_t)
        if masked:
            j = lax.broadcasted_iota(jnp.int32, (chunk, rows), 0)
            i = lax.broadcasted_iota(jnp.int32, (chunk, rows), 1)
            score = jnp.where((j <= i) & (j < length), score, -jnp.inf)
        top = jnp.max(score, axis=0, keepdims=True) * factor2
        exp = jnp.exp2(score * factor2 - top)
        exps[at, :] = exp
        tops[pl.ds(c, 1), :] = top
        sums[pl.ds(c, 1), :] = jnp.sum(exp, axis=0, keepdims=True)
        dprobs[at, :] = dot(values[at, :], grad_t)

    def first_step(c, carry):
        first(c, False)
        return carry

    lax.fori_loop(0, prompt_chunks, first_step, 0)
    first(prompt_chunks, True)

    top = jnp.max(tops[:chunks, :], axis=0, keepdims=True)
    scale = jnp.exp2(tops[:chunks, :] - top)
    total = jnp.sum(scale * sums[:chunks, :], axis=0, keepdims=True)
    sums[:chunks, :] = scale / total

    def second_step(c, mixture):
        at = pl.ds(pl.multiple_of(c * chunk, chunk), chunk)
        weight = (exps[at, :] * sums[pl.ds(c, 1), :]).astype(BF16)
        weights[at, :] = weight
        return mixture + dot(values_t[:, at], weight)

    mixture = lax.fori_loop(0, chunks, second_step, jnp.zeros((HD, rows), F32))
    live_lanes = lax.broadcasted_iota(jnp.int32, (HD, rows), 1) < length
    attended = jnp.where(live_lanes, mixture, 0.0).astype(BF16).astype(F32)
    out_ref[...] = attended.T.astype(BF16)
    delta = jnp.sum(grad_t32 * attended, axis=0, keepdims=True)

    def third_step(c, dquery):
        at = pl.ds(pl.multiple_of(c * chunk, chunk), chunk)
        frac = exps[at, :] * sums[pl.ds(c, 1), :]
        sgrad = (frac * (dprobs[at, :] - delta)).astype(BF16)
        dk_sum[at, :] += dot(sgrad, query)
        dv_sum[at, :] += dot(weights[at, :], grad)
        return dquery + dot(keys_t[:, at], sgrad)

    dquery = lax.fori_loop(0, chunks, third_step, jnp.zeros((HD, rows), F32))
    dq_ref[...] = (factor * dquery).T.astype(BF16)

    @pl.when(step == heads_per - 1)
    def _():
        for p in range(parts):
            at = pl.ds(p * part_rows, part_rows)
            dcache_ref[p, 0] = (factor * dk_sum[at, :]).astype(BF16)
            dcache_ref[p, 1] = dv_sum[at, :].astype(BF16)
        at = pl.ds(prompt_rows, rows)
        dkr_ref[...] = (factor * dk_sum[at, :]).astype(BF16)
        dvr_ref[...] = dv_sum[at, :].astype(BF16)


def attend(pair, heads_per, lengths, queries, out_grad, cache, resp_keys, resp_values, earlier):
    rows, query_width = queries.shape
    parts = cache.shape[0]
    prompt_rows = parts * cache.shape[2]
    total_rows = prompt_rows + rows
    head_block = pl.BlockSpec((rows, HD), lambda s: (0, pair * heads_per + s))
    pair_block = pl.BlockSpec((rows, HD), lambda s: (0, pair))
    cache_block = pl.BlockSpec(cache.shape, lambda s: (0, 0, 0, 0))
    chunk_rows = -(-(prompt_rows // rows + 1) // 8) * 8
    in_specs = [
        pl.BlockSpec(memory_space=pltpu.SMEM),
        head_block,
        head_block,
        cache_block,
        pair_block,
        pair_block,
    ] + [pl.BlockSpec(memory_space=pl.ANY)] * len(earlier)
    aliases = {6 + i: i for i in range(len(earlier))}
    return pl.pallas_call(
        functools.partial(attention_kernel, parts, heads_per),
        grid=(heads_per,),
        in_specs=in_specs,
        out_specs=[head_block, head_block, pair_block, pair_block, cache_block],
        out_shape=[
            jax.ShapeDtypeStruct(queries.shape, BF16),
            jax.ShapeDtypeStruct(queries.shape, BF16),
            jax.ShapeDtypeStruct(resp_keys.shape, BF16),
            jax.ShapeDtypeStruct(resp_keys.shape, BF16),
            jax.ShapeDtypeStruct(cache.shape, BF16),
        ],
        scratch_shapes=[
            pltpu.VMEM((total_rows, HD), BF16),
            pltpu.VMEM((total_rows, HD), BF16),
            pltpu.VMEM((HD, total_rows), BF16),
            pltpu.VMEM((HD, total_rows), BF16),
            pltpu.VMEM((total_rows, rows), F32),
            pltpu.VMEM((total_rows, rows), F32),
            pltpu.VMEM((total_rows, rows), BF16),
            pltpu.VMEM((total_rows, HD), F32),
            pltpu.VMEM((total_rows, HD), F32),
            pltpu.VMEM((chunk_rows, rows), F32),
            pltpu.VMEM((chunk_rows, rows), F32),
        ],
        input_output_aliases=aliases,
        cost_estimate=pl.CostEstimate(
            flops=12 * heads_per * rows * total_rows * HD,
            bytes_accessed=8 * heads_per * rows * HD,
            transcendentals=heads_per * rows * total_rows,
        ),
        compiler_params=pltpu.CompilerParams(vmem_limit_bytes=48 * 1024 * 1024),
        name=f"attend_pair_{pair}",
    )(lengths, queries, out_grad, cache, resp_keys, resp_values, *earlier)


def per_device(queries, resp_keys, resp_values, prompt_keys, prompt_values, out_grad, lengths):
    _, seq_len, query_width = queries.shape
    pair_width = resp_keys.shape[2]
    pairs = pair_width // HD
    heads_per = query_width // pair_width
    queries, out_grad, resp_keys, resp_values = (
        a[0] for a in (queries, out_grad, resp_keys, resp_values)
    )
    own = jnp.stack([prompt_keys, prompt_values])
    own = lax.all_to_all(own, "tensor", split_axis=2, concat_axis=1, tiled=True)
    caches = [
        lax.all_gather(own[:, :, p * HD : (p + 1) * HD], "resp", axis=0) for p in range(pairs)
    ]
    earlier = ()
    sums = []
    for p in range(pairs):
        *earlier, dcache = attend(
            p, heads_per, lengths, queries, out_grad, caches[p], resp_keys, resp_values, earlier
        )
        sums.append(lax.psum_scatter(dcache, "resp", scatter_dimension=0))
    sums = jnp.concatenate(sums, axis=2)
    sums = lax.all_to_all(sums, "tensor", split_axis=1, concat_axis=2, tiled=True).astype(F32)
    return (*(a[None] for a in earlier), sums[0], sums[1])


def solution(mesh):
    rows = P(("group", "resp"), None, "tensor")
    prompt = P(("group", "resp", "tensor"), None)
    return jax.shard_map(
        per_device,
        mesh=mesh,
        in_specs=(rows, rows, rows, prompt, prompt, rows, P(("group", "resp"))),
        out_specs=(rows, rows, rows, rows, prompt, prompt),
        check_vma=False,
    )
```

```python
import functools
import math

import jax
import jax.numpy as jnp
from jax import lax
from jax.experimental import pallas as pl
from jax.experimental.pallas import tpu as pltpu
from jax.sharding import PartitionSpec as P

HD = 128
SUB = 128
LOWEST = -1e30
BF16 = jnp.bfloat16
F32 = jnp.float32


def dot(a, b):
    return jnp.dot(a, b, preferred_element_type=F32)


def attention_kernel(
    parts,
    heads_per,
    len_ref,
    q_ref,
    g_ref,
    cache_ref,
    kr_ref,
    vr_ref,
    *rest,
):
    (
        out_ref,
        dq_ref,
        dkr_ref,
        dvr_ref,
        dcache_ref,
        keys,
        values,
        keys_t,
        values_t,
        query,
        query_t,
        grad,
        grad_t,
        exps_even,
        exps_odd,
        fracs,
        deltas,
        dk_sum,
        dv_sum,
        dq_sum,
        tops,
        sums,
    ) = rest[-22:]
    rows = q_ref.shape[0]
    part_rows = cache_ref.shape[2]
    prompt_rows = parts * part_rows
    chunk = rows
    blocks = chunk // SUB
    prompt_chunks = prompt_rows // chunk
    chunks = prompt_chunks + 1
    stats = chunks * blocks
    factor = HD ** (-0.5)
    factor2 = factor * math.log2(math.e)
    length = len_ref[0]
    step = pl.program_id(0)
    slots = (exps_even, exps_odd)

    @pl.when(step == 0)
    def _():
        for p in range(parts):
            at = pl.ds(p * part_rows, part_rows)
            keys[at, :] = cache_ref[p, 0]
            values[at, :] = cache_ref[p, 1]
            keys_t[:, at] = cache_ref[p, 0].astype(F32).T.astype(BF16)
            values_t[:, at] = cache_ref[p, 1].astype(F32).T.astype(BF16)
        at = pl.ds(prompt_rows, rows)
        keys[at, :] = kr_ref[...]
        values[at, :] = vr_ref[...]
        keys_t[:, at] = kr_ref[...].astype(F32).T.astype(BF16)
        values_t[:, at] = vr_ref[...].astype(F32).T.astype(BF16)
        dk_sum[...] = jnp.zeros_like(dk_sum)
        dv_sum[...] = jnp.zeros_like(dv_sum)

    def rows_at(c):
        return pl.ds(pl.multiple_of(c * chunk, chunk), chunk)

    def score_part(now, c, masked):
        score = dot(keys[rows_at(c), :], query_t[now])
        if masked:
            j = lax.broadcasted_iota(jnp.int32, (chunk, rows), 0)
            i = lax.broadcasted_iota(jnp.int32, (chunk, rows), 1)
            score = jnp.where((j <= i) & (j < length), score, -jnp.inf)
        for u in range(blocks):
            block = score[u * SUB : (u + 1) * SUB, :]
            top = jnp.max(block, axis=0, keepdims=True)
            top = jnp.maximum(top, LOWEST) * factor2
            exp = jnp.exp2(block * factor2 - top)
            slots[now][pl.ds(pl.multiple_of(c * chunk + u * SUB, SUB), SUB), :] = exp
            tops[pl.ds(c * blocks + u, 1), :] = top
            sums[pl.ds(c * blocks + u, 1), :] = jnp.sum(exp, axis=0, keepdims=True)

    def scaled(slot, c, u):
        at = pl.ds(pl.multiple_of(c * chunk + u * SUB, SUB), SUB)
        return slots[slot][at, :] * fracs[slot, pl.ds(c * blocks + u, 1), :]

    def grad_part(before, c):
        at = rows_at(c)
        dprob = dot(values[at, :], grad_t[before])
        delta = deltas[before]
        weight, sgrad = [], []
        for u in range(blocks):
            frac = scaled(before, c, u)
            weight.append(frac.astype(BF16))
            sgrad.append((frac * (dprob[u * SUB : (u + 1) * SUB, :] - delta)).astype(BF16))
        weight, sgrad = jnp.concatenate(weight, 0), jnp.concatenate(sgrad, 0)
        dv_sum[at, :] += dot(weight, grad[before])
        dk_sum[at, :] += dot(sgrad, query[before])
        dq_sum[...] += dot(keys_t[:, at], sgrad)

    def run(now, with_score, with_grad):
        def body(c, carry, masked=False):
            if with_score:
                score_part(now, c, masked)
            if with_grad:
                grad_part(1 - now, c)
            return carry

        if with_grad:
            dq_sum[...] = jnp.zeros_like(dq_sum)
        lax.fori_loop(0, prompt_chunks, body, 0)
        body(prompt_chunks, 0, True)
        if with_grad:
            dq_ref[...] = (factor * dq_sum[...]).T.astype(BF16)

    def prepare(now):
        live_rows = lax.broadcasted_iota(jnp.int32, (rows, HD), 0) < length
        live_grad = jnp.where(live_rows, g_ref[...].astype(F32), 0.0)
        grad[now] = live_grad.astype(BF16)
        grad_t[now] = live_grad.T.astype(BF16)
        query[now] = q_ref[...]
        query_t[now] = q_ref[...].astype(F32).T.astype(BF16)

    def finish(now):
        top = jnp.max(tops[:stats, :], axis=0, keepdims=True)
        scale = jnp.exp2(tops[:stats, :] - top)
        total = jnp.sum(scale * sums[:stats, :], axis=0, keepdims=True)
        fracs[now, :stats, :] = scale / total

        mixture = jnp.zeros((HD, rows), F32)
        for c in range(chunks):
            weight = jnp.concatenate(
                [scaled(now, c, u).astype(BF16) for u in range(blocks)], 0
            )
            mixture = mixture + dot(values_t[:, c * chunk : (c + 1) * chunk], weight)
        live_lanes = lax.broadcasted_iota(jnp.int32, (HD, rows), 1) < length
        attended = jnp.where(live_lanes, mixture, 0.0).astype(BF16).astype(F32)
        out_ref[...] = attended.T.astype(BF16)
        deltas[now] = jnp.sum(grad_t[now].astype(F32) * attended, axis=0, keepdims=True)

    @pl.when(step == 0)
    def _():
        prepare(0)
        run(0, True, False)
        finish(0)

    for now in range(2):
        @pl.when((step > 0) & (step < heads_per) & (lax.rem(step, 2) == now))
        def _():
            prepare(now)
            run(now, True, True)
            finish(now)

    @pl.when(step == heads_per)
    def _():
        run(heads_per % 2, False, True)

    @pl.when(step == heads_per)
    def _():
        for p in range(parts):
            at = pl.ds(p * part_rows, part_rows)
            dcache_ref[p, 0] = (factor * dk_sum[at, :]).astype(BF16)
            dcache_ref[p, 1] = dv_sum[at, :].astype(BF16)
        at = pl.ds(prompt_rows, rows)
        dkr_ref[...] = (factor * dk_sum[at, :]).astype(BF16)
        dvr_ref[...] = dv_sum[at, :].astype(BF16)


def attend(pair, heads_per, lengths, queries, out_grad, cache, resp_keys, resp_values, earlier):
    rows, query_width = queries.shape
    parts = cache.shape[0]
    prompt_rows = parts * cache.shape[2]
    total_rows = prompt_rows + rows
    first, last = pair * heads_per, (pair + 1) * heads_per - 1
    head_block = pl.BlockSpec((rows, HD), lambda s: (0, jnp.minimum(first + s, last)))
    late_block = pl.BlockSpec((rows, HD), lambda s: (0, jnp.maximum(first + s - 1, first)))
    pair_block = pl.BlockSpec((rows, HD), lambda s: (0, pair))
    cache_block = pl.BlockSpec(cache.shape, lambda s: (0, 0, 0, 0))
    stats = -(-total_rows // SUB // 8) * 8
    in_specs = [
        pl.BlockSpec(memory_space=pltpu.SMEM),
        head_block,
        head_block,
        cache_block,
        pair_block,
        pair_block,
    ] + [pl.BlockSpec(memory_space=pl.ANY)] * len(earlier)
    aliases = {6 + i: i for i in range(len(earlier))}
    return pl.pallas_call(
        functools.partial(attention_kernel, parts, heads_per),
        grid=(heads_per + 1,),
        in_specs=in_specs,
        out_specs=[head_block, late_block, pair_block, pair_block, cache_block],
        out_shape=[
            jax.ShapeDtypeStruct(queries.shape, BF16),
            jax.ShapeDtypeStruct(queries.shape, BF16),
            jax.ShapeDtypeStruct(resp_keys.shape, BF16),
            jax.ShapeDtypeStruct(resp_keys.shape, BF16),
            jax.ShapeDtypeStruct(cache.shape, BF16),
        ],
        scratch_shapes=[
            pltpu.VMEM((total_rows, HD), BF16),
            pltpu.VMEM((total_rows, HD), BF16),
            pltpu.VMEM((HD, total_rows), BF16),
            pltpu.VMEM((HD, total_rows), BF16),
            pltpu.VMEM((2, rows, HD), BF16),
            pltpu.VMEM((2, HD, rows), BF16),
            pltpu.VMEM((2, rows, HD), BF16),
            pltpu.VMEM((2, HD, rows), BF16),
            pltpu.VMEM((total_rows, rows), F32),
            pltpu.VMEM((total_rows, rows), F32),
            pltpu.VMEM((2, stats, rows), F32),
            pltpu.VMEM((2, 1, rows), F32),
            pltpu.VMEM((total_rows, HD), F32),
            pltpu.VMEM((total_rows, HD), F32),
            pltpu.VMEM((HD, rows), F32),
            pltpu.VMEM((stats, rows), F32),
            pltpu.VMEM((stats, rows), F32),
        ],
        input_output_aliases=aliases,
        cost_estimate=pl.CostEstimate(
            flops=12 * heads_per * rows * total_rows * HD,
            bytes_accessed=8 * heads_per * rows * HD,
            transcendentals=heads_per * rows * total_rows,
        ),
        compiler_params=pltpu.CompilerParams(vmem_limit_bytes=48 * 1024 * 1024),
        name=f"attend_pair_{pair}",
    )(lengths, queries, out_grad, cache, resp_keys, resp_values, *earlier)


def whole_block(shape):
    return pl.BlockSpec(shape, lambda: (0,) * len(shape))


def cut_kernel(width, k_ref, v_ref, *outs):
    me = lax.axis_index("tensor")
    for i, out in enumerate(outs):
        columns = pl.ds(pl.multiple_of((me ^ i) * width, width), width)
        out[0] = k_ref[:, columns]
        out[1] = v_ref[:, columns]


def cut(prompt_keys, prompt_values, width):
    rows, columns = prompt_keys.shape
    count = columns // width
    return pl.pallas_call(
        functools.partial(cut_kernel, width),
        in_specs=[whole_block((rows, columns))] * 2,
        out_specs=[whole_block((2, rows, width))] * count,
        out_shape=[jax.ShapeDtypeStruct((2, rows, width), BF16)] * count,
        name="cut",
    )(prompt_keys, prompt_values)


def line_up_kernel(ins, *refs):
    ins, outs = refs[:ins], refs[ins:]
    for i, block in enumerate(ins):
        rows = block.shape[1]
        for p, out in enumerate(outs):
            out[:, i * rows : (i + 1) * rows, :] = block[:, :, p * HD : (p + 1) * HD]


def line_up(blocks):
    _, rows, width = blocks[0].shape
    shape = (2, rows * len(blocks), HD)
    return pl.pallas_call(
        functools.partial(line_up_kernel, len(blocks)),
        in_specs=[whole_block(blocks[0].shape)] * len(blocks),
        out_specs=[whole_block(shape)] * (width // HD),
        out_shape=[jax.ShapeDtypeStruct(shape, BF16)] * (width // HD),
        name="line_up",
    )(*blocks)


def split_kernel(ins, *refs):
    ins, outs = refs[:ins], refs[ins:]
    for p, block in enumerate(ins):
        for i, out in enumerate(outs):
            rows = out.shape[1]
            out[:, :, p * HD : (p + 1) * HD] = block[:, i * rows : (i + 1) * rows, :]


def split(sums, rows):
    count = sums[0].shape[1] // rows
    shape = (2, rows, HD * len(sums))
    return pl.pallas_call(
        functools.partial(split_kernel, len(sums)),
        in_specs=[whole_block(sums[0].shape)] * len(sums),
        out_specs=[whole_block(shape)] * count,
        out_shape=[jax.ShapeDtypeStruct(shape, BF16)] * count,
        name="split",
    )(*sums)


def place_kernel(*refs):
    *ins, dk_ref, dv_ref = refs
    me = lax.axis_index("tensor")
    for i, block in enumerate(ins):
        width = block.shape[2]
        columns = pl.ds(pl.multiple_of((me ^ i) * width, width), width)
        dk_ref[:, columns] = block[0].astype(F32)
        dv_ref[:, columns] = block[1].astype(F32)


def place(blocks):
    _, rows, width = blocks[0].shape
    shape = (rows, width * len(blocks))
    return pl.pallas_call(
        place_kernel,
        in_specs=[whole_block(blocks[0].shape)] * len(blocks),
        out_specs=[whole_block(shape)] * 2,
        out_shape=[jax.ShapeDtypeStruct(shape, F32)] * 2,
        name="place",
    )(*blocks)


def exchange(blocks):
    count = len(blocks)
    return [blocks[0]] + [
        lax.ppermute(blocks[i], "tensor", [(j, j ^ i) for j in range(count)])
        for i in range(1, count)
    ]


def per_device(queries, resp_keys, resp_values, prompt_keys, prompt_values, out_grad, lengths):
    _, seq_len, query_width = queries.shape
    pair_width = resp_keys.shape[2]
    pairs = pair_width // HD
    heads_per = query_width // pair_width
    queries, out_grad, resp_keys, resp_values = (
        a[0] for a in (queries, out_grad, resp_keys, resp_values)
    )
    own = line_up(exchange(cut(prompt_keys, prompt_values, pair_width)))
    caches = [lax.all_gather(own[p], "resp", axis=0) for p in range(pairs)]
    earlier = ()
    sums = []
    for p in range(pairs):
        *earlier, dcache = attend(
            p, heads_per, lengths, queries, out_grad, caches[p], resp_keys, resp_values, earlier
        )
        if sums:
            dcache, sums[-1] = lax.optimization_barrier((dcache, sums[-1]))
        sums.append(lax.psum_scatter(dcache, "resp", scatter_dimension=0))
    key_grad, value_grad = place(exchange(split(sums, prompt_keys.shape[0])))
    return (*(a[None] for a in earlier), key_grad, value_grad)


def solution(mesh):
    rows = P(("group", "resp"), None, "tensor")
    prompt = P(("group", "resp", "tensor"), None)
    return jax.shard_map(
        per_device,
        mesh=mesh,
        in_specs=(rows, rows, rows, prompt, prompt, rows, P(("group", "resp"))),
        out_specs=(rows, rows, rows, rows, prompt, prompt),
        check_vma=False,
    )
```

```python
import functools
import math

import jax
import jax.numpy as jnp
from jax import lax
from jax.experimental import pallas as pl
from jax.experimental.pallas import tpu as pltpu
from jax.sharding import PartitionSpec as P

HD = 128
SUB = 128
LOWEST = -1e30
BF16 = jnp.bfloat16
F32 = jnp.float32


def dot(a, b):
    return jnp.dot(a, b, preferred_element_type=F32)


def attention_kernel(
    parts,
    heads_per,
    len_ref,
    q_ref,
    g_ref,
    cache_ref,
    kr_ref,
    vr_ref,
    *rest,
):
    (
        out_ref,
        dq_ref,
        dkr_ref,
        dvr_ref,
        dcache_ref,
        keys,
        values,
        keys_t,
        values_t,
        query,
        query_t,
        grad,
        grad_t,
        exps_even,
        exps_odd,
        weights_even,
        weights_odd,
        sgrads,
        score_even,
        score_odd,
        dprob_even,
        dprob_odd,
        fracs,
        deltas,
        dk_sum,
        dv_sum,
        tops,
        sums,
    ) = rest[-28:]
    rows = q_ref.shape[0]
    part_rows = cache_ref.shape[2]
    prompt_rows = parts * part_rows
    total_rows = prompt_rows + rows
    half = rows // 2
    pieces = [(at, rows, 0) for at in range(0, prompt_rows, rows)]
    pieces += [(prompt_rows, half, 0), (prompt_rows + half, half, half)]
    count = len(pieces)
    factor = HD ** (-0.5)
    factor2 = factor * math.log2(math.e)
    length = len_ref[0]
    step = pl.program_id(0)
    exps = (exps_even, exps_odd)
    weights = (weights_even, weights_odd)
    scores = (score_even, score_odd)
    dprobs = (dprob_even, dprob_odd)

    @pl.when(step == 0)
    def _():
        for p in range(parts):
            at = pl.ds(p * part_rows, part_rows)
            keys[at, :] = cache_ref[p, 0]
            values[at, :] = cache_ref[p, 1]
            keys_t[:, at] = cache_ref[p, 0].T
            values_t[:, at] = cache_ref[p, 1].T
        at = pl.ds(prompt_rows, rows)
        keys[at, :] = kr_ref[...]
        values[at, :] = vr_ref[...]
        keys_t[:, at] = kr_ref[...].T
        values_t[:, at] = vr_ref[...].T
        dk_sum[...] = jnp.zeros_like(dk_sum)
        dv_sum[...] = jnp.zeros_like(dv_sum)
        tops[...] = jnp.full_like(tops, LOWEST)
        sums[...] = jnp.zeros_like(sums)
        for ref in (*weights, sgrads):
            ref[prompt_rows + half :, :half] = jnp.zeros((half, half), BF16)

    def blocks(piece):
        at, size, row = pieces[piece]
        for u in range(0, size, SUB):
            for r in range(0, rows - row, SUB):
                yield u, r, slice(at + u, at + u + SUB), slice(row + r, row + r + SUB)

    def stat(block_at):
        return slice(block_at.start // SUB * 8, block_at.start // SUB * 8 + 8)

    def score_product(now, piece):
        at, size, row = pieces[piece]
        scores[piece % 2][:size, : rows - row] = dot(
            keys[at : at + size, :], query_t[now, :, row:]
        )

    def score_chain(now, piece):
        for u, r, key_at, row_at in blocks(piece):
            block = scores[piece % 2][u : u + SUB, r : r + SUB]
            if key_at.start >= prompt_rows:
                j = lax.broadcasted_iota(jnp.int32, (SUB, SUB), 0) + key_at.start - prompt_rows
                i = lax.broadcasted_iota(jnp.int32, (SUB, SUB), 1) + row_at.start
                block = jnp.where((j <= i) & (j < length), block, -jnp.inf)
            block = block.reshape(SUB // 8, 8, SUB) * factor2
            top = jnp.maximum(jnp.max(block, axis=0), LOWEST)
            exp = jnp.exp2(block - top[None])
            exps[now][key_at, row_at] = exp.reshape(SUB, SUB)
            tops[stat(key_at), row_at] = top
            sums[stat(key_at), row_at] = jnp.sum(exp, axis=0)

    def frac(slot, key_at, row_at):
        block = exps[slot][key_at, row_at].reshape(SUB // 8, 8, SUB)
        return block * fracs[slot, stat(key_at), row_at][None]

    def dprob_product(before, piece):
        at, size, row = pieces[piece]
        dprobs[piece % 2][:size, : rows - row] = dot(
            values[at : at + size, :], grad_t[before, :, row:]
        )

    def grad_chain(before, piece):
        for u, r, key_at, row_at in blocks(piece):
            dprob = dprobs[piece % 2][u : u + SUB, r : r + SUB].reshape(SUB // 8, 8, SUB)
            sgrad = frac(before, key_at, row_at) * (dprob - deltas[before, :, row_at][None])
            sgrads[key_at, row_at] = sgrad.reshape(SUB, SUB).astype(BF16)

    def grad_products(before, piece):
        at, size, row = pieces[piece]
        key_at = slice(at, at + size)
        dv_sum[key_at, :] += dot(weights[before][key_at, row:], grad[before, row:, :])
        dk_sum[key_at, :] += dot(sgrads[key_at, row:], query[before, row:, :])

    def run(now, with_score, with_grad):
        before = 1 - now
        for stage in range(-1, count + 1):
            if stage + 1 < count:
                if with_score:
                    score_product(now, stage + 1)
                if with_grad:
                    dprob_product(before, stage + 1)
            if 0 <= stage < count:
                if with_score:
                    score_chain(now, stage)
                if with_grad:
                    grad_chain(before, stage)
            if stage >= 1 and with_grad:
                grad_products(before, stage - 1)
        if with_grad:
            dquery = dot(keys_t[...], sgrads[...])
            dq_ref[...] = (factor * dquery).T.astype(BF16)
        if with_score:
            finish(now)

    def prepare(now):
        live_rows = lax.broadcasted_iota(jnp.int32, (rows, HD), 0) < length
        live_grad = jnp.where(live_rows, g_ref[...].astype(F32), 0.0)
        grad[now] = live_grad.astype(BF16)
        grad_t[now] = live_grad.T.astype(BF16)
        query[now] = q_ref[...]
        query_t[now] = q_ref[...].T

    def finish(now):
        top = jnp.max(tops[...], axis=0, keepdims=True)
        scale = jnp.exp2(tops[...] - top)
        total = jnp.sum(scale * sums[...], axis=0, keepdims=True)
        fracs[now] = scale * (1.0 / total)
        for piece in range(count):
            for _, _, key_at, row_at in blocks(piece):
                weight = frac(now, key_at, row_at).reshape(SUB, SUB)
                weights[now][key_at, row_at] = weight.astype(BF16)
        mixture = dot(values_t[...], weights[now][...])
        live_lanes = lax.broadcasted_iota(jnp.int32, (HD, rows), 1) < length
        attended = jnp.where(live_lanes, mixture, 0.0).astype(BF16).astype(F32)
        out_ref[...] = attended.T.astype(BF16)
        delta = jnp.sum(grad_t[now].astype(F32) * attended, axis=0, keepdims=True)
        deltas[now] = jnp.broadcast_to(delta, (8, rows))

    @pl.when(step == 0)
    def _():
        prepare(0)
        run(0, True, False)

    for now in range(2):
        @pl.when((step > 0) & (step < heads_per) & (lax.rem(step, 2) == now))
        def _():
            prepare(now)
            run(now, True, True)

    @pl.when(step == heads_per)
    def _():
        run(heads_per % 2, False, True)
        for p in range(parts):
            at = pl.ds(p * part_rows, part_rows)
            dcache_ref[p, 0] = (factor * dk_sum[at, :]).astype(BF16)
            dcache_ref[p, 1] = dv_sum[at, :].astype(BF16)
        at = pl.ds(prompt_rows, rows)
        dkr_ref[...] = (factor * dk_sum[at, :]).astype(BF16)
        dvr_ref[...] = dv_sum[at, :].astype(BF16)


def attend(pair, heads_per, lengths, queries, out_grad, cache, resp_keys, resp_values, earlier):
    rows, query_width = queries.shape
    parts = cache.shape[0]
    prompt_rows = parts * cache.shape[2]
    total_rows = prompt_rows + rows
    first, last = pair * heads_per, (pair + 1) * heads_per - 1
    head_block = pl.BlockSpec((rows, HD), lambda s: (0, jnp.minimum(first + s, last)))
    late_block = pl.BlockSpec((rows, HD), lambda s: (0, jnp.maximum(first + s - 1, first)))
    pair_block = pl.BlockSpec((rows, HD), lambda s: (0, pair))
    cache_block = pl.BlockSpec(cache.shape, lambda s: (0, 0, 0, 0))
    stats = total_rows // SUB * 8
    in_specs = [
        pl.BlockSpec(memory_space=pltpu.SMEM),
        head_block,
        head_block,
        cache_block,
        pair_block,
        pair_block,
    ] + [pl.BlockSpec(memory_space=pl.ANY)] * len(earlier)
    aliases = {6 + i: i for i in range(len(earlier))}
    return pl.pallas_call(
        functools.partial(attention_kernel, parts, heads_per),
        grid=(heads_per + 1,),
        in_specs=in_specs,
        out_specs=[head_block, late_block, pair_block, pair_block, cache_block],
        out_shape=[
            jax.ShapeDtypeStruct(queries.shape, BF16),
            jax.ShapeDtypeStruct(queries.shape, BF16),
            jax.ShapeDtypeStruct(resp_keys.shape, BF16),
            jax.ShapeDtypeStruct(resp_keys.shape, BF16),
            jax.ShapeDtypeStruct(cache.shape, BF16),
        ],
        scratch_shapes=[
            pltpu.VMEM((total_rows, HD), BF16),
            pltpu.VMEM((total_rows, HD), BF16),
            pltpu.VMEM((HD, total_rows), BF16),
            pltpu.VMEM((HD, total_rows), BF16),
            pltpu.VMEM((2, rows, HD), BF16),
            pltpu.VMEM((2, HD, rows), BF16),
            pltpu.VMEM((2, rows, HD), BF16),
            pltpu.VMEM((2, HD, rows), BF16),
            pltpu.VMEM((total_rows, rows), F32),
            pltpu.VMEM((total_rows, rows), F32),
            pltpu.VMEM((total_rows, rows), BF16),
            pltpu.VMEM((total_rows, rows), BF16),
            pltpu.VMEM((total_rows, rows), BF16),
            pltpu.VMEM((rows, rows), F32),
            pltpu.VMEM((rows, rows), F32),
            pltpu.VMEM((rows, rows), F32),
            pltpu.VMEM((rows, rows), F32),
            pltpu.VMEM((2, stats, rows), F32),
            pltpu.VMEM((2, 8, rows), F32),
            pltpu.VMEM((total_rows, HD), F32),
            pltpu.VMEM((total_rows, HD), F32),
            pltpu.VMEM((stats, rows), F32),
            pltpu.VMEM((stats, rows), F32),
        ],
        input_output_aliases=aliases,
        cost_estimate=pl.CostEstimate(
            flops=12 * heads_per * rows * total_rows * HD,
            bytes_accessed=8 * heads_per * rows * HD,
            transcendentals=heads_per * rows * total_rows,
        ),
        compiler_params=pltpu.CompilerParams(vmem_limit_bytes=48 * 1024 * 1024),
        name=f"attend_pair_{pair}",
    )(lengths, queries, out_grad, cache, resp_keys, resp_values, *earlier)


def whole_block(shape):
    return pl.BlockSpec(shape, lambda: (0,) * len(shape))


def cut_kernel(width, k_ref, v_ref, *outs):
    me = lax.axis_index("tensor")
    for i, out in enumerate(outs):
        columns = pl.ds(pl.multiple_of((me ^ i) * width, width), width)
        out[0] = k_ref[:, columns]
        out[1] = v_ref[:, columns]


def cut(prompt_keys, prompt_values, width):
    rows, columns = prompt_keys.shape
    count = columns // width
    return pl.pallas_call(
        functools.partial(cut_kernel, width),
        in_specs=[whole_block((rows, columns))] * 2,
        out_specs=[whole_block((2, rows, width))] * count,
        out_shape=[jax.ShapeDtypeStruct((2, rows, width), BF16)] * count,
        name="cut",
    )(prompt_keys, prompt_values)


def line_up_kernel(ins, *refs):
    ins, outs = refs[:ins], refs[ins:]
    for i, block in enumerate(ins):
        rows = block.shape[1]
        for p, out in enumerate(outs):
            out[:, i * rows : (i + 1) * rows, :] = block[:, :, p * HD : (p + 1) * HD]


def line_up(blocks):
    _, rows, width = blocks[0].shape
    shape = (2, rows * len(blocks), HD)
    return pl.pallas_call(
        functools.partial(line_up_kernel, len(blocks)),
        in_specs=[whole_block(blocks[0].shape)] * len(blocks),
        out_specs=[whole_block(shape)] * (width // HD),
        out_shape=[jax.ShapeDtypeStruct(shape, BF16)] * (width // HD),
        name="line_up",
    )(*blocks)


def split_kernel(ins, *refs):
    ins, outs = refs[:ins], refs[ins:]
    for p, block in enumerate(ins):
        for i, out in enumerate(outs):
            rows = out.shape[1]
            out[:, :, p * HD : (p + 1) * HD] = block[:, i * rows : (i + 1) * rows, :]


def split(sums, rows):
    count = sums[0].shape[1] // rows
    shape = (2, rows, HD * len(sums))
    return pl.pallas_call(
        functools.partial(split_kernel, len(sums)),
        in_specs=[whole_block(sums[0].shape)] * len(sums),
        out_specs=[whole_block(shape)] * count,
        out_shape=[jax.ShapeDtypeStruct(shape, BF16)] * count,
        name="split",
    )(*sums)


def place_kernel(*refs):
    *ins, dk_ref, dv_ref = refs
    me = lax.axis_index("tensor")
    for i, block in enumerate(ins):
        width = block.shape[2]
        columns = pl.ds(pl.multiple_of((me ^ i) * width, width), width)
        dk_ref[:, columns] = block[0].astype(F32)
        dv_ref[:, columns] = block[1].astype(F32)


def place(blocks):
    _, rows, width = blocks[0].shape
    shape = (rows, width * len(blocks))
    return pl.pallas_call(
        place_kernel,
        in_specs=[whole_block(blocks[0].shape)] * len(blocks),
        out_specs=[whole_block(shape)] * 2,
        out_shape=[jax.ShapeDtypeStruct(shape, F32)] * 2,
        name="place",
    )(*blocks)


def exchange(blocks):
    count = len(blocks)
    return [blocks[0]] + [
        lax.ppermute(blocks[i], "tensor", [(j, j ^ i) for j in range(count)])
        for i in range(1, count)
    ]


def per_device(queries, resp_keys, resp_values, prompt_keys, prompt_values, out_grad, lengths):
    _, seq_len, query_width = queries.shape
    pair_width = resp_keys.shape[2]
    pairs = pair_width // HD
    heads_per = query_width // pair_width
    queries, out_grad, resp_keys, resp_values = (
        a[0] for a in (queries, out_grad, resp_keys, resp_values)
    )
    own = line_up(exchange(cut(prompt_keys, prompt_values, pair_width)))
    caches = [lax.all_gather(own[p], "resp", axis=0) for p in range(pairs)]
    earlier = ()
    sums = []
    for p in range(pairs):
        *earlier, dcache = attend(
            p, heads_per, lengths, queries, out_grad, caches[p], resp_keys, resp_values, earlier
        )
        if sums:
            dcache, sums[-1] = lax.optimization_barrier((dcache, sums[-1]))
        sums.append(lax.psum_scatter(dcache, "resp", scatter_dimension=0))
    key_grad, value_grad = place(exchange(split(sums, prompt_keys.shape[0])))
    return (*(a[None] for a in earlier), key_grad, value_grad)


def solution(mesh):
    rows = P(("group", "resp"), None, "tensor")
    prompt = P(("group", "resp", "tensor"), None)
    return jax.shard_map(
        per_device,
        mesh=mesh,
        in_specs=(rows, rows, rows, prompt, prompt, rows, P(("group", "resp"))),
        out_specs=(rows, rows, rows, rows, prompt, prompt),
        check_vma=False,
    )
```

```python
import functools
import math

import jax
import jax.numpy as jnp
from jax import lax
from jax.experimental import pallas as pl
from jax.experimental.pallas import tpu as pltpu
from jax.sharding import PartitionSpec as P

HD = 128
SUB = 128
LOWEST = -1e30
BF16 = jnp.bfloat16
F32 = jnp.float32


def dot(a, b):
    return jnp.dot(a, b, preferred_element_type=F32)


def attention_kernel(
    layout,
    heads_per,
    earlier,
    len_ref,
    q_ref,
    g_ref,
    kr_ref,
    vr_ref,
    *rest,
):
    caches, rest = rest[: layout.caches], rest[layout.caches + earlier :]
    out_ref, dq_ref, dkr_ref, dvr_ref, *rest = rest
    dcaches, rest = rest[: layout.dcaches], rest[layout.dcaches :]
    (
        keys,
        values,
        keys_t,
        values_t,
        query,
        query_t,
        grad,
        grad_t,
        exps_even,
        exps_odd,
        weights_even,
        weights_odd,
        sgrads,
        score_even,
        score_odd,
        dprob_even,
        dprob_odd,
        fracs,
        deltas,
        dk_sum,
        dv_sum,
        tops,
        sums,
    ) = rest
    rows = q_ref.shape[0]
    prompt_rows = layout.prompt_rows
    total_rows = prompt_rows + rows
    half = rows // 2
    pieces = [(at, rows, 0) for at in range(0, prompt_rows, rows)]
    pieces += [(prompt_rows, half, 0), (prompt_rows + half, half, half)]
    count = len(pieces)
    factor = HD ** (-0.5)
    factor2 = factor * math.log2(math.e)
    length = len_ref[0]
    step = pl.program_id(0)
    exps = (exps_even, exps_odd)
    weights = (weights_even, weights_odd)
    scores = (score_even, score_odd)
    dprobs = (dprob_even, dprob_odd)

    @pl.when(step == 0)
    def _():
        for at, key_block, value_block in layout.load(caches):
            keys[at, :] = key_block
            values[at, :] = value_block
        for at in range(0, prompt_rows, rows):
            at = pl.ds(at, rows)
            keys_t[:, at] = keys[at, :].T
            values_t[:, at] = values[at, :].T
        at = pl.ds(prompt_rows, rows)
        keys[at, :] = kr_ref[...]
        values[at, :] = vr_ref[...]
        keys_t[:, at] = kr_ref[...].T
        values_t[:, at] = vr_ref[...].T
        dk_sum[...] = jnp.zeros_like(dk_sum)
        dv_sum[...] = jnp.zeros_like(dv_sum)
        tops[...] = jnp.full_like(tops, LOWEST)
        sums[...] = jnp.zeros_like(sums)
        for ref in (*weights, sgrads):
            ref[prompt_rows + half :, :half] = jnp.zeros((half, half), BF16)

    def blocks(piece):
        at, size, row = pieces[piece]
        for u in range(0, size, SUB):
            for r in range(0, rows - row, SUB):
                yield u, r, slice(at + u, at + u + SUB), slice(row + r, row + r + SUB)

    def stat(block_at):
        return slice(block_at.start // SUB * 8, block_at.start // SUB * 8 + 8)

    def score_product(now, piece):
        at, size, row = pieces[piece]
        scores[piece % 2][:size, : rows - row] = dot(
            keys[at : at + size, :], query_t[now, :, row:]
        )

    def score_chain(now, piece):
        for u, r, key_at, row_at in blocks(piece):
            block = scores[piece % 2][u : u + SUB, r : r + SUB]
            if key_at.start >= prompt_rows:
                j = lax.broadcasted_iota(jnp.int32, (SUB, SUB), 0) + key_at.start - prompt_rows
                i = lax.broadcasted_iota(jnp.int32, (SUB, SUB), 1) + row_at.start
                block = jnp.where((j <= i) & (j < length), block, -jnp.inf)
            block = block.reshape(SUB // 8, 8, SUB) * factor2
            top = jnp.maximum(jnp.max(block, axis=0), LOWEST)
            exp = jnp.exp2(block - top[None])
            exps[now][key_at, row_at] = exp.reshape(SUB, SUB)
            tops[stat(key_at), row_at] = top
            sums[stat(key_at), row_at] = jnp.sum(exp, axis=0)

    def frac(slot, key_at, row_at):
        block = exps[slot][key_at, row_at].reshape(SUB // 8, 8, SUB)
        return block * fracs[slot, stat(key_at), row_at][None]

    def dprob_product(before, piece):
        at, size, row = pieces[piece]
        dprobs[piece % 2][:size, : rows - row] = dot(
            values[at : at + size, :], grad_t[before, :, row:]
        )

    def grad_chain(before, piece):
        for u, r, key_at, row_at in blocks(piece):
            dprob = dprobs[piece % 2][u : u + SUB, r : r + SUB].reshape(SUB // 8, 8, SUB)
            sgrad = frac(before, key_at, row_at) * (dprob - deltas[before, :, row_at][None])
            sgrads[key_at, row_at] = sgrad.reshape(SUB, SUB).astype(BF16)

    def grad_products(before, piece):
        at, size, row = pieces[piece]
        key_at = slice(at, at + size)
        dv_sum[key_at, :] += dot(weights[before][key_at, row:], grad[before, row:, :])
        dk_sum[key_at, :] += dot(sgrads[key_at, row:], query[before, row:, :])

    def run(now, with_score, with_grad):
        before = 1 - now
        for stage in range(-1, count + 1):
            if stage + 1 < count:
                if with_score:
                    score_product(now, stage + 1)
                if with_grad:
                    dprob_product(before, stage + 1)
            if 0 <= stage < count:
                if with_score:
                    score_chain(now, stage)
                if with_grad:
                    grad_chain(before, stage)
            if stage >= 1 and with_grad:
                grad_products(before, stage - 1)
        if with_grad:
            dquery = dot(keys_t[...], sgrads[...])
            dq_ref[...] = (factor * dquery).T.astype(BF16)
        if with_score:
            finish(now)

    def prepare(now):
        live_rows = lax.broadcasted_iota(jnp.int32, (rows, HD), 0) < length
        live_grad = jnp.where(live_rows, g_ref[...].astype(F32), 0.0)
        grad[now] = live_grad.astype(BF16)
        grad_t[now] = live_grad.T.astype(BF16)
        query[now] = q_ref[...]
        query_t[now] = q_ref[...].T

    def finish(now):
        top = jnp.max(tops[...], axis=0, keepdims=True)
        scale = jnp.exp2(tops[...] - top)
        total = jnp.sum(scale * sums[...], axis=0, keepdims=True)
        fracs[now] = scale * (1.0 / total)
        for piece in range(count):
            for _, _, key_at, row_at in blocks(piece):
                weight = frac(now, key_at, row_at).reshape(SUB, SUB)
                weights[now][key_at, row_at] = weight.astype(BF16)
        mixture = dot(values_t[...], weights[now][...])
        live_lanes = lax.broadcasted_iota(jnp.int32, (HD, rows), 1) < length
        attended = jnp.where(live_lanes, mixture, 0.0).astype(BF16).astype(F32)
        out_ref[...] = attended.T.astype(BF16)
        delta = jnp.sum(grad_t[now].astype(F32) * attended, axis=0, keepdims=True)
        deltas[now] = jnp.broadcast_to(delta, (8, rows))

    @pl.when(step == 0)
    def _():
        prepare(0)
        run(0, True, False)

    for now in range(2):
        @pl.when((step > 0) & (step < heads_per) & (lax.rem(step, 2) == now))
        def _():
            prepare(now)
            run(now, True, True)

    @pl.when(step == heads_per)
    def _():
        run(heads_per % 2, False, True)
        layout.store(dcaches, dk_sum, dv_sum, factor)
        at = pl.ds(prompt_rows, rows)
        dkr_ref[...] = (factor * dk_sum[at, :]).astype(BF16)
        dvr_ref[...] = dv_sum[at, :].astype(BF16)


class Gathered:
    def __init__(self, members, ranks, own_rows):
        self.members, self.ranks, self.own_rows = members, ranks, own_rows
        self.part_rows = ranks * own_rows
        self.prompt_rows = members * self.part_rows
        self.caches = 1
        self.dcaches = members * ranks

    def cache_shapes(self):
        return [(self.members, 2, self.part_rows, HD)]

    def dcache_shapes(self):
        return [(2, self.own_rows, HD)] * self.dcaches

    def load(self, caches):
        for m in range(self.members):
            at = pl.ds(m * self.part_rows, self.part_rows)
            yield at, caches[0][m, 0], caches[0][m, 1]

    def store(self, dcaches, dk_sum, dv_sum, factor):
        me = lax.axis_index("resp")
        for shift in range(self.members):
            part = lax.rem(me + shift, self.members) * self.part_rows
            for i in range(self.ranks):
                at = pl.multiple_of(part + i * self.own_rows, self.own_rows)
                at = pl.ds(at, self.own_rows)
                ref = dcaches[shift * self.ranks + i]
                ref[0] = (factor * dk_sum[at, :]).astype(BF16)
                ref[1] = dv_sum[at, :].astype(BF16)


class Scattered(Gathered):
    def __init__(self, members, ranks, own_rows):
        super().__init__(members, ranks, own_rows)
        self.caches, self.dcaches = self.dcaches, self.caches

    def cache_shapes(self):
        return [(2, self.own_rows, HD)] * self.caches

    def dcache_shapes(self):
        return [(self.members, 2, self.part_rows, HD)]

    def load(self, caches):
        for i, ref in enumerate(caches):
            yield pl.ds(i * self.own_rows, self.own_rows), ref[0], ref[1]

    def store(self, dcaches, dk_sum, dv_sum, factor):
        me = lax.axis_index("resp")
        for shift in range(self.members):
            part = lax.rem(me - shift + self.members, self.members)
            at = pl.ds(shift * self.part_rows, self.part_rows)
            dcaches[0][part, 0] = (factor * dk_sum[at, :]).astype(BF16)
            dcaches[0][part, 1] = dv_sum[at, :].astype(BF16)


def attend(
    layout, pair, heads_per, lengths, queries, out_grad, caches, resp_keys, resp_values, earlier
):
    rows, query_width = queries.shape
    total_rows = layout.prompt_rows + rows
    first, last = pair * heads_per, (pair + 1) * heads_per - 1
    head_block = pl.BlockSpec((rows, HD), lambda s: (0, jnp.minimum(first + s, last)))
    late_block = pl.BlockSpec((rows, HD), lambda s: (0, jnp.maximum(first + s - 1, first)))
    pair_block = pl.BlockSpec((rows, HD), lambda s: (0, pair))
    cache_blocks = [
        pl.BlockSpec(shape, lambda s, rank=len(shape): (0,) * rank)
        for shape in layout.cache_shapes()
    ]
    dcache_blocks = [
        pl.BlockSpec(shape, lambda s, rank=len(shape): (0,) * rank)
        for shape in layout.dcache_shapes()
    ]
    stats = total_rows // SUB * 8
    in_specs = [
        pl.BlockSpec(memory_space=pltpu.SMEM),
        head_block,
        head_block,
        pair_block,
        pair_block,
        *cache_blocks,
    ] + [pl.BlockSpec(memory_space=pl.ANY)] * len(earlier)
    aliases = {5 + layout.caches + i: i for i in range(len(earlier))}
    return pl.pallas_call(
        functools.partial(attention_kernel, layout, heads_per, len(earlier)),
        grid=(heads_per + 1,),
        in_specs=in_specs,
        out_specs=[head_block, late_block, pair_block, pair_block, *dcache_blocks],
        out_shape=[
            jax.ShapeDtypeStruct(queries.shape, BF16),
            jax.ShapeDtypeStruct(queries.shape, BF16),
            jax.ShapeDtypeStruct(resp_keys.shape, BF16),
            jax.ShapeDtypeStruct(resp_keys.shape, BF16),
            *[jax.ShapeDtypeStruct(shape, BF16) for shape in layout.dcache_shapes()],
        ],
        scratch_shapes=[
            pltpu.VMEM((total_rows, HD), BF16),
            pltpu.VMEM((total_rows, HD), BF16),
            pltpu.VMEM((HD, total_rows), BF16),
            pltpu.VMEM((HD, total_rows), BF16),
            pltpu.VMEM((2, rows, HD), BF16),
            pltpu.VMEM((2, HD, rows), BF16),
            pltpu.VMEM((2, rows, HD), BF16),
            pltpu.VMEM((2, HD, rows), BF16),
            pltpu.VMEM((total_rows, rows), F32),
            pltpu.VMEM((total_rows, rows), F32),
            pltpu.VMEM((total_rows, rows), BF16),
            pltpu.VMEM((total_rows, rows), BF16),
            pltpu.VMEM((total_rows, rows), BF16),
            pltpu.VMEM((rows, rows), F32),
            pltpu.VMEM((rows, rows), F32),
            pltpu.VMEM((rows, rows), F32),
            pltpu.VMEM((rows, rows), F32),
            pltpu.VMEM((2, stats, rows), F32),
            pltpu.VMEM((2, 8, rows), F32),
            pltpu.VMEM((total_rows, HD), F32),
            pltpu.VMEM((total_rows, HD), F32),
            pltpu.VMEM((stats, rows), F32),
            pltpu.VMEM((stats, rows), F32),
        ],
        input_output_aliases=aliases,
        cost_estimate=pl.CostEstimate(
            flops=12 * heads_per * rows * total_rows * HD,
            bytes_accessed=8 * heads_per * rows * HD,
            transcendentals=heads_per * rows * total_rows,
        ),
        compiler_params=pltpu.CompilerParams(vmem_limit_bytes=60 * 1024 * 1024),
        name=f"attend_pair_{pair}",
    )(lengths, queries, out_grad, resp_keys, resp_values, *caches, *earlier)


def whole_block(shape):
    return pl.BlockSpec(shape, lambda: (0,) * len(shape))


def cut_kernel(pairs, k_ref, v_ref, *outs):
    me = lax.axis_index("tensor")
    ranks = len(outs) // pairs
    for p in range(pairs):
        for i in range(ranks):
            columns = pl.ds(pl.multiple_of(((me ^ i) * pairs + p) * HD, HD), HD)
            outs[p * ranks + i][0] = k_ref[:, columns]
            outs[p * ranks + i][1] = v_ref[:, columns]


def cut(prompt_keys, prompt_values, pairs):
    rows, columns = prompt_keys.shape
    count = columns // HD
    blocks = pl.pallas_call(
        functools.partial(cut_kernel, pairs),
        in_specs=[whole_block((rows, columns))] * 2,
        out_specs=[whole_block((2, rows, HD))] * count,
        out_shape=[jax.ShapeDtypeStruct((2, rows, HD), BF16)] * count,
        name="cut",
    )(prompt_keys, prompt_values)
    return [blocks[p * count // pairs : (p + 1) * count // pairs] for p in range(pairs)]


def place_kernel(members, pairs, *refs):
    *ins, dk_ref, dv_ref = refs
    me = lax.axis_index("tensor")
    ranks = dk_ref.shape[1] // HD // pairs
    for i in range(ranks):
        at = 0
        for p, count in enumerate(members):
            columns = pl.ds(pl.multiple_of(((me ^ i) * pairs + p) * HD, HD), HD)
            blocks = [ins[at + m * ranks + i] for m in range(count)]
            at += count * ranks
            dk_ref[:, columns] = sum(block[0].astype(F32) for block in blocks)
            dv_ref[:, columns] = sum(block[1].astype(F32) for block in blocks)


def place(blocks, members, pairs, columns):
    _, rows, _ = blocks[0].shape
    shape = (rows, columns)
    return pl.pallas_call(
        functools.partial(place_kernel, members, pairs),
        in_specs=[whole_block(blocks[0].shape)] * len(blocks),
        out_specs=[whole_block(shape)] * 2,
        out_shape=[jax.ShapeDtypeStruct(shape, F32)] * 2,
        name="place",
    )(*blocks)


def swap(blocks):
    count = len(blocks)
    return [blocks[0]] + [
        lax.ppermute(blocks[i], "tensor", [(j, j ^ i) for j in range(count)])
        for i in range(1, count)
    ]


def send(block, members, ranks, shift, i):
    if shift == 0 and i == 0:
        return block
    pairs = [
        (m * ranks + j, (m + shift) % members * ranks + (j ^ i))
        for m in range(members)
        for j in range(ranks)
    ]
    return lax.ppermute(block, ("resp", "tensor"), pairs)


def cut_rows(block, count):
    rows = block.shape[1] // count
    return [block[:, i * rows : (i + 1) * rows] for i in range(count)]


def per_device(
    members, ranks, queries, resp_keys, resp_values, prompt_keys, prompt_values, out_grad, lengths
):
    query_width = queries.shape[2]
    pair_width = resp_keys.shape[2]
    pairs = pair_width // HD
    heads_per = query_width // pair_width
    own_rows, columns = prompt_keys.shape
    queries, out_grad, resp_keys, resp_values = (
        a[0] for a in (queries, out_grad, resp_keys, resp_values)
    )
    cuts = cut(prompt_keys, prompt_values, pairs)
    kinds = [Scattered(members, ranks, own_rows)]
    kinds += [Gathered(members, ranks, own_rows) for _ in range(pairs - 1)]
    caches = [
        [send(cuts[0][i], members, ranks, shift, i) for shift in range(members) for i in range(ranks)]
    ]
    for p in range(1, pairs):
        own = jnp.concatenate(swap(cuts[p]), axis=1)
        own, caches[0] = lax.optimization_barrier((own, caches[0]))
        caches.append([lax.all_gather(own, "resp", axis=0)])
    earlier = ()
    total = None
    blocks, counts = [], []
    for p in range(pairs):
        results = attend(
            kinds[p],
            p,
            heads_per,
            lengths,
            queries,
            out_grad,
            caches[p],
            resp_keys,
            resp_values,
            earlier,
        )
        earlier, dcaches = results[:4], results[4:]
        if total is not None:
            dcaches, total = lax.optimization_barrier((dcaches, total))
            blocks += swap(cut_rows(total, ranks))
            counts.append(1)
            total = None
        if isinstance(kinds[p], Scattered):
            total = lax.psum_scatter(dcaches[0], "resp", scatter_dimension=0)
        else:
            blocks += [
                send(dcaches[shift * ranks + i], members, ranks, shift, i)
                for shift in range(members)
                for i in range(ranks)
            ]
            counts.append(members)
    if total is not None:
        blocks += swap(cut_rows(total, ranks))
        counts.append(1)
    key_grad, value_grad = place(blocks, counts, pairs, columns)
    return (*(a[None] for a in earlier), key_grad, value_grad)


def solution(mesh):
    rows = P(("group", "resp"), None, "tensor")
    prompt = P(("group", "resp", "tensor"), None)
    return jax.shard_map(
        functools.partial(per_device, mesh.shape["resp"], mesh.shape["tensor"]),
        mesh=mesh,
        in_specs=(rows, rows, rows, prompt, prompt, rows, P(("group", "resp"))),
        out_specs=(rows, rows, rows, rows, prompt, prompt),
        check_vma=False,
    )
```

```python
import functools
import math

import jax
import jax.numpy as jnp
from jax import lax
from jax.experimental import pallas as pl
from jax.experimental.pallas import tpu as pltpu
from jax.sharding import PartitionSpec as P

HD = 128
SUB = 128
LANES = 256
LOWEST = -1e30
BF16 = jnp.bfloat16
F32 = jnp.float32


def dot(a, b):
    return jnp.dot(a, b, preferred_element_type=F32)


def attention_kernel(
    layout,
    heads_per,
    earlier,
    len_ref,
    q_ref,
    g_ref,
    kr_ref,
    vr_ref,
    *rest,
):
    caches, rest = rest[: layout.caches], rest[layout.caches + earlier :]
    out_ref, dq_ref, dkr_ref, dvr_ref, *rest = rest
    dcaches, rest = rest[: layout.dcaches], rest[layout.dcaches :]
    (
        keys,
        values,
        keys_t,
        values_t,
        query,
        query_t,
        grad,
        grad_t,
        exps_even,
        exps_odd,
        weights_even,
        weights_odd,
        sgrads,
        fracs,
        deltas,
        dk_sum,
        dv_sum,
        tops,
        sums,
    ) = rest
    rows = q_ref.shape[0]
    prompt_rows = layout.prompt_rows
    total_rows = prompt_rows + rows
    half = rows // 2
    pieces = [(at, rows, 0) for at in range(0, prompt_rows, rows)]
    pieces += [(prompt_rows, half, 0), (prompt_rows + half, half, half)]
    count = len(pieces)
    factor = HD ** (-0.5)
    factor2 = factor * math.log2(math.e)
    length = len_ref[0]
    step = pl.program_id(0)
    exps = (exps_even, exps_odd)
    weights = (weights_even, weights_odd)

    @pl.when(step == 0)
    def _():
        for at, key_block, value_block in layout.load(caches):
            keys[at, :] = key_block
            values[at, :] = value_block
        for at in range(0, prompt_rows, rows):
            at = pl.ds(at, rows)
            keys_t[:, at] = keys[at, :].T
            values_t[:, at] = values[at, :].T
        at = pl.ds(prompt_rows, rows)
        keys[at, :] = kr_ref[...]
        values[at, :] = vr_ref[...]
        keys_t[:, at] = kr_ref[...].T
        values_t[:, at] = vr_ref[...].T
        dk_sum[...] = jnp.zeros_like(dk_sum)
        dv_sum[...] = jnp.zeros_like(dv_sum)
        tops[...] = jnp.full_like(tops, LOWEST)
        sums[...] = jnp.zeros_like(sums)
        for ref in (*weights, sgrads):
            ref[prompt_rows + half :, :half] = jnp.zeros((half, half), BF16)

    def blocks(piece):
        at, size, row = pieces[piece]
        for r in range(row, rows, LANES):
            for u in range(at, at + size, SUB):
                yield slice(u, u + SUB), slice(r, r + LANES)

    def stat(block_at):
        return slice(block_at.start // SUB * 8, block_at.start // SUB * 8 + 8)

    def tiled(block):
        return block.reshape(SUB // 8, 8, LANES)

    def score_chain(now, piece):
        for key_at, row_at in blocks(piece):
            block = dot(keys[key_at, :], query_t[now, :, row_at])
            if key_at.start >= prompt_rows:
                j = lax.broadcasted_iota(jnp.int32, (SUB, LANES), 0) + key_at.start - prompt_rows
                i = lax.broadcasted_iota(jnp.int32, (SUB, LANES), 1) + row_at.start
                block = jnp.where((j <= i) & (j < length), block, -jnp.inf)
            block = tiled(block) * factor2
            top = jnp.maximum(jnp.max(block, axis=0), LOWEST)
            exp = jnp.exp2(block - top[None])
            exps[now][key_at, row_at] = exp.reshape(SUB, LANES)
            tops[stat(key_at), row_at] = top
            sums[stat(key_at), row_at] = jnp.sum(exp, axis=0)

    def frac(slot, key_at, row_at):
        return tiled(exps[slot][key_at, row_at]) * fracs[slot, stat(key_at), row_at][None]

    def grad_chain(before, piece):
        for key_at, row_at in blocks(piece):
            dprob = tiled(dot(values[key_at, :], grad_t[before, :, row_at]))
            sgrad = frac(before, key_at, row_at) * (dprob - deltas[before, :, row_at][None])
            sgrads[key_at, row_at] = sgrad.reshape(SUB, LANES).astype(BF16)

    def grad_products(before, piece):
        at, size, row = pieces[piece]
        key_at = slice(at, at + size)
        dv_sum[key_at, :] += dot(weights[before][key_at, row:], grad[before, row:, :])
        dk_sum[key_at, :] += dot(sgrads[key_at, row:], query[before, row:, :])

    def run(now, with_score, with_grad):
        before = 1 - now
        for piece in range(count + 1):
            if piece < count:
                if with_score:
                    score_chain(now, piece)
                if with_grad:
                    grad_chain(before, piece)
            if piece >= 1 and with_grad:
                grad_products(before, piece - 1)
        if with_grad:
            dquery = dot(keys_t[...], sgrads[...])
            dq_ref[...] = (factor * dquery).T.astype(BF16)
        if with_score:
            finish(now)

    def prepare(now):
        live_rows = lax.broadcasted_iota(jnp.int32, (rows, HD), 0) < length
        live_grad = jnp.where(live_rows, g_ref[...].astype(F32), 0.0)
        grad[now] = live_grad.astype(BF16)
        grad_t[now] = live_grad.T.astype(BF16)
        query[now] = q_ref[...]
        query_t[now] = q_ref[...].T

    def finish(now):
        top = jnp.max(tops[...], axis=0, keepdims=True)
        scale = jnp.exp2(tops[...] - top)
        total = jnp.sum(scale * sums[...], axis=0, keepdims=True)
        fracs[now] = scale * (1.0 / total)
        for piece in range(count):
            for key_at, row_at in blocks(piece):
                weight = frac(now, key_at, row_at).reshape(SUB, LANES)
                weights[now][key_at, row_at] = weight.astype(BF16)
        mixture = dot(values_t[...], weights[now][...])
        live_lanes = lax.broadcasted_iota(jnp.int32, (HD, rows), 1) < length
        attended = jnp.where(live_lanes, mixture, 0.0).astype(BF16).astype(F32)
        out_ref[...] = attended.T.astype(BF16)
        delta = jnp.sum(grad_t[now].astype(F32) * attended, axis=0, keepdims=True)
        deltas[now] = jnp.broadcast_to(delta, (8, rows))

    @pl.when(step == 0)
    def _():
        prepare(0)
        run(0, True, False)

    for now in range(2):
        @pl.when((step > 0) & (step < heads_per) & (lax.rem(step, 2) == now))
        def _():
            prepare(now)
            run(now, True, True)

    @pl.when(step == heads_per)
    def _():
        run(heads_per % 2, False, True)
        layout.store(dcaches, dk_sum, dv_sum, factor)
        at = pl.ds(prompt_rows, rows)
        dkr_ref[...] = (factor * dk_sum[at, :]).astype(BF16)
        dvr_ref[...] = dv_sum[at, :].astype(BF16)


class Gathered:
    def __init__(self, members, ranks, own_rows):
        self.members, self.part_rows = members, ranks * own_rows
        self.prompt_rows = members * self.part_rows
        self.caches = 1
        self.dcaches = members

    def cache_shapes(self):
        return [(self.members, 2, self.part_rows, HD)]

    def dcache_shapes(self):
        return [(2, self.part_rows, HD)] * self.dcaches

    def load(self, caches):
        for m in range(self.members):
            at = pl.ds(m * self.part_rows, self.part_rows)
            yield at, caches[0][m, 0], caches[0][m, 1]

    def store(self, dcaches, dk_sum, dv_sum, factor):
        me = lax.axis_index("resp")
        for shift in range(self.members):
            part = lax.rem(me + shift, self.members) * self.part_rows
            at = pl.ds(pl.multiple_of(part, self.part_rows), self.part_rows)
            dcaches[shift][0] = (factor * dk_sum[at, :]).astype(BF16)
            dcaches[shift][1] = dv_sum[at, :].astype(BF16)


class Scattered(Gathered):
    def __init__(self, members, ranks, own_rows):
        super().__init__(members, ranks, own_rows)
        self.caches, self.dcaches = self.dcaches, self.caches

    def cache_shapes(self):
        return [(2, self.part_rows, HD)] * self.caches

    def dcache_shapes(self):
        return [(self.members, 2, self.part_rows, HD)]

    def load(self, caches):
        for i, ref in enumerate(caches):
            yield pl.ds(i * self.part_rows, self.part_rows), ref[0], ref[1]

    def store(self, dcaches, dk_sum, dv_sum, factor):
        me = lax.axis_index("resp")
        for shift in range(self.members):
            part = lax.rem(me - shift + self.members, self.members)
            at = pl.ds(shift * self.part_rows, self.part_rows)
            dcaches[0][part, 0] = (factor * dk_sum[at, :]).astype(BF16)
            dcaches[0][part, 1] = dv_sum[at, :].astype(BF16)


def attend(
    layout, pair, heads_per, lengths, queries, out_grad, caches, resp_keys, resp_values, earlier
):
    rows, query_width = queries.shape
    total_rows = layout.prompt_rows + rows
    first, last = pair * heads_per, (pair + 1) * heads_per - 1
    head_block = pl.BlockSpec((rows, HD), lambda s: (0, jnp.minimum(first + s, last)))
    late_block = pl.BlockSpec((rows, HD), lambda s: (0, jnp.maximum(first + s - 1, first)))
    pair_block = pl.BlockSpec((rows, HD), lambda s: (0, pair))
    cache_blocks = [
        pl.BlockSpec(shape, lambda s, rank=len(shape): (0,) * rank)
        for shape in layout.cache_shapes()
    ]
    dcache_blocks = [
        pl.BlockSpec(shape, lambda s, rank=len(shape): (0,) * rank)
        for shape in layout.dcache_shapes()
    ]
    stats = total_rows // SUB * 8
    in_specs = [
        pl.BlockSpec(memory_space=pltpu.SMEM),
        head_block,
        head_block,
        pair_block,
        pair_block,
        *cache_blocks,
    ] + [pl.BlockSpec(memory_space=pl.ANY)] * len(earlier)
    aliases = {5 + layout.caches + i: i for i in range(len(earlier))}
    return pl.pallas_call(
        functools.partial(attention_kernel, layout, heads_per, len(earlier)),
        grid=(heads_per + 1,),
        in_specs=in_specs,
        out_specs=[head_block, late_block, pair_block, pair_block, *dcache_blocks],
        out_shape=[
            jax.ShapeDtypeStruct(queries.shape, BF16),
            jax.ShapeDtypeStruct(queries.shape, BF16),
            jax.ShapeDtypeStruct(resp_keys.shape, BF16),
            jax.ShapeDtypeStruct(resp_keys.shape, BF16),
            *[jax.ShapeDtypeStruct(shape, BF16) for shape in layout.dcache_shapes()],
        ],
        scratch_shapes=[
            pltpu.VMEM((total_rows, HD), BF16),
            pltpu.VMEM((total_rows, HD), BF16),
            pltpu.VMEM((HD, total_rows), BF16),
            pltpu.VMEM((HD, total_rows), BF16),
            pltpu.VMEM((2, rows, HD), BF16),
            pltpu.VMEM((2, HD, rows), BF16),
            pltpu.VMEM((2, rows, HD), BF16),
            pltpu.VMEM((2, HD, rows), BF16),
            pltpu.VMEM((total_rows, rows), F32),
            pltpu.VMEM((total_rows, rows), F32),
            pltpu.VMEM((total_rows, rows), BF16),
            pltpu.VMEM((total_rows, rows), BF16),
            pltpu.VMEM((total_rows, rows), BF16),
            pltpu.VMEM((2, stats, rows), F32),
            pltpu.VMEM((2, 8, rows), F32),
            pltpu.VMEM((total_rows, HD), F32),
            pltpu.VMEM((total_rows, HD), F32),
            pltpu.VMEM((stats, rows), F32),
            pltpu.VMEM((stats, rows), F32),
        ],
        input_output_aliases=aliases,
        cost_estimate=pl.CostEstimate(
            flops=12 * heads_per * rows * total_rows * HD,
            bytes_accessed=8 * heads_per * rows * HD,
            transcendentals=heads_per * rows * total_rows,
        ),
        compiler_params=pltpu.CompilerParams(vmem_limit_bytes=60 * 1024 * 1024),
        name=f"attend_pair_{pair}",
    )(lengths, queries, out_grad, resp_keys, resp_values, *caches, *earlier)


def whole_block(shape):
    return pl.BlockSpec(shape, lambda: (0,) * len(shape))


def cut_kernel(pairs, k_ref, v_ref, *outs):
    me = lax.axis_index("tensor")
    ranks = len(outs) // pairs
    for p in range(pairs):
        for i in range(ranks):
            columns = pl.ds(pl.multiple_of(((me ^ i) * pairs + p) * HD, HD), HD)
            outs[p * ranks + i][0] = k_ref[:, columns]
            outs[p * ranks + i][1] = v_ref[:, columns]


def cut(prompt_keys, prompt_values, pairs):
    rows, columns = prompt_keys.shape
    count = columns // HD
    blocks = pl.pallas_call(
        functools.partial(cut_kernel, pairs),
        in_specs=[whole_block((rows, columns))] * 2,
        out_specs=[whole_block((2, rows, HD))] * count,
        out_shape=[jax.ShapeDtypeStruct((2, rows, HD), BF16)] * count,
        name="cut",
    )(prompt_keys, prompt_values)
    return [blocks[p * count // pairs : (p + 1) * count // pairs] for p in range(pairs)]


def place_kernel(pairs, *refs):
    *ins, dk_ref, dv_ref = refs
    me = lax.axis_index("tensor")
    ranks = len(ins) // pairs
    for p in range(pairs):
        for i in range(ranks):
            columns = pl.ds(pl.multiple_of(((me ^ i) * pairs + p) * HD, HD), HD)
            dk_ref[:, columns] = ins[p * ranks + i][0].astype(F32)
            dv_ref[:, columns] = ins[p * ranks + i][1].astype(F32)


def place(blocks, pairs, columns):
    _, rows, _ = blocks[0].shape
    shape = (rows, columns)
    return pl.pallas_call(
        functools.partial(place_kernel, pairs),
        in_specs=[whole_block(blocks[0].shape)] * len(blocks),
        out_specs=[whole_block(shape)] * 2,
        out_shape=[jax.ShapeDtypeStruct(shape, F32)] * 2,
        name="place",
    )(*blocks)


def swap(blocks):
    count = len(blocks)
    return [blocks[0]] + [
        lax.ppermute(blocks[i], "tensor", [(j, j ^ i) for j in range(count)])
        for i in range(1, count)
    ]


def send(block, members, shift):
    return lax.ppermute(block, "resp", [(m, (m + shift) % members) for m in range(members)])


def cut_rows(block, count):
    rows = block.shape[1] // count
    return [block[:, i * rows : (i + 1) * rows] for i in range(count)]


def per_device(
    members, ranks, queries, resp_keys, resp_values, prompt_keys, prompt_values, out_grad, lengths
):
    query_width = queries.shape[2]
    pair_width = resp_keys.shape[2]
    pairs = pair_width // HD
    heads_per = query_width // pair_width
    own_rows, columns = prompt_keys.shape
    queries, out_grad, resp_keys, resp_values = (
        a[0] for a in (queries, out_grad, resp_keys, resp_values)
    )
    cuts = cut(prompt_keys, prompt_values, pairs)
    kinds = [Scattered(members, ranks, own_rows)]
    kinds += [Gathered(members, ranks, own_rows) for _ in range(pairs - 1)]
    own = jnp.concatenate(swap(cuts[0]), axis=1)
    if pairs > 1:
        own, cuts[1:] = lax.optimization_barrier((own, cuts[1:]))
    caches = [[own] + [send(own, members, shift) for shift in range(1, members)]]
    for p in range(1, pairs):
        own = jnp.concatenate(swap(cuts[p]), axis=1)
        own, caches[0] = lax.optimization_barrier((own, caches[0]))
        caches.append([lax.all_gather(own, "resp", axis=0)])
    earlier = ()
    totals = []
    for p in range(pairs):
        results = attend(
            kinds[p],
            p,
            heads_per,
            lengths,
            queries,
            out_grad,
            caches[p],
            resp_keys,
            resp_values,
            earlier,
        )
        earlier, dcaches = results[:4], results[4:]
        if totals:
            dcaches, totals[-1] = lax.optimization_barrier((dcaches, totals[-1]))
        if isinstance(kinds[p], Scattered):
            totals.append(lax.psum_scatter(dcaches[0], "resp", scatter_dimension=0))
        else:
            arrived = [dcaches[0]] + [
                send(dcaches[shift], members, shift) for shift in range(1, members)
            ]
            totals.append(sum(block.astype(F32) for block in arrived).astype(BF16))
    blocks = [block for total in totals for block in swap(cut_rows(total, ranks))]
    key_grad, value_grad = place(blocks, pairs, columns)
    return (*(a[None] for a in earlier), key_grad, value_grad)


def solution(mesh):
    rows = P(("group", "resp"), None, "tensor")
    prompt = P(("group", "resp", "tensor"), None)
    return jax.shard_map(
        functools.partial(per_device, mesh.shape["resp"], mesh.shape["tensor"]),
        mesh=mesh,
        in_specs=(rows, rows, rows, prompt, prompt, rows, P(("group", "resp"))),
        out_specs=(rows, rows, rows, rows, prompt, prompt),
        check_vma=False,
    )
```

```python
import functools
import math

import jax
import jax.numpy as jnp
from jax import lax
from jax.experimental import pallas as pl
from jax.experimental.pallas import tpu as pltpu
from jax.sharding import PartitionSpec as P

HD = 128
SUB = 128
PIECE = 1024
LOWEST = -1e30
BF16 = jnp.bfloat16
F32 = jnp.float32


def dot(a, b):
    return jnp.dot(a, b, preferred_element_type=F32)


def attention_kernel(
    layout,
    heads_per,
    earlier,
    len_ref,
    q_ref,
    g_ref,
    kr_ref,
    vr_ref,
    *rest,
):
    caches, rest = rest[: layout.caches], rest[layout.caches + earlier :]
    out_ref, dkr_ref, dvr_ref, sgrads, keys_t, *rest = rest
    dcaches, rest = rest[: layout.dcaches], rest[layout.dcaches :]
    (
        keys,
        values,
        values_t,
        query,
        query_t,
        grad,
        grad_t,
        exps_even,
        exps_odd,
        weights_even,
        weights_odd,
        score_even,
        score_odd,
        dprob_even,
        dprob_odd,
        fracs,
        deltas,
        dk_sum,
        dv_sum,
        tops,
        sums,
    ) = rest
    rows = q_ref.shape[0]
    prompt_rows = layout.prompt_rows
    total_rows = prompt_rows + rows
    half = rows // 2
    pieces = [(at, PIECE, 0) for at in range(0, prompt_rows, PIECE)]
    pieces += [(prompt_rows, half, 0), (prompt_rows + half, half, half)]
    count = len(pieces)
    factor = HD ** (-0.5)
    factor2 = factor * math.log2(math.e)
    length = len_ref[0]
    step = pl.program_id(0)
    exps = (exps_even, exps_odd)
    weights = (weights_even, weights_odd)
    scores = (score_even, score_odd)
    dprobs = (dprob_even, dprob_odd)

    @pl.when(step == 0)
    def _():
        for at, key_block, value_block in layout.load(caches):
            keys[at, :] = key_block
            values[at, :] = value_block
        for at in range(0, prompt_rows, rows):
            at = pl.ds(at, rows)
            keys_t[:, at] = keys[at, :].T
            values_t[:, at] = values[at, :].T
        at = pl.ds(prompt_rows, rows)
        keys[at, :] = kr_ref[...]
        values[at, :] = vr_ref[...]
        keys_t[:, at] = kr_ref[...].T
        values_t[:, at] = vr_ref[...].T
        dk_sum[...] = jnp.zeros_like(dk_sum)
        dv_sum[...] = jnp.zeros_like(dv_sum)
        tops[...] = jnp.full_like(tops, LOWEST)
        sums[...] = jnp.zeros_like(sums)
        for ref in weights:
            ref[prompt_rows + half :, :half] = jnp.zeros((half, half), BF16)

    def blocks(piece):
        at, size, row = pieces[piece]
        for u in range(0, size, SUB):
            for r in range(0, rows - row, SUB):
                yield u, r, slice(at + u, at + u + SUB), slice(row + r, row + r + SUB)

    def stat(block_at):
        return slice(block_at.start // SUB * 8, block_at.start // SUB * 8 + 8)

    def score_product(now, piece):
        at, size, row = pieces[piece]
        scores[piece % 2][:size, : rows - row] = dot(
            keys[at : at + size, :], query_t[now, :, row:]
        )

    def score_chain(now, piece):
        for u, r, key_at, row_at in blocks(piece):
            block = scores[piece % 2][u : u + SUB, r : r + SUB]
            if key_at.start >= prompt_rows:
                j = lax.broadcasted_iota(jnp.int32, (SUB, SUB), 0) + key_at.start - prompt_rows
                i = lax.broadcasted_iota(jnp.int32, (SUB, SUB), 1) + row_at.start
                block = jnp.where((j <= i) & (j < length), block, -jnp.inf)
            block = block.reshape(SUB // 8, 8, SUB) * factor2
            top = jnp.maximum(jnp.max(block, axis=0), LOWEST)
            exp = jnp.exp2(block - top[None])
            exps[now][key_at, row_at] = exp.reshape(SUB, SUB)
            tops[stat(key_at), row_at] = top
            sums[stat(key_at), row_at] = jnp.sum(exp, axis=0)

    def frac(slot, key_at, row_at):
        block = exps[slot][key_at, row_at].reshape(SUB // 8, 8, SUB)
        return block * fracs[slot, stat(key_at), row_at][None]

    def dprob_product(before, piece):
        at, size, row = pieces[piece]
        dprobs[piece % 2][:size, : rows - row] = dot(
            values[at : at + size, :], grad_t[before, :, row:]
        )

    def grad_chain(before, piece):
        for u, r, key_at, row_at in blocks(piece):
            dprob = dprobs[piece % 2][u : u + SUB, r : r + SUB].reshape(SUB // 8, 8, SUB)
            sgrad = frac(before, key_at, row_at) * (dprob - deltas[before, :, row_at][None])
            sgrads[0, key_at, row_at] = sgrad.reshape(SUB, SUB).astype(BF16)

    def grad_products(before, piece):
        at, size, row = pieces[piece]
        key_at = slice(at, at + size)
        dv_sum[key_at, :] += dot(weights[before][key_at, row:], grad[before, row:, :])
        dk_sum[key_at, :] += dot(sgrads[0, key_at, row:], query[before, row:, :])

    def run(now, with_score, with_grad):
        before = 1 - now
        for stage in range(-1, count + 1):
            if stage + 1 < count:
                if with_score:
                    score_product(now, stage + 1)
                if with_grad:
                    dprob_product(before, stage + 1)
            if 0 <= stage < count:
                if with_score:
                    score_chain(now, stage)
                if with_grad:
                    grad_chain(before, stage)
            if stage >= 1 and with_grad:
                grad_products(before, stage - 1)
        if with_grad:
            sgrads[0, prompt_rows + half :, :half] = jnp.zeros((half, half), BF16)
        if with_score:
            finish(now)

    def prepare(now):
        live_rows = lax.broadcasted_iota(jnp.int32, (rows, HD), 0) < length
        live_grad = jnp.where(live_rows, g_ref[...].astype(F32), 0.0)
        grad[now] = live_grad.astype(BF16)
        grad_t[now] = live_grad.T.astype(BF16)
        query[now] = q_ref[...]
        query_t[now] = q_ref[...].T

    def finish(now):
        top = jnp.max(tops[...], axis=0, keepdims=True)
        scale = jnp.exp2(tops[...] - top)
        total = jnp.sum(scale * sums[...], axis=0, keepdims=True)
        fracs[now] = scale * (1.0 / total)
        for piece in range(count):
            for _, _, key_at, row_at in blocks(piece):
                weight = frac(now, key_at, row_at).reshape(SUB, SUB)
                weights[now][key_at, row_at] = weight.astype(BF16)
        mixture = dot(values_t[...], weights[now][...])
        live_lanes = lax.broadcasted_iota(jnp.int32, (HD, rows), 1) < length
        attended = jnp.where(live_lanes, mixture, 0.0).astype(BF16).astype(F32)
        out_ref[...] = attended.T.astype(BF16)
        delta = jnp.sum(grad_t[now].astype(F32) * attended, axis=0, keepdims=True)
        deltas[now] = jnp.broadcast_to(delta, (8, rows))

    @pl.when(step == 0)
    def _():
        prepare(0)
        run(0, True, False)

    for now in range(2):
        @pl.when((step > 0) & (step < heads_per) & (lax.rem(step, 2) == now))
        def _():
            prepare(now)
            run(now, True, True)

    @pl.when(step == heads_per)
    def _():
        run(heads_per % 2, False, True)
        layout.store(dcaches, dk_sum, dv_sum, factor)
        at = pl.ds(prompt_rows, rows)
        dkr_ref[...] = (factor * dk_sum[at, :]).astype(BF16)
        dvr_ref[...] = dv_sum[at, :].astype(BF16)


class Gathered:
    def __init__(self, members, ranks, own_rows):
        self.members, self.part_rows = members, ranks * own_rows
        self.prompt_rows = members * self.part_rows
        self.caches = 1
        self.dcaches = members

    def cache_shapes(self):
        return [(self.members, 2, self.part_rows, HD)]

    def dcache_shapes(self):
        return [(2, self.part_rows, HD)] * self.dcaches

    def load(self, caches):
        for m in range(self.members):
            at = pl.ds(m * self.part_rows, self.part_rows)
            yield at, caches[0][m, 0], caches[0][m, 1]

    def store(self, dcaches, dk_sum, dv_sum, factor):
        me = lax.axis_index("resp")
        for shift in range(self.members):
            part = lax.rem(me + shift, self.members) * self.part_rows
            at = pl.ds(pl.multiple_of(part, self.part_rows), self.part_rows)
            dcaches[shift][0] = (factor * dk_sum[at, :]).astype(BF16)
            dcaches[shift][1] = dv_sum[at, :].astype(BF16)


class Scattered(Gathered):
    def __init__(self, members, ranks, own_rows):
        super().__init__(members, ranks, own_rows)
        self.caches, self.dcaches = self.dcaches, self.caches

    def cache_shapes(self):
        return [(2, self.part_rows, HD)] * self.caches

    def dcache_shapes(self):
        return [(self.members, 2, self.part_rows, HD)]

    def load(self, caches):
        for i, ref in enumerate(caches):
            yield pl.ds(i * self.part_rows, self.part_rows), ref[0], ref[1]

    def store(self, dcaches, dk_sum, dv_sum, factor):
        me = lax.axis_index("resp")
        for shift in range(self.members):
            part = lax.rem(me - shift + self.members, self.members)
            at = pl.ds(shift * self.part_rows, self.part_rows)
            dcaches[0][part, 0] = (factor * dk_sum[at, :]).astype(BF16)
            dcaches[0][part, 1] = dv_sum[at, :].astype(BF16)


def attend(
    layout, pair, heads_per, lengths, queries, out_grad, caches, resp_keys, resp_values, earlier
):
    rows, query_width = queries.shape
    total_rows = layout.prompt_rows + rows
    first, last = pair * heads_per, (pair + 1) * heads_per - 1
    head_block = pl.BlockSpec((rows, HD), lambda s: (0, jnp.minimum(first + s, last)))
    late_block = pl.BlockSpec((1, total_rows, rows), lambda s: (jnp.maximum(s - 1, 0), 0, 0))
    keys_block = pl.BlockSpec((HD, total_rows), lambda s: (0, 0))
    pair_block = pl.BlockSpec((rows, HD), lambda s: (0, pair))
    cache_blocks = [
        pl.BlockSpec(shape, lambda s, rank=len(shape): (0,) * rank)
        for shape in layout.cache_shapes()
    ]
    dcache_blocks = [
        pl.BlockSpec(shape, lambda s, rank=len(shape): (0,) * rank)
        for shape in layout.dcache_shapes()
    ]
    stats = total_rows // SUB * 8
    in_specs = [
        pl.BlockSpec(memory_space=pltpu.SMEM),
        head_block,
        head_block,
        pair_block,
        pair_block,
        *cache_blocks,
    ] + [pl.BlockSpec(memory_space=pl.ANY)] * len(earlier)
    aliases = {5 + layout.caches + i: i for i in range(len(earlier))}
    return pl.pallas_call(
        functools.partial(attention_kernel, layout, heads_per, len(earlier)),
        grid=(heads_per + 1,),
        in_specs=in_specs,
        out_specs=[head_block, pair_block, pair_block, late_block, keys_block, *dcache_blocks],
        out_shape=[
            jax.ShapeDtypeStruct(queries.shape, BF16),
            jax.ShapeDtypeStruct(resp_keys.shape, BF16),
            jax.ShapeDtypeStruct(resp_keys.shape, BF16),
            jax.ShapeDtypeStruct((heads_per, total_rows, rows), BF16),
            jax.ShapeDtypeStruct((HD, total_rows), BF16),
            *[jax.ShapeDtypeStruct(shape, BF16) for shape in layout.dcache_shapes()],
        ],
        scratch_shapes=[
            pltpu.VMEM((total_rows, HD), BF16),
            pltpu.VMEM((total_rows, HD), BF16),
            pltpu.VMEM((HD, total_rows), BF16),
            pltpu.VMEM((2, rows, HD), BF16),
            pltpu.VMEM((2, HD, rows), BF16),
            pltpu.VMEM((2, rows, HD), BF16),
            pltpu.VMEM((2, HD, rows), BF16),
            pltpu.VMEM((total_rows, rows), F32),
            pltpu.VMEM((total_rows, rows), F32),
            pltpu.VMEM((total_rows, rows), BF16),
            pltpu.VMEM((total_rows, rows), BF16),
            pltpu.VMEM((PIECE, rows), F32),
            pltpu.VMEM((PIECE, rows), F32),
            pltpu.VMEM((PIECE, rows), F32),
            pltpu.VMEM((PIECE, rows), F32),
            pltpu.VMEM((2, stats, rows), F32),
            pltpu.VMEM((2, 8, rows), F32),
            pltpu.VMEM((total_rows, HD), F32),
            pltpu.VMEM((total_rows, HD), F32),
            pltpu.VMEM((stats, rows), F32),
            pltpu.VMEM((stats, rows), F32),
        ],
        input_output_aliases=aliases,
        cost_estimate=pl.CostEstimate(
            flops=12 * heads_per * rows * total_rows * HD,
            bytes_accessed=8 * heads_per * rows * HD,
            transcendentals=heads_per * rows * total_rows,
        ),
        compiler_params=pltpu.CompilerParams(vmem_limit_bytes=60 * 1024 * 1024),
        name=f"attend_pair_{pair}",
    )(lengths, queries, out_grad, resp_keys, resp_values, *caches, *earlier)


def query_grad_kernel(heads_per, *refs):
    *ins, dq_ref = refs
    pairs = len(ins) // 2
    step = pl.program_id(0)
    for p in range(pairs):
        @pl.when((step >= p * heads_per) & (step < (p + 1) * heads_per))
        def _():
            dquery = dot(ins[2 * p + 1][...], ins[2 * p][0])
            dq_ref[...] = (HD ** (-0.5) * dquery).T.astype(BF16)


def query_grads(sgrads, keys):
    heads_per, total_rows, rows = sgrads[0].shape
    pairs = len(sgrads)
    in_specs = []
    for p in range(pairs):
        in_specs.append(
            pl.BlockSpec(
                (1, total_rows, rows),
                lambda s, p=p: (jnp.clip(s - p * heads_per, 0, heads_per - 1), 0, 0),
            )
        )
        in_specs.append(pl.BlockSpec((HD, total_rows), lambda s: (0, 0)))
    return pl.pallas_call(
        functools.partial(query_grad_kernel, heads_per),
        grid=(pairs * heads_per,),
        in_specs=in_specs,
        out_specs=pl.BlockSpec((rows, HD), lambda s: (0, s)),
        out_shape=jax.ShapeDtypeStruct((rows, pairs * heads_per * HD), BF16),
        cost_estimate=pl.CostEstimate(
            flops=2 * pairs * heads_per * rows * total_rows * HD,
            bytes_accessed=2 * pairs * heads_per * rows * total_rows,
            transcendentals=0,
        ),
        compiler_params=pltpu.CompilerParams(vmem_limit_bytes=60 * 1024 * 1024),
        name="query_grads",
    )(*[a for both in zip(sgrads, keys) for a in both])


def whole_block(shape):
    return pl.BlockSpec(shape, lambda: (0,) * len(shape))


def cut_kernel(pairs, k_ref, v_ref, *outs):
    me = lax.axis_index("tensor")
    ranks = len(outs) // pairs
    for p in range(pairs):
        for i in range(ranks):
            columns = pl.ds(pl.multiple_of(((me ^ i) * pairs + p) * HD, HD), HD)
            outs[p * ranks + i][0] = k_ref[:, columns]
            outs[p * ranks + i][1] = v_ref[:, columns]


def cut(prompt_keys, prompt_values, pairs):
    rows, columns = prompt_keys.shape
    count = columns // HD
    blocks = pl.pallas_call(
        functools.partial(cut_kernel, pairs),
        in_specs=[whole_block((rows, columns))] * 2,
        out_specs=[whole_block((2, rows, HD))] * count,
        out_shape=[jax.ShapeDtypeStruct((2, rows, HD), BF16)] * count,
        name="cut",
    )(prompt_keys, prompt_values)
    return [blocks[p * count // pairs : (p + 1) * count // pairs] for p in range(pairs)]


def place_kernel(pairs, *refs):
    *ins, dk_ref, dv_ref = refs
    me = lax.axis_index("tensor")
    ranks = len(ins) // pairs
    for p in range(pairs):
        for i in range(ranks):
            columns = pl.ds(pl.multiple_of(((me ^ i) * pairs + p) * HD, HD), HD)
            dk_ref[:, columns] = ins[p * ranks + i][0].astype(F32)
            dv_ref[:, columns] = ins[p * ranks + i][1].astype(F32)


def place(blocks, pairs, columns):
    _, rows, _ = blocks[0].shape
    shape = (rows, columns)
    return pl.pallas_call(
        functools.partial(place_kernel, pairs),
        in_specs=[whole_block(blocks[0].shape)] * len(blocks),
        out_specs=[whole_block(shape)] * 2,
        out_shape=[jax.ShapeDtypeStruct(shape, F32)] * 2,
        name="place",
    )(*blocks)


def swap(blocks):
    count = len(blocks)
    return [blocks[0]] + [
        lax.ppermute(blocks[i], "tensor", [(j, j ^ i) for j in range(count)])
        for i in range(1, count)
    ]


def send(block, members, shift):
    return lax.ppermute(block, "resp", [(m, (m + shift) % members) for m in range(members)])


def cut_rows(block, count):
    rows = block.shape[1] // count
    return [block[:, i * rows : (i + 1) * rows] for i in range(count)]


def per_device(
    members, ranks, queries, resp_keys, resp_values, prompt_keys, prompt_values, out_grad, lengths
):
    query_width = queries.shape[2]
    pair_width = resp_keys.shape[2]
    pairs = pair_width // HD
    heads_per = query_width // pair_width
    own_rows, columns = prompt_keys.shape
    queries, out_grad, resp_keys, resp_values = (
        a[0] for a in (queries, out_grad, resp_keys, resp_values)
    )
    cuts = cut(prompt_keys, prompt_values, pairs)
    kinds = [Scattered(members, ranks, own_rows)]
    kinds += [Gathered(members, ranks, own_rows) for _ in range(pairs - 1)]
    own = jnp.concatenate(swap(cuts[0]), axis=1)
    if pairs > 1:
        own, cuts[1:] = lax.optimization_barrier((own, cuts[1:]))
    caches = [[own] + [send(own, members, shift) for shift in range(1, members)]]
    for p in range(1, pairs):
        own = jnp.concatenate(swap(cuts[p]), axis=1)
        own, caches[0] = lax.optimization_barrier((own, caches[0]))
        caches.append([lax.all_gather(own, "resp", axis=0)])
    earlier = ()
    totals, sgrads, keys = [], [], []
    for p in range(pairs):
        results = attend(
            kinds[p],
            p,
            heads_per,
            lengths,
            queries,
            out_grad,
            caches[p],
            resp_keys,
            resp_values,
            earlier,
        )
        earlier, (sgrad, key), dcaches = results[:3], results[3:5], results[5:]
        sgrads.append(sgrad)
        keys.append(key)
        if totals:
            dcaches, totals[-1] = lax.optimization_barrier((dcaches, totals[-1]))
        if isinstance(kinds[p], Scattered):
            totals.append(lax.psum_scatter(dcaches[0], "resp", scatter_dimension=0))
        else:
            totals.append(
                [dcaches[0]]
                + [send(dcaches[shift], members, shift) for shift in range(1, members)]
            )
    sgrads = lax.optimization_barrier(sgrads)
    dquery = query_grads(sgrads, keys)
    if isinstance(totals[-1], list):
        dquery, arrived = lax.optimization_barrier((dquery, totals[-1]))
        totals[-1] = sum(block.astype(F32) for block in arrived).astype(BF16)
    blocks = [block for total in totals for block in swap(cut_rows(total, ranks))]
    key_grad, value_grad = place(blocks, pairs, columns)
    attended, resp_key_grad, resp_value_grad = (a[None] for a in earlier)
    return attended, dquery[None], resp_key_grad, resp_value_grad, key_grad, value_grad


def solution(mesh):
    rows = P(("group", "resp"), None, "tensor")
    prompt = P(("group", "resp", "tensor"), None)
    return jax.shard_map(
        functools.partial(per_device, mesh.shape["resp"], mesh.shape["tensor"]),
        mesh=mesh,
        in_specs=(rows, rows, rows, prompt, prompt, rows, P(("group", "resp"))),
        out_specs=(rows, rows, rows, rows, prompt, prompt),
        check_vma=False,
    )
```

```python
import functools
import math

import jax
import jax.numpy as jnp
from jax import lax
from jax.experimental import pallas as pl
from jax.experimental.pallas import tpu as pltpu
from jax.sharding import PartitionSpec as P

HD = 128
SUB = 128
WIDE = 256
LOWEST = -1e30
BF16 = jnp.bfloat16
F32 = jnp.float32


def dot(a, b):
    return jnp.dot(a, b, preferred_element_type=F32)


def attention_kernel(
    layout,
    heads_per,
    earlier,
    len_ref,
    q_ref,
    g_ref,
    kr_ref,
    vr_ref,
    *rest,
):
    caches, rest = rest[: layout.caches], rest[layout.caches + earlier :]
    out_ref, dq_ref, dkr_ref, dvr_ref, *rest = rest
    dcaches, rest = rest[: layout.dcaches], rest[layout.dcaches :]
    (
        keys,
        values,
        keys_t,
        values_t,
        query,
        query_t,
        grad,
        grad_t,
        exps_even,
        exps_odd,
        weights_even,
        weights_odd,
        sgrads,
        score_even,
        score_odd,
        dprob_even,
        dprob_odd,
        fracs,
        deltas,
        dk_sum,
        dv_sum,
        tops,
        sums,
        mixture,
    ) = rest
    rows = q_ref.shape[0]
    prompt_rows = layout.prompt_rows
    total_rows = prompt_rows + rows
    half = rows // 2
    pieces = [(at, rows, 0) for at in range(0, prompt_rows, rows)]
    pieces += [(prompt_rows, half, 0), (prompt_rows + half, half, half)]
    count = len(pieces)
    factor = HD ** (-0.5)
    factor2 = factor * math.log2(math.e)
    length = len_ref[0]
    step = pl.program_id(0)
    exps = (exps_even, exps_odd)
    weights = (weights_even, weights_odd)
    scores = (score_even, score_odd)
    dprobs = (dprob_even, dprob_odd)

    @pl.when(step == 0)
    def _():
        for at, key_block, value_block in layout.load(caches):
            keys[at, :] = key_block
            values[at, :] = value_block
        for at in range(0, prompt_rows, rows):
            at = pl.ds(at, rows)
            keys_t[:, at] = keys[at, :].T
            values_t[:, at] = values[at, :].T
        at = pl.ds(prompt_rows, rows)
        keys[at, :] = kr_ref[...]
        values[at, :] = vr_ref[...]
        keys_t[:, at] = kr_ref[...].T
        values_t[:, at] = vr_ref[...].T
        dk_sum[...] = jnp.zeros_like(dk_sum)
        dv_sum[...] = jnp.zeros_like(dv_sum)
        tops[...] = jnp.full_like(tops, LOWEST)
        sums[...] = jnp.zeros_like(sums)
        for ref in (*weights, sgrads):
            ref[prompt_rows + half :, :half] = jnp.zeros((half, half), BF16)

    def blocks(piece):
        at, size, row = pieces[piece]
        for u in range(0, size, SUB):
            for r in range(0, rows - row, SUB):
                yield u, r, slice(at + u, at + u + SUB), slice(row + r, row + r + SUB)

    def stat(block_at):
        return slice(block_at.start // SUB * 8, block_at.start // SUB * 8 + 8)

    def tiled(block):
        return block.reshape(SUB // 8, 8, SUB)

    def score_products(now, piece):
        at, size, row = pieces[piece]

        def product(r):
            scores[piece % 2][:size, r - row : r - row + WIDE] = dot(
                keys[at : at + size, :], query_t[now, :, r : r + WIDE]
            )

        return [functools.partial(product, r) for r in range(row, rows, WIDE)]

    def dprob_products(before, piece):
        at, size, row = pieces[piece]

        def product(r):
            dprobs[piece % 2][:size, r - row : r - row + WIDE] = dot(
                values[at : at + size, :], grad_t[before, :, r : r + WIDE]
            )

        return [functools.partial(product, r) for r in range(row, rows, WIDE)]

    def score_chains(now, piece):
        def chain(u, r, key_at, row_at):
            block = scores[piece % 2][u : u + SUB, r : r + SUB]
            if key_at.start >= prompt_rows:
                j = lax.broadcasted_iota(jnp.int32, (SUB, SUB), 0) + key_at.start - prompt_rows
                i = lax.broadcasted_iota(jnp.int32, (SUB, SUB), 1) + row_at.start
                block = jnp.where((j <= i) & (j < length), block, -jnp.inf)
            block = tiled(block) * factor2
            top = jnp.maximum(jnp.max(block, axis=0), LOWEST)
            exp = jnp.exp2(block - top[None])
            exps[now][key_at, row_at] = exp.reshape(SUB, SUB)
            tops[stat(key_at), row_at] = top
            sums[stat(key_at), row_at] = jnp.sum(exp, axis=0)

        return [functools.partial(chain, *block) for block in blocks(piece)]

    def frac(slot, key_at, row_at):
        return tiled(exps[slot][key_at, row_at]) * fracs[slot, stat(key_at), row_at][None]

    def grad_chains(before, piece):
        def chain(u, r, key_at, row_at):
            dprob = tiled(dprobs[piece % 2][u : u + SUB, r : r + SUB])
            sgrad = frac(before, key_at, row_at) * (dprob - deltas[before, :, row_at][None])
            sgrads[key_at, row_at] = sgrad.reshape(SUB, SUB).astype(BF16)

        return [functools.partial(chain, *block) for block in blocks(piece)]

    def weight_chains(now, piece):
        def chain(u, r, key_at, row_at):
            weight = frac(now, key_at, row_at).reshape(SUB, SUB)
            weights[now][key_at, row_at] = weight.astype(BF16)

        return [functools.partial(chain, *block) for block in blocks(piece)]

    def grad_products(before, piece):
        at, size, row = pieces[piece]

        def value_product(u):
            at = slice(u, u + WIDE)
            dv_sum[at, :] += dot(weights[before][at, row:], grad[before, row:, :])

        def key_product(u):
            at = slice(u, u + WIDE)
            dk_sum[at, :] += dot(sgrads[at, row:], query[before, row:, :])

        return [
            functools.partial(product, u)
            for u in range(at, at + size, WIDE)
            for product in (value_product, key_product)
        ]

    def query_products():
        def product(r):
            dquery = dot(keys_t[...], sgrads[:, r : r + WIDE])
            dq_ref[r : r + WIDE, :] = (factor * dquery).T.astype(BF16)

        return [functools.partial(product, r) for r in range(0, rows, WIDE)]

    def out_products(now, piece):
        at, size, row = pieces[piece]

        def product(r):
            term = dot(values_t[:, at : at + size], weights[now][at : at + size, r : r + WIDE])
            if piece:
                term += mixture[:, r : r + WIDE]
            mixture[:, r : r + WIDE] = term

        return [functools.partial(product, r) for r in range(row, rows, WIDE)]

    def weave(products, chains):
        count = max(len(products), len(chains))
        for i in range(count):
            for jobs in (products, chains):
                for job in jobs[i * len(jobs) // count : (i + 1) * len(jobs) // count]:
                    job()

    def run(now, with_score, with_grad):
        before = 1 - now
        for stage in range(-1, count):
            products, chains = [], []
            if stage + 1 < count:
                if with_score:
                    products += score_products(now, stage + 1)
                if with_grad:
                    products += dprob_products(before, stage + 1)
            if stage >= 1 and with_grad:
                products += grad_products(before, stage - 1)
            if stage >= 0:
                both = [score_chains(now, stage)] if with_score else []
                both += [grad_chains(before, stage)] if with_grad else []
                chains = [chain for pair in zip(*both) for chain in pair]
            weave(products, chains)
        products = []
        if with_grad:
            products += grad_products(before, count - 1) + query_products()
        chains = []
        if with_score:
            set_fracs(now)
            chains = weight_chains(now, 0)
        weave(products, chains)
        if with_score:
            for piece in range(count):
                weave(
                    out_products(now, piece),
                    weight_chains(now, piece + 1) if piece + 1 < count else [],
                )
            finish(now)

    def prepare(now):
        live_rows = lax.broadcasted_iota(jnp.int32, (rows, HD), 0) < length
        live_grad = jnp.where(live_rows, g_ref[...].astype(F32), 0.0)
        grad[now] = live_grad.astype(BF16)
        grad_t[now] = live_grad.T.astype(BF16)
        query[now] = q_ref[...]
        query_t[now] = q_ref[...].T

    def set_fracs(now):
        top = jnp.max(tops[...], axis=0, keepdims=True)
        scale = jnp.exp2(tops[...] - top)
        total = jnp.sum(scale * sums[...], axis=0, keepdims=True)
        fracs[now] = scale * (1.0 / total)

    def finish(now):
        live_lanes = lax.broadcasted_iota(jnp.int32, (HD, rows), 1) < length
        attended = jnp.where(live_lanes, mixture[...], 0.0).astype(BF16).astype(F32)
        out_ref[...] = attended.T.astype(BF16)
        delta = jnp.sum(grad_t[now].astype(F32) * attended, axis=0, keepdims=True)
        deltas[now] = jnp.broadcast_to(delta, (8, rows))

    @pl.when(step == 0)
    def _():
        prepare(0)
        run(0, True, False)

    for now in range(2):
        @pl.when((step > 0) & (step < heads_per) & (lax.rem(step, 2) == now))
        def _():
            prepare(now)
            run(now, True, True)

    @pl.when(step == heads_per)
    def _():
        run(heads_per % 2, False, True)
        layout.store(dcaches, dk_sum, dv_sum, factor)
        at = pl.ds(prompt_rows, rows)
        dkr_ref[...] = (factor * dk_sum[at, :]).astype(BF16)
        dvr_ref[...] = dv_sum[at, :].astype(BF16)


class Gathered:
    def __init__(self, members, ranks, own_rows):
        self.members, self.part_rows = members, ranks * own_rows
        self.prompt_rows = members * self.part_rows
        self.caches = 1
        self.dcaches = members

    def cache_shapes(self):
        return [(self.members, 2, self.part_rows, HD)]

    def dcache_shapes(self):
        return [(2, self.part_rows, HD)] * self.dcaches

    def load(self, caches):
        for m in range(self.members):
            at = pl.ds(m * self.part_rows, self.part_rows)
            yield at, caches[0][m, 0], caches[0][m, 1]

    def store(self, dcaches, dk_sum, dv_sum, factor):
        me = lax.axis_index("resp")
        for shift in range(self.members):
            part = lax.rem(me + shift, self.members) * self.part_rows
            at = pl.ds(pl.multiple_of(part, self.part_rows), self.part_rows)
            dcaches[shift][0] = (factor * dk_sum[at, :]).astype(BF16)
            dcaches[shift][1] = dv_sum[at, :].astype(BF16)


class Scattered(Gathered):
    def __init__(self, members, ranks, own_rows):
        super().__init__(members, ranks, own_rows)
        self.caches, self.dcaches = self.dcaches, self.caches

    def cache_shapes(self):
        return [(2, self.part_rows, HD)] * self.caches

    def dcache_shapes(self):
        return [(self.members, 2, self.part_rows, HD)]

    def load(self, caches):
        for i, ref in enumerate(caches):
            yield pl.ds(i * self.part_rows, self.part_rows), ref[0], ref[1]

    def store(self, dcaches, dk_sum, dv_sum, factor):
        me = lax.axis_index("resp")
        for shift in range(self.members):
            part = lax.rem(me - shift + self.members, self.members)
            at = pl.ds(shift * self.part_rows, self.part_rows)
            dcaches[0][part, 0] = (factor * dk_sum[at, :]).astype(BF16)
            dcaches[0][part, 1] = dv_sum[at, :].astype(BF16)


def attend(
    layout, pair, heads_per, lengths, queries, out_grad, caches, resp_keys, resp_values, earlier
):
    rows, query_width = queries.shape
    total_rows = layout.prompt_rows + rows
    first, last = pair * heads_per, (pair + 1) * heads_per - 1
    head_block = pl.BlockSpec((rows, HD), lambda s: (0, jnp.minimum(first + s, last)))
    late_block = pl.BlockSpec((rows, HD), lambda s: (0, jnp.maximum(first + s - 1, first)))
    pair_block = pl.BlockSpec((rows, HD), lambda s: (0, pair))
    cache_blocks = [
        pl.BlockSpec(shape, lambda s, rank=len(shape): (0,) * rank)
        for shape in layout.cache_shapes()
    ]
    dcache_blocks = [
        pl.BlockSpec(shape, lambda s, rank=len(shape): (0,) * rank)
        for shape in layout.dcache_shapes()
    ]
    stats = total_rows // SUB * 8
    in_specs = [
        pl.BlockSpec(memory_space=pltpu.SMEM),
        head_block,
        head_block,
        pair_block,
        pair_block,
        *cache_blocks,
    ] + [pl.BlockSpec(memory_space=pl.ANY)] * len(earlier)
    aliases = {5 + layout.caches + i: i for i in range(len(earlier))}
    return pl.pallas_call(
        functools.partial(attention_kernel, layout, heads_per, len(earlier)),
        grid=(heads_per + 1,),
        in_specs=in_specs,
        out_specs=[head_block, late_block, pair_block, pair_block, *dcache_blocks],
        out_shape=[
            jax.ShapeDtypeStruct(queries.shape, BF16),
            jax.ShapeDtypeStruct(queries.shape, BF16),
            jax.ShapeDtypeStruct(resp_keys.shape, BF16),
            jax.ShapeDtypeStruct(resp_keys.shape, BF16),
            *[jax.ShapeDtypeStruct(shape, BF16) for shape in layout.dcache_shapes()],
        ],
        scratch_shapes=[
            pltpu.VMEM((total_rows, HD), BF16),
            pltpu.VMEM((total_rows, HD), BF16),
            pltpu.VMEM((HD, total_rows), BF16),
            pltpu.VMEM((HD, total_rows), BF16),
            pltpu.VMEM((2, rows, HD), BF16),
            pltpu.VMEM((2, HD, rows), BF16),
            pltpu.VMEM((2, rows, HD), BF16),
            pltpu.VMEM((2, HD, rows), BF16),
            pltpu.VMEM((total_rows, rows), F32),
            pltpu.VMEM((total_rows, rows), F32),
            pltpu.VMEM((total_rows, rows), BF16),
            pltpu.VMEM((total_rows, rows), BF16),
            pltpu.VMEM((total_rows, rows), BF16),
            pltpu.VMEM((rows, rows), F32),
            pltpu.VMEM((rows, rows), F32),
            pltpu.VMEM((rows, rows), F32),
            pltpu.VMEM((rows, rows), F32),
            pltpu.VMEM((2, stats, rows), F32),
            pltpu.VMEM((2, 8, rows), F32),
            pltpu.VMEM((total_rows, HD), F32),
            pltpu.VMEM((total_rows, HD), F32),
            pltpu.VMEM((stats, rows), F32),
            pltpu.VMEM((stats, rows), F32),
            pltpu.VMEM((HD, rows), F32),
        ],
        input_output_aliases=aliases,
        cost_estimate=pl.CostEstimate(
            flops=12 * heads_per * rows * total_rows * HD,
            bytes_accessed=8 * heads_per * rows * HD,
            transcendentals=heads_per * rows * total_rows,
        ),
        compiler_params=pltpu.CompilerParams(vmem_limit_bytes=60 * 1024 * 1024),
        name=f"attend_pair_{pair}",
    )(lengths, queries, out_grad, resp_keys, resp_values, *caches, *earlier)


def whole_block(shape):
    return pl.BlockSpec(shape, lambda: (0,) * len(shape))


def cut_kernel(pairs, k_ref, v_ref, *outs):
    me = lax.axis_index("tensor")
    ranks = len(outs) // pairs
    for p in range(pairs):
        for i in range(ranks):
            columns = pl.ds(pl.multiple_of(((me ^ i) * pairs + p) * HD, HD), HD)
            outs[p * ranks + i][0] = k_ref[:, columns]
            outs[p * ranks + i][1] = v_ref[:, columns]


def cut(prompt_keys, prompt_values, pairs):
    rows, columns = prompt_keys.shape
    count = columns // HD
    blocks = pl.pallas_call(
        functools.partial(cut_kernel, pairs),
        in_specs=[whole_block((rows, columns))] * 2,
        out_specs=[whole_block((2, rows, HD))] * count,
        out_shape=[jax.ShapeDtypeStruct((2, rows, HD), BF16)] * count,
        name="cut",
    )(prompt_keys, prompt_values)
    return [blocks[p * count // pairs : (p + 1) * count // pairs] for p in range(pairs)]


def place_kernel(pairs, *refs):
    *ins, dk_ref, dv_ref = refs
    me = lax.axis_index("tensor")
    ranks = len(ins) // pairs
    for p in range(pairs):
        for i in range(ranks):
            columns = pl.ds(pl.multiple_of(((me ^ i) * pairs + p) * HD, HD), HD)
            dk_ref[:, columns] = ins[p * ranks + i][0].astype(F32)
            dv_ref[:, columns] = ins[p * ranks + i][1].astype(F32)


def place(blocks, pairs, columns):
    _, rows, _ = blocks[0].shape
    shape = (rows, columns)
    return pl.pallas_call(
        functools.partial(place_kernel, pairs),
        in_specs=[whole_block(blocks[0].shape)] * len(blocks),
        out_specs=[whole_block(shape)] * 2,
        out_shape=[jax.ShapeDtypeStruct(shape, F32)] * 2,
        name="place",
    )(*blocks)


def swap(blocks):
    count = len(blocks)
    return [blocks[0]] + [
        lax.ppermute(blocks[i], "tensor", [(j, j ^ i) for j in range(count)])
        for i in range(1, count)
    ]


def send(block, members, shift):
    return lax.ppermute(block, "resp", [(m, (m + shift) % members) for m in range(members)])


def cut_rows(block, count):
    rows = block.shape[1] // count
    return [block[:, i * rows : (i + 1) * rows] for i in range(count)]


def per_device(
    members, ranks, queries, resp_keys, resp_values, prompt_keys, prompt_values, out_grad, lengths
):
    query_width = queries.shape[2]
    pair_width = resp_keys.shape[2]
    pairs = pair_width // HD
    heads_per = query_width // pair_width
    own_rows, columns = prompt_keys.shape
    queries, out_grad, resp_keys, resp_values = (
        a[0] for a in (queries, out_grad, resp_keys, resp_values)
    )
    cuts = cut(prompt_keys, prompt_values, pairs)
    kinds = [Scattered(members, ranks, own_rows)]
    kinds += [Gathered(members, ranks, own_rows) for _ in range(pairs - 1)]
    own = jnp.concatenate(swap(cuts[0]), axis=1)
    if pairs > 1:
        own, cuts[1:] = lax.optimization_barrier((own, cuts[1:]))
    caches = [[own] + [send(own, members, shift) for shift in range(1, members)]]
    for p in range(1, pairs):
        own = jnp.concatenate(swap(cuts[p]), axis=1)
        own, caches[0] = lax.optimization_barrier((own, caches[0]))
        caches.append([lax.all_gather(own, "resp", axis=0)])
    earlier = ()
    totals = []
    for p in range(pairs):
        results = attend(
            kinds[p],
            p,
            heads_per,
            lengths,
            queries,
            out_grad,
            caches[p],
            resp_keys,
            resp_values,
            earlier,
        )
        earlier, dcaches = results[:4], results[4:]
        if totals:
            dcaches, totals[-1] = lax.optimization_barrier((dcaches, totals[-1]))
        if isinstance(kinds[p], Scattered):
            totals.append(lax.psum_scatter(dcaches[0], "resp", scatter_dimension=0))
        else:
            arrived = [dcaches[0]] + [
                send(dcaches[shift], members, shift) for shift in range(1, members)
            ]
            totals.append(sum(block.astype(F32) for block in arrived).astype(BF16))
    blocks = [block for total in totals for block in swap(cut_rows(total, ranks))]
    key_grad, value_grad = place(blocks, pairs, columns)
    return (*(a[None] for a in earlier), key_grad, value_grad)


def solution(mesh):
    rows = P(("group", "resp"), None, "tensor")
    prompt = P(("group", "resp", "tensor"), None)
    return jax.shard_map(
        functools.partial(per_device, mesh.shape["resp"], mesh.shape["tensor"]),
        mesh=mesh,
        in_specs=(rows, rows, rows, prompt, prompt, rows, P(("group", "resp"))),
        out_specs=(rows, rows, rows, rows, prompt, prompt),
        check_vma=False,
    )
```

```python
import functools
import math

import jax
import jax.numpy as jnp
from jax import lax
from jax.experimental import pallas as pl
from jax.experimental.pallas import tpu as pltpu
from jax.sharding import PartitionSpec as P

HD = 128
SUB = 128
WIDE = 256
LOWEST = -1e30
BF16 = jnp.bfloat16
F32 = jnp.float32


def dot(a, b):
    return jnp.dot(a, b, preferred_element_type=F32)


def attention_kernel(
    layout,
    heads_per,
    earlier,
    len_ref,
    q_ref,
    qt_ref,
    g_ref,
    gt_ref,
    kr_ref,
    vr_ref,
    *rest,
):
    caches, rest = rest[: layout.caches], rest[layout.caches + earlier :]
    out_ref, dq_ref, dkr_ref, dvr_ref, *rest = rest
    dcaches, rest = rest[: layout.dcaches], rest[layout.dcaches :]
    (
        keys,
        values,
        keys_t,
        values_t,
        query,
        query_t,
        grad,
        grad_t,
        exps_even,
        exps_odd,
        weights_even,
        weights_odd,
        sgrads,
        score_even,
        score_odd,
        dprob_even,
        dprob_odd,
        fracs,
        deltas,
        dk_sum,
        dv_sum,
        tops,
        sums,
        mixture,
    ) = rest
    rows = q_ref.shape[0]
    prompt_rows = layout.prompt_rows
    total_rows = prompt_rows + rows
    half = rows // 2
    pieces = [(at, rows, 0) for at in range(0, prompt_rows, rows)]
    pieces += [(prompt_rows, half, 0), (prompt_rows + half, half, half)]
    count = len(pieces)
    factor = HD ** (-0.5)
    factor2 = factor * math.log2(math.e)
    length = len_ref[0]
    step = pl.program_id(0)
    exps = (exps_even, exps_odd)
    weights = (weights_even, weights_odd)
    scores = (score_even, score_odd)
    dprobs = (dprob_even, dprob_odd)

    @pl.when(step == 0)
    def _():
        for at, key_block, value_block in layout.load(caches):
            keys[at, :] = key_block
            values[at, :] = value_block
        for at in range(0, prompt_rows, rows):
            at = pl.ds(at, rows)
            keys_t[:, at] = keys[at, :].T
            values_t[:, at] = values[at, :].T
        at = pl.ds(prompt_rows, rows)
        keys[at, :] = kr_ref[...]
        values[at, :] = vr_ref[...]
        keys_t[:, at] = kr_ref[...].T
        values_t[:, at] = vr_ref[...].T
        dk_sum[...] = jnp.zeros_like(dk_sum)
        dv_sum[...] = jnp.zeros_like(dv_sum)
        tops[...] = jnp.full_like(tops, LOWEST)
        sums[...] = jnp.zeros_like(sums)
        for ref in (*weights, sgrads):
            ref[prompt_rows + half :, :half] = jnp.zeros((half, half), BF16)

    def blocks(piece):
        at, size, row = pieces[piece]
        for u in range(0, size, SUB):
            for r in range(0, rows - row, SUB):
                yield u, r, slice(at + u, at + u + SUB), slice(row + r, row + r + SUB)

    def stat(block_at):
        return slice(block_at.start // SUB * 8, block_at.start // SUB * 8 + 8)

    def tiled(block):
        return block.reshape(SUB // 8, 8, SUB)

    def score_products(now, piece):
        at, size, row = pieces[piece]

        def product(r):
            scores[piece % 2][:size, r - row : r - row + WIDE] = dot(
                keys[at : at + size, :], query_t[now, :, r : r + WIDE]
            )

        return [functools.partial(product, r) for r in range(row, rows, WIDE)]

    def dprob_products(before, piece):
        at, size, row = pieces[piece]

        def product(r):
            dprobs[piece % 2][:size, r - row : r - row + WIDE] = dot(
                values[at : at + size, :], grad_t[before, :, r : r + WIDE]
            )

        return [functools.partial(product, r) for r in range(row, rows, WIDE)]

    def score_chains(now, piece):
        def chain(u, r, key_at, row_at):
            block = scores[piece % 2][u : u + SUB, r : r + SUB]
            if key_at.start >= prompt_rows:
                j = lax.broadcasted_iota(jnp.int32, (SUB, SUB), 0) + key_at.start - prompt_rows
                i = lax.broadcasted_iota(jnp.int32, (SUB, SUB), 1) + row_at.start
                block = jnp.where((j <= i) & (j < length), block, -jnp.inf)
            block = tiled(block) * factor2
            top = jnp.maximum(jnp.max(block, axis=0), LOWEST)
            exp = jnp.exp2(block - top[None])
            exps[now][key_at, row_at] = exp.reshape(SUB, SUB)
            tops[stat(key_at), row_at] = top
            sums[stat(key_at), row_at] = jnp.sum(exp, axis=0)

        return [functools.partial(chain, *block) for block in blocks(piece)]

    def frac(slot, key_at, row_at):
        return tiled(exps[slot][key_at, row_at]) * fracs[slot, stat(key_at), row_at][None]

    def grad_chains(before, piece):
        def chain(u, r, key_at, row_at):
            dprob = tiled(dprobs[piece % 2][u : u + SUB, r : r + SUB])
            sgrad = frac(before, key_at, row_at) * (dprob - deltas[before, :, row_at][None])
            sgrads[key_at, row_at] = sgrad.reshape(SUB, SUB).astype(BF16)

        return [functools.partial(chain, *block) for block in blocks(piece)]

    def weight_chains(now, piece):
        def chain(u, r, key_at, row_at):
            weight = frac(now, key_at, row_at).reshape(SUB, SUB)
            weights[now][key_at, row_at] = weight.astype(BF16)

        return [functools.partial(chain, *block) for block in blocks(piece)]

    def grad_products(before, piece):
        at, size, row = pieces[piece]

        def value_product(u):
            at = slice(u, u + WIDE)
            dv_sum[at, :] += dot(weights[before][at, row:], grad[before, row:, :])

        def key_product(u):
            at = slice(u, u + WIDE)
            dk_sum[at, :] += dot(sgrads[at, row:], query[before, row:, :])

        return [
            functools.partial(product, u)
            for u in range(at, at + size, WIDE)
            for product in (value_product, key_product)
        ]

    def query_products():
        def product(r):
            dquery = dot(keys_t[...], sgrads[:, r : r + WIDE])
            dq_ref[:, r : r + WIDE] = (factor * dquery).astype(BF16)

        return [functools.partial(product, r) for r in range(0, rows, WIDE)]

    def out_products(now, piece):
        at, size, row = pieces[piece]

        def product(r):
            term = dot(values_t[:, at : at + size], weights[now][at : at + size, r : r + WIDE])
            if piece:
                term += mixture[:, r : r + WIDE]
            mixture[:, r : r + WIDE] = term

        return [functools.partial(product, r) for r in range(row, rows, WIDE)]

    def weave(products, chains):
        count = max(len(products), len(chains))
        for i in range(count):
            for jobs in (products, chains):
                for job in jobs[i * len(jobs) // count : (i + 1) * len(jobs) // count]:
                    job()

    def run(now, with_score, with_grad):
        before = 1 - now
        for stage in range(-1, count):
            products, chains = [], []
            if stage + 1 < count:
                if with_score:
                    products += score_products(now, stage + 1)
                if with_grad:
                    products += dprob_products(before, stage + 1)
            if stage >= 1 and with_grad:
                products += grad_products(before, stage - 1)
            if stage >= 0:
                both = [score_chains(now, stage)] if with_score else []
                both += [grad_chains(before, stage)] if with_grad else []
                chains = [chain for pair in zip(*both) for chain in pair]
            weave(products, chains)
        products = []
        if with_grad:
            products += grad_products(before, count - 1) + query_products()
        chains = []
        if with_score:
            set_fracs(now)
            chains = weight_chains(now, 0)
        weave(products, chains)
        if with_score:
            for piece in range(count):
                weave(
                    out_products(now, piece),
                    weight_chains(now, piece + 1) if piece + 1 < count else [],
                )
            finish(now)

    def prepare(now):
        live_rows = lax.broadcasted_iota(jnp.int32, (rows, HD), 0) < length
        live_lanes = lax.broadcasted_iota(jnp.int32, (HD, rows), 1) < length
        grad[now] = jnp.where(live_rows, g_ref[...].astype(F32), 0.0).astype(BF16)
        grad_t[now] = jnp.where(live_lanes, gt_ref[...].astype(F32), 0.0).astype(BF16)
        query[now] = q_ref[...]
        query_t[now] = qt_ref[...]

    def set_fracs(now):
        top = jnp.max(tops[...], axis=0, keepdims=True)
        scale = jnp.exp2(tops[...] - top)
        total = jnp.sum(scale * sums[...], axis=0, keepdims=True)
        fracs[now] = scale * (1.0 / total)

    def finish(now):
        live_lanes = lax.broadcasted_iota(jnp.int32, (HD, rows), 1) < length
        attended = jnp.where(live_lanes, mixture[...], 0.0).astype(BF16)
        out_ref[...] = attended
        delta = grad_t[now].astype(F32) * attended.astype(F32)
        delta = jnp.sum(delta, axis=0, keepdims=True)
        deltas[now] = jnp.broadcast_to(delta, (8, rows))

    @pl.when(step == 0)
    def _():
        prepare(0)
        run(0, True, False)

    for now in range(2):
        @pl.when((step > 0) & (step < heads_per) & (lax.rem(step, 2) == now))
        def _():
            prepare(now)
            run(now, True, True)

    @pl.when(step == heads_per)
    def _():
        run(heads_per % 2, False, True)
        layout.store(dcaches, dk_sum, dv_sum, factor)
        at = pl.ds(prompt_rows, rows)
        dkr_ref[...] = (factor * dk_sum[at, :]).astype(BF16)
        dvr_ref[...] = dv_sum[at, :].astype(BF16)


class Gathered:
    def __init__(self, members, ranks, own_rows):
        self.members, self.part_rows = members, ranks * own_rows
        self.prompt_rows = members * self.part_rows
        self.caches = 1
        self.dcaches = members

    def cache_shapes(self):
        return [(self.members, 2, self.part_rows, HD)]

    def dcache_shapes(self):
        return [(2, self.part_rows, HD)] * self.dcaches

    def load(self, caches):
        for m in range(self.members):
            at = pl.ds(m * self.part_rows, self.part_rows)
            yield at, caches[0][m, 0], caches[0][m, 1]

    def store(self, dcaches, dk_sum, dv_sum, factor):
        me = lax.axis_index("resp")
        for shift in range(self.members):
            part = lax.rem(me + shift, self.members) * self.part_rows
            at = pl.ds(pl.multiple_of(part, self.part_rows), self.part_rows)
            dcaches[shift][0] = (factor * dk_sum[at, :]).astype(BF16)
            dcaches[shift][1] = dv_sum[at, :].astype(BF16)


class Scattered(Gathered):
    def __init__(self, members, ranks, own_rows):
        super().__init__(members, ranks, own_rows)
        self.caches, self.dcaches = self.dcaches, self.caches

    def cache_shapes(self):
        return [(2, self.part_rows, HD)] * self.caches

    def dcache_shapes(self):
        return [(self.members, 2, self.part_rows, HD)]

    def load(self, caches):
        for i, ref in enumerate(caches):
            yield pl.ds(i * self.part_rows, self.part_rows), ref[0], ref[1]

    def store(self, dcaches, dk_sum, dv_sum, factor):
        me = lax.axis_index("resp")
        for shift in range(self.members):
            part = lax.rem(me - shift + self.members, self.members)
            at = pl.ds(shift * self.part_rows, self.part_rows)
            dcaches[0][part, 0] = (factor * dk_sum[at, :]).astype(BF16)
            dcaches[0][part, 1] = dv_sum[at, :].astype(BF16)


def attend(
    layout, pair, heads_per, lengths, queries, out_grad, caches, resp_keys, resp_values, earlier
):
    rows, query_width = queries[0].shape
    total_rows = layout.prompt_rows + rows
    first, last = pair * heads_per, (pair + 1) * heads_per - 1
    head_block = pl.BlockSpec((rows, HD), lambda s: (0, jnp.minimum(first + s, last)))
    turned_block = pl.BlockSpec((HD, rows), lambda s: (jnp.minimum(first + s, last), 0))
    late_block = pl.BlockSpec((HD, rows), lambda s: (jnp.maximum(first + s - 1, first), 0))
    pair_block = pl.BlockSpec((rows, HD), lambda s: (0, pair))
    cache_blocks = [
        pl.BlockSpec(shape, lambda s, rank=len(shape): (0,) * rank)
        for shape in layout.cache_shapes()
    ]
    dcache_blocks = [
        pl.BlockSpec(shape, lambda s, rank=len(shape): (0,) * rank)
        for shape in layout.dcache_shapes()
    ]
    stats = total_rows // SUB * 8
    in_specs = [
        pl.BlockSpec(memory_space=pltpu.SMEM),
        head_block,
        turned_block,
        head_block,
        turned_block,
        pair_block,
        pair_block,
        *cache_blocks,
    ] + [pl.BlockSpec(memory_space=pl.ANY)] * len(earlier)
    aliases = {7 + layout.caches + i: i for i in range(len(earlier))}
    return pl.pallas_call(
        functools.partial(attention_kernel, layout, heads_per, len(earlier)),
        grid=(heads_per + 1,),
        in_specs=in_specs,
        out_specs=[turned_block, late_block, pair_block, pair_block, *dcache_blocks],
        out_shape=[
            jax.ShapeDtypeStruct((query_width, rows), BF16),
            jax.ShapeDtypeStruct((query_width, rows), BF16),
            jax.ShapeDtypeStruct(resp_keys.shape, BF16),
            jax.ShapeDtypeStruct(resp_keys.shape, BF16),
            *[jax.ShapeDtypeStruct(shape, BF16) for shape in layout.dcache_shapes()],
        ],
        scratch_shapes=[
            pltpu.VMEM((total_rows, HD), BF16),
            pltpu.VMEM((total_rows, HD), BF16),
            pltpu.VMEM((HD, total_rows), BF16),
            pltpu.VMEM((HD, total_rows), BF16),
            pltpu.VMEM((2, rows, HD), BF16),
            pltpu.VMEM((2, HD, rows), BF16),
            pltpu.VMEM((2, rows, HD), BF16),
            pltpu.VMEM((2, HD, rows), BF16),
            pltpu.VMEM((total_rows, rows), F32),
            pltpu.VMEM((total_rows, rows), F32),
            pltpu.VMEM((total_rows, rows), BF16),
            pltpu.VMEM((total_rows, rows), BF16),
            pltpu.VMEM((total_rows, rows), BF16),
            pltpu.VMEM((rows, rows), F32),
            pltpu.VMEM((rows, rows), F32),
            pltpu.VMEM((rows, rows), F32),
            pltpu.VMEM((rows, rows), F32),
            pltpu.VMEM((2, stats, rows), F32),
            pltpu.VMEM((2, 8, rows), F32),
            pltpu.VMEM((total_rows, HD), F32),
            pltpu.VMEM((total_rows, HD), F32),
            pltpu.VMEM((stats, rows), F32),
            pltpu.VMEM((stats, rows), F32),
            pltpu.VMEM((HD, rows), F32),
        ],
        input_output_aliases=aliases,
        cost_estimate=pl.CostEstimate(
            flops=12 * heads_per * rows * total_rows * HD,
            bytes_accessed=8 * heads_per * rows * HD,
            transcendentals=heads_per * rows * total_rows,
        ),
        compiler_params=pltpu.CompilerParams(vmem_limit_bytes=60 * 1024 * 1024),
        name=f"attend_pair_{pair}",
    )(lengths, *queries, *out_grad, resp_keys, resp_values, *caches, *earlier)


def whole_block(shape):
    return pl.BlockSpec(shape, lambda: (0,) * len(shape))


def cut_kernel(pairs, k_ref, v_ref, *outs):
    me = lax.axis_index("tensor")
    ranks = len(outs) // pairs
    for p in range(pairs):
        for i in range(ranks):
            columns = pl.ds(pl.multiple_of(((me ^ i) * pairs + p) * HD, HD), HD)
            outs[p * ranks + i][0] = k_ref[:, columns]
            outs[p * ranks + i][1] = v_ref[:, columns]


def cut(prompt_keys, prompt_values, pairs):
    rows, columns = prompt_keys.shape
    count = columns // HD
    blocks = pl.pallas_call(
        functools.partial(cut_kernel, pairs),
        in_specs=[whole_block((rows, columns))] * 2,
        out_specs=[whole_block((2, rows, HD))] * count,
        out_shape=[jax.ShapeDtypeStruct((2, rows, HD), BF16)] * count,
        name="cut",
    )(prompt_keys, prompt_values)
    return [blocks[p * count // pairs : (p + 1) * count // pairs] for p in range(pairs)]


def place_kernel(pairs, *refs):
    *ins, dk_ref, dv_ref = refs
    me = lax.axis_index("tensor")
    ranks = len(ins) // pairs
    for p in range(pairs):
        for i in range(ranks):
            columns = pl.ds(pl.multiple_of(((me ^ i) * pairs + p) * HD, HD), HD)
            dk_ref[:, columns] = ins[p * ranks + i][0].astype(F32)
            dv_ref[:, columns] = ins[p * ranks + i][1].astype(F32)


def place(blocks, pairs, columns):
    _, rows, _ = blocks[0].shape
    shape = (rows, columns)
    return pl.pallas_call(
        functools.partial(place_kernel, pairs),
        in_specs=[whole_block(blocks[0].shape)] * len(blocks),
        out_specs=[whole_block(shape)] * 2,
        out_shape=[jax.ShapeDtypeStruct(shape, F32)] * 2,
        name="place",
    )(*blocks)


def swap(blocks):
    count = len(blocks)
    return [blocks[0]] + [
        lax.ppermute(blocks[i], "tensor", [(j, j ^ i) for j in range(count)])
        for i in range(1, count)
    ]


def send(block, members, shift):
    return lax.ppermute(block, "resp", [(m, (m + shift) % members) for m in range(members)])


def cut_rows(block, count):
    rows = block.shape[1] // count
    return [block[:, i * rows : (i + 1) * rows] for i in range(count)]


def per_device(
    members, ranks, queries, resp_keys, resp_values, prompt_keys, prompt_values, out_grad, lengths
):
    query_width = queries.shape[2]
    pair_width = resp_keys.shape[2]
    pairs = pair_width // HD
    heads_per = query_width // pair_width
    own_rows, columns = prompt_keys.shape
    queries, out_grad, resp_keys, resp_values = (
        a[0] for a in (queries, out_grad, resp_keys, resp_values)
    )
    cuts = cut(prompt_keys, prompt_values, pairs)
    queries, out_grad = (queries, queries.T), (out_grad, out_grad.T)
    kinds = [Scattered(members, ranks, own_rows)]
    kinds += [Gathered(members, ranks, own_rows) for _ in range(pairs - 1)]
    own = jnp.concatenate(swap(cuts[0]), axis=1)
    if pairs > 1:
        own, cuts[1:] = lax.optimization_barrier((own, cuts[1:]))
    caches = [[own] + [send(own, members, shift) for shift in range(1, members)]]
    for p in range(1, pairs):
        own = jnp.concatenate(swap(cuts[p]), axis=1)
        own, caches[0] = lax.optimization_barrier((own, caches[0]))
        caches.append([lax.all_gather(own, "resp", axis=0)])
    earlier = ()
    totals = []
    for p in range(pairs):
        results = attend(
            kinds[p],
            p,
            heads_per,
            lengths,
            queries,
            out_grad,
            caches[p],
            resp_keys,
            resp_values,
            earlier,
        )
        earlier, dcaches = results[:4], results[4:]
        if totals:
            dcaches, totals[-1] = lax.optimization_barrier((dcaches, totals[-1]))
        if isinstance(kinds[p], Scattered):
            totals.append(lax.psum_scatter(dcaches[0], "resp", scatter_dimension=0))
        else:
            totals.append(
                [dcaches[0]]
                + [send(dcaches[shift], members, shift) for shift in range(1, members)]
            )
    attended, query_grad = earlier[0].T, earlier[1].T
    if isinstance(totals[-1], list):
        attended, query_grad, arrived = lax.optimization_barrier(
            (attended, query_grad, totals[-1])
        )
        totals[-1] = sum(block.astype(F32) for block in arrived).astype(BF16)
    blocks = [block for total in totals for block in swap(cut_rows(total, ranks))]
    key_grad, value_grad = place(blocks, pairs, columns)
    outs = (a[None] for a in (attended, query_grad, *earlier[2:]))
    return (*outs, key_grad, value_grad)


def solution(mesh):
    rows = P(("group", "resp"), None, "tensor")
    prompt = P(("group", "resp", "tensor"), None)
    return jax.shard_map(
        functools.partial(per_device, mesh.shape["resp"], mesh.shape["tensor"]),
        mesh=mesh,
        in_specs=(rows, rows, rows, prompt, prompt, rows, P(("group", "resp"))),
        out_specs=(rows, rows, rows, rows, prompt, prompt),
        check_vma=False,
    )
```

```python
import functools
import math

import jax
import jax.numpy as jnp
from jax import lax
from jax.experimental import pallas as pl
from jax.experimental.pallas import tpu as pltpu
from jax.sharding import PartitionSpec as P

HD = 128
SUB = 128
WIDE = 256
LOWEST = -1e30
BF16 = jnp.bfloat16
F32 = jnp.float32


def dot(a, b):
    return jnp.dot(a, b, preferred_element_type=F32)


def attention_kernel(
    layout,
    heads_per,
    earlier,
    len_ref,
    q_ref,
    g_ref,
    kr_ref,
    vr_ref,
    *rest,
):
    caches, rest = rest[: layout.caches], rest[layout.caches + earlier :]
    out_ref, dq_ref, dkr_ref, dvr_ref, *rest = rest
    dcaches, rest = rest[: layout.dcaches], rest[layout.dcaches :]
    (
        keys,
        values,
        keys_t,
        values_t,
        query,
        query_t,
        grad,
        grad_t,
        exps_even,
        exps_odd,
        weights_even,
        weights_odd,
        sgrads,
        score_even,
        score_odd,
        dprob_even,
        dprob_odd,
        fracs,
        deltas,
        dk_sum,
        dv_sum,
        tops,
        sums,
        mixture,
    ) = rest
    rows = q_ref.shape[0]
    prompt_rows = layout.prompt_rows
    total_rows = prompt_rows + rows
    half = rows // 2
    pieces = [(at, rows, 0) for at in range(0, prompt_rows, rows)]
    pieces += [(prompt_rows, half, 0), (prompt_rows + half, half, half)]
    count = len(pieces)
    factor = HD ** (-0.5)
    factor2 = factor * math.log2(math.e)
    length = len_ref[0]
    step = pl.program_id(0)
    exps = (exps_even, exps_odd)
    weights = (weights_even, weights_odd)
    scores = (score_even, score_odd)
    dprobs = (dprob_even, dprob_odd)

    @pl.when(step == 0)
    def _():
        layout.load(caches, keys, values)
        for at in range(0, prompt_rows, rows):
            at = pl.ds(at, rows)
            keys_t[:, at] = keys[at, :].T
            values_t[:, at] = values[at, :].T
        at = pl.ds(prompt_rows, rows)
        keys[at, :] = kr_ref[...]
        values[at, :] = vr_ref[...]
        keys_t[:, at] = kr_ref[...].T
        values_t[:, at] = vr_ref[...].T
        dk_sum[...] = jnp.zeros_like(dk_sum)
        dv_sum[...] = jnp.zeros_like(dv_sum)
        tops[...] = jnp.full_like(tops, LOWEST)
        sums[...] = jnp.zeros_like(sums)
        for ref in (*weights, sgrads):
            ref[prompt_rows + half :, :half] = jnp.zeros((half, half), BF16)

    def blocks(piece):
        at, size, row = pieces[piece]
        for u in range(0, size, SUB):
            for r in range(0, rows - row, SUB):
                yield u, r, slice(at + u, at + u + SUB), slice(row + r, row + r + SUB)

    def stat(block_at):
        return slice(block_at.start // SUB * 8, block_at.start // SUB * 8 + 8)

    def tiled(block):
        return block.reshape(SUB // 8, 8, SUB)

    def score_products(now, piece):
        at, size, row = pieces[piece]

        def product(r):
            scores[piece % 2][:size, r - row : r - row + WIDE] = dot(
                keys[at : at + size, :], query_t[now, :, r : r + WIDE]
            )

        return [functools.partial(product, r) for r in range(row, rows, WIDE)]

    def dprob_products(before, piece):
        at, size, row = pieces[piece]

        def product(r):
            dprobs[piece % 2][:size, r - row : r - row + WIDE] = dot(
                values[at : at + size, :], grad_t[before, :, r : r + WIDE]
            )

        return [functools.partial(product, r) for r in range(row, rows, WIDE)]

    def score_chains(now, piece):
        def chain(u, r, key_at, row_at):
            block = scores[piece % 2][u : u + SUB, r : r + SUB]
            if key_at.start >= prompt_rows:
                j = lax.broadcasted_iota(jnp.int32, (SUB, SUB), 0) + key_at.start - prompt_rows
                i = lax.broadcasted_iota(jnp.int32, (SUB, SUB), 1) + row_at.start
                block = jnp.where((j <= i) & (j < length), block, -jnp.inf)
            block = tiled(block) * factor2
            top = jnp.maximum(jnp.max(block, axis=0), LOWEST)
            exp = jnp.exp2(block - top[None])
            exps[now][key_at, row_at] = exp.reshape(SUB, SUB)
            tops[stat(key_at), row_at] = top
            sums[stat(key_at), row_at] = jnp.sum(exp, axis=0)

        return [functools.partial(chain, *block) for block in blocks(piece)]

    def frac(slot, key_at, row_at):
        return tiled(exps[slot][key_at, row_at]) * fracs[slot, stat(key_at), row_at][None]

    def grad_chains(before, piece):
        def chain(u, r, key_at, row_at):
            dprob = tiled(dprobs[piece % 2][u : u + SUB, r : r + SUB])
            sgrad = frac(before, key_at, row_at) * (dprob - deltas[before, :, row_at][None])
            sgrads[key_at, row_at] = sgrad.reshape(SUB, SUB).astype(BF16)

        return [functools.partial(chain, *block) for block in blocks(piece)]

    def weight_chains(now, piece):
        def chain(u, r, key_at, row_at):
            weight = frac(now, key_at, row_at).reshape(SUB, SUB)
            weights[now][key_at, row_at] = weight.astype(BF16)

        return [functools.partial(chain, *block) for block in blocks(piece)]

    def grad_products(before, piece):
        at, size, row = pieces[piece]

        def value_product(u):
            at = slice(u, u + WIDE)
            dv_sum[at, :] += dot(weights[before][at, row:], grad[before, row:, :])

        def key_product(u):
            at = slice(u, u + WIDE)
            dk_sum[at, :] += dot(sgrads[at, row:], query[before, row:, :])

        return [
            functools.partial(product, u)
            for u in range(at, at + size, WIDE)
            for product in (value_product, key_product)
        ]

    def query_products():
        def product(r):
            dquery = dot(keys_t[...], sgrads[:, r : r + WIDE])
            dq_ref[r : r + WIDE, :] = (factor * dquery).T.astype(BF16)

        return [functools.partial(product, r) for r in range(0, rows, WIDE)]

    def out_products(now, piece):
        at, size, row = pieces[piece]

        def product(r):
            term = dot(values_t[:, at : at + size], weights[now][at : at + size, r : r + WIDE])
            if piece:
                term += mixture[:, r : r + WIDE]
            mixture[:, r : r + WIDE] = term

        return [functools.partial(product, r) for r in range(row, rows, WIDE)]

    def weave(products, chains):
        count = max(len(products), len(chains))
        for i in range(count):
            for jobs in (products, chains):
                for job in jobs[i * len(jobs) // count : (i + 1) * len(jobs) // count]:
                    job()

    def run(now, with_score, with_grad):
        before = 1 - now
        for stage in range(-1, count):
            products, chains = [], []
            if stage + 1 < count:
                if with_score:
                    products += score_products(now, stage + 1)
                if with_grad:
                    products += dprob_products(before, stage + 1)
            if stage >= 1 and with_grad:
                products += grad_products(before, stage - 1)
            if stage >= 0:
                both = [score_chains(now, stage)] if with_score else []
                both += [grad_chains(before, stage)] if with_grad else []
                chains = [chain for pair in zip(*both) for chain in pair]
            weave(products, chains)
        products = []
        if with_grad:
            products += grad_products(before, count - 1) + query_products()
        chains = []
        if with_score:
            set_fracs(now)
            chains = weight_chains(now, 0)
        weave(products, chains)
        if with_score:
            for piece in range(count):
                weave(
                    out_products(now, piece),
                    weight_chains(now, piece + 1) if piece + 1 < count else [],
                )
            finish(now)

    def prepare(now):
        live_rows = lax.broadcasted_iota(jnp.int32, (rows, HD), 0) < length
        live_grad = jnp.where(live_rows, g_ref[...].astype(F32), 0.0)
        grad[now] = live_grad.astype(BF16)
        grad_t[now] = live_grad.T.astype(BF16)
        query[now] = q_ref[...]
        query_t[now] = q_ref[...].T

    def set_fracs(now):
        top = jnp.max(tops[...], axis=0, keepdims=True)
        scale = jnp.exp2(tops[...] - top)
        total = jnp.sum(scale * sums[...], axis=0, keepdims=True)
        fracs[now] = scale * (1.0 / total)

    def finish(now):
        live_lanes = lax.broadcasted_iota(jnp.int32, (HD, rows), 1) < length
        attended = jnp.where(live_lanes, mixture[...], 0.0).astype(BF16).astype(F32)
        out_ref[...] = attended.T.astype(BF16)
        delta = jnp.sum(grad_t[now].astype(F32) * attended, axis=0, keepdims=True)
        deltas[now] = jnp.broadcast_to(delta, (8, rows))

    @pl.when(step == 0)
    def _():
        prepare(0)
        run(0, True, False)

    for now in range(2):
        @pl.when((step > 0) & (step < heads_per) & (lax.rem(step, 2) == now))
        def _():
            prepare(now)
            run(now, True, True)

    @pl.when(step == heads_per)
    def _():
        run(heads_per % 2, False, True)
        layout.store(dcaches, dk_sum, dv_sum, factor)
        at = pl.ds(prompt_rows, rows)
        dkr_ref[...] = (factor * dk_sum[at, :]).astype(BF16)
        dvr_ref[...] = dv_sum[at, :].astype(BF16)


def fill(keys, values, at, ref):
    keys[at, :] = ref[0]
    values[at, :] = ref[1]


class Gathered:
    def __init__(self, members, part_rows):
        self.members, self.part_rows = members, part_rows
        self.prompt_rows = members * self.part_rows
        self.caches = 1
        self.dcaches = members + (members == 4)

    def cache_shapes(self):
        return [(self.members, 2, self.part_rows, HD)]

    def dcache_shapes(self):
        return [(2, self.part_rows, HD)] * self.dcaches

    def load(self, caches, keys, values):
        for m in range(self.members):
            fill(keys, values, pl.ds(m * self.part_rows, self.part_rows), caches[0].at[m])

    def store(self, dcaches, dk_sum, dv_sum, factor):
        me = lax.axis_index("resp")
        parts = [lax.rem(me + shift, self.members) for shift in range(self.members)]
        if self.members == 4:
            parts = [parts[0], parts[1], parts[3], parts[2], 3 - me]
        for part, ref in zip(parts, dcaches):
            at = pl.ds(pl.multiple_of(part * self.part_rows, self.part_rows), self.part_rows)
            ref[0] = (factor * dk_sum[at, :]).astype(BF16)
            ref[1] = dv_sum[at, :].astype(BF16)


class Scattered(Gathered):
    def __init__(self, members, part_rows):
        super().__init__(members, part_rows)
        self.caches, self.dcaches = self.dcaches, self.caches

    def cache_shapes(self):
        return [(2, self.part_rows, HD)] * self.caches

    def dcache_shapes(self):
        return [(self.members, 2, self.part_rows, HD)]

    def load(self, caches, keys, values):
        ats = [pl.ds(m * self.part_rows, self.part_rows) for m in range(self.members)]
        if self.members != 4:
            for at, ref in zip(ats, caches):
                fill(keys, values, at, ref)
            return
        own, left, right, two, far = caches
        me = lax.axis_index("resp")
        fill(keys, values, ats[0], own)
        fill(keys, values, ats[1], left)
        fill(keys, values, ats[2], two)
        fill(keys, values, ats[3], right)
        for end, at in ((0, ats[1]), (3, ats[3])):
            @pl.when(me == end)
            def _():
                fill(keys, values, at, far)

    def store(self, dcaches, dk_sum, dv_sum, factor):
        me = lax.axis_index("resp")
        for shift in range(self.members):
            part = lax.rem(me - shift + self.members, self.members)
            at = pl.ds(shift * self.part_rows, self.part_rows)
            dcaches[0][part, 0] = (factor * dk_sum[at, :]).astype(BF16)
            dcaches[0][part, 1] = dv_sum[at, :].astype(BF16)


def attend(
    layout, pair, heads_per, lengths, queries, out_grad, caches, resp_keys, resp_values, earlier
):
    rows, query_width = queries.shape
    total_rows = layout.prompt_rows + rows
    first, last = pair * heads_per, (pair + 1) * heads_per - 1
    head_block = pl.BlockSpec((rows, HD), lambda s: (0, jnp.minimum(first + s, last)))
    late_block = pl.BlockSpec((rows, HD), lambda s: (0, jnp.maximum(first + s - 1, first)))
    pair_block = pl.BlockSpec((rows, HD), lambda s: (0, pair))
    cache_blocks = [
        pl.BlockSpec(shape, lambda s, rank=len(shape): (0,) * rank)
        for shape in layout.cache_shapes()
    ]
    dcache_blocks = [
        pl.BlockSpec(shape, lambda s, rank=len(shape): (0,) * rank)
        for shape in layout.dcache_shapes()
    ]
    stats = total_rows // SUB * 8
    in_specs = [
        pl.BlockSpec(memory_space=pltpu.SMEM),
        head_block,
        head_block,
        pair_block,
        pair_block,
        *cache_blocks,
    ] + [pl.BlockSpec(memory_space=pl.ANY)] * len(earlier)
    aliases = {5 + layout.caches + i: i for i in range(len(earlier))}
    return pl.pallas_call(
        functools.partial(attention_kernel, layout, heads_per, len(earlier)),
        grid=(heads_per + 1,),
        in_specs=in_specs,
        out_specs=[head_block, late_block, pair_block, pair_block, *dcache_blocks],
        out_shape=[
            jax.ShapeDtypeStruct(queries.shape, BF16),
            jax.ShapeDtypeStruct(queries.shape, BF16),
            jax.ShapeDtypeStruct(resp_keys.shape, BF16),
            jax.ShapeDtypeStruct(resp_keys.shape, BF16),
            *[jax.ShapeDtypeStruct(shape, BF16) for shape in layout.dcache_shapes()],
        ],
        scratch_shapes=[
            pltpu.VMEM((total_rows, HD), BF16),
            pltpu.VMEM((total_rows, HD), BF16),
            pltpu.VMEM((HD, total_rows), BF16),
            pltpu.VMEM((HD, total_rows), BF16),
            pltpu.VMEM((2, rows, HD), BF16),
            pltpu.VMEM((2, HD, rows), BF16),
            pltpu.VMEM((2, rows, HD), BF16),
            pltpu.VMEM((2, HD, rows), BF16),
            pltpu.VMEM((total_rows, rows), F32),
            pltpu.VMEM((total_rows, rows), F32),
            pltpu.VMEM((total_rows, rows), BF16),
            pltpu.VMEM((total_rows, rows), BF16),
            pltpu.VMEM((total_rows, rows), BF16),
            pltpu.VMEM((rows, rows), F32),
            pltpu.VMEM((rows, rows), F32),
            pltpu.VMEM((rows, rows), F32),
            pltpu.VMEM((rows, rows), F32),
            pltpu.VMEM((2, stats, rows), F32),
            pltpu.VMEM((2, 8, rows), F32),
            pltpu.VMEM((total_rows, HD), F32),
            pltpu.VMEM((total_rows, HD), F32),
            pltpu.VMEM((stats, rows), F32),
            pltpu.VMEM((stats, rows), F32),
            pltpu.VMEM((HD, rows), F32),
        ],
        input_output_aliases=aliases,
        cost_estimate=pl.CostEstimate(
            flops=12 * heads_per * rows * total_rows * HD,
            bytes_accessed=8 * heads_per * rows * HD,
            transcendentals=heads_per * rows * total_rows,
        ),
        compiler_params=pltpu.CompilerParams(vmem_limit_bytes=60 * 1024 * 1024),
        name=f"attend_pair_{pair}",
    )(lengths, queries, out_grad, resp_keys, resp_values, *caches, *earlier)


def whole_block(shape):
    return pl.BlockSpec(shape, lambda: (0,) * len(shape))


def cut_kernel(pairs, k_ref, v_ref, *outs):
    me = lax.axis_index("tensor")
    ranks = len(outs) // pairs
    for p in range(pairs):
        for i in range(ranks):
            columns = pl.ds(pl.multiple_of(((me ^ i) * pairs + p) * HD, HD), HD)
            outs[p * ranks + i][0] = k_ref[:, columns]
            outs[p * ranks + i][1] = v_ref[:, columns]


def cut(prompt_keys, prompt_values, pairs):
    rows, columns = prompt_keys.shape
    count = columns // HD
    blocks = pl.pallas_call(
        functools.partial(cut_kernel, pairs),
        in_specs=[whole_block((rows, columns))] * 2,
        out_specs=[whole_block((2, rows, HD))] * count,
        out_shape=[jax.ShapeDtypeStruct((2, rows, HD), BF16)] * count,
        name="cut",
    )(prompt_keys, prompt_values)
    return [blocks[p * count // pairs : (p + 1) * count // pairs] for p in range(pairs)]


def place_kernel(pairs, *refs):
    *ins, dk_ref, dv_ref = refs
    me = lax.axis_index("tensor")
    ranks = len(ins) // pairs
    for p in range(pairs):
        for i in range(ranks):
            columns = pl.ds(pl.multiple_of(((me ^ i) * pairs + p) * HD, HD), HD)
            dk_ref[:, columns] = ins[p * ranks + i][0].astype(F32)
            dv_ref[:, columns] = ins[p * ranks + i][1].astype(F32)


def place(blocks, pairs, columns):
    _, rows, _ = blocks[0].shape
    shape = (rows, columns)
    return pl.pallas_call(
        functools.partial(place_kernel, pairs),
        in_specs=[whole_block(blocks[0].shape)] * len(blocks),
        out_specs=[whole_block(shape)] * 2,
        out_shape=[jax.ShapeDtypeStruct(shape, F32)] * 2,
        name="place",
    )(*blocks)


def swap(blocks):
    count = len(blocks)
    return [blocks[0]] + [
        lax.ppermute(blocks[i], "tensor", [(j, j ^ i) for j in range(count)])
        for i in range(1, count)
    ]


def shift_all(block, members, shift):
    return lax.ppermute(block, "resp", [(m, (m + shift) % members) for m in range(members)])


RIGHT, LEFT = [(0, 1), (1, 2), (2, 3)], [(1, 0), (2, 1), (3, 2)]


def spread(own, members):
    if members != 4:
        return [own] + [shift_all(own, members, shift) for shift in range(1, members)]
    two = shift_all(own, members, 2)
    right, left = lax.ppermute(own, "resp", RIGHT), lax.ppermute(own, "resp", LEFT)
    far = lax.ppermute(two, "resp", [(2, 3), (1, 0)])
    return [own, right, left, two, far]


def collect(parts, members):
    if members != 4:
        return [parts[0]] + [shift_all(parts[s], members, s) for s in range(1, members)]
    own, right, left, two, far = parts
    far = lax.ppermute(far, "resp", [(3, 2), (0, 1)])
    right, left = lax.ppermute(right, "resp", RIGHT), lax.ppermute(left, "resp", LEFT)
    two = (two.astype(F32) + far.astype(F32)).astype(BF16)
    return [own, right, left, shift_all(two, members, 2)]


def cut_rows(block, count):
    rows = block.shape[1] // count
    return [block[:, i * rows : (i + 1) * rows] for i in range(count)]


def per_device(
    members, ranks, queries, resp_keys, resp_values, prompt_keys, prompt_values, out_grad, lengths
):
    query_width = queries.shape[2]
    pair_width = resp_keys.shape[2]
    pairs = pair_width // HD
    heads_per = query_width // pair_width
    own_rows, columns = prompt_keys.shape
    queries, out_grad, resp_keys, resp_values = (
        a[0] for a in (queries, out_grad, resp_keys, resp_values)
    )
    cuts = cut(prompt_keys, prompt_values, pairs)
    kinds = [Scattered(members, ranks * own_rows)]
    kinds += [Gathered(members, ranks * own_rows) for _ in range(pairs - 1)]
    own = jnp.concatenate(swap(cuts[0]), axis=1)
    if pairs > 1:
        own, cuts[1:] = lax.optimization_barrier((own, cuts[1:]))
    caches = [spread(own, members)]
    for p in range(1, pairs):
        own = jnp.concatenate(swap(cuts[p]), axis=1)
        own, caches[0] = lax.optimization_barrier((own, caches[0]))
        caches.append([lax.all_gather(own, "resp", axis=0)])
    earlier = ()
    totals = []
    for p in range(pairs):
        results = attend(
            kinds[p],
            p,
            heads_per,
            lengths,
            queries,
            out_grad,
            caches[p],
            resp_keys,
            resp_values,
            earlier,
        )
        earlier, dcaches = results[:4], results[4:]
        if totals:
            dcaches, totals[-1] = lax.optimization_barrier((dcaches, totals[-1]))
        if isinstance(kinds[p], Scattered):
            totals.append(lax.psum_scatter(dcaches[0], "resp", scatter_dimension=0))
        else:
            arrived = collect(dcaches, members)
            totals.append(sum(block.astype(F32) for block in arrived).astype(BF16))
    blocks = [block for total in totals for block in swap(cut_rows(total, ranks))]
    key_grad, value_grad = place(blocks, pairs, columns)
    return (*(a[None] for a in earlier), key_grad, value_grad)


def solution(mesh):
    rows = P(("group", "resp"), None, "tensor")
    prompt = P(("group", "resp", "tensor"), None)
    return jax.shard_map(
        functools.partial(per_device, mesh.shape["resp"], mesh.shape["tensor"]),
        mesh=mesh,
        in_specs=(rows, rows, rows, prompt, prompt, rows, P(("group", "resp"))),
        out_specs=(rows, rows, rows, rows, prompt, prompt),
        check_vma=False,
    )
```

```python
import functools
import math

import jax
import jax.numpy as jnp
from jax import lax
from jax.experimental import pallas as pl
from jax.experimental.pallas import tpu as pltpu
from jax.sharding import PartitionSpec as P

HD = 128
SUB = 128
WIDE = 256
LOWEST = -1e30
BF16 = jnp.bfloat16
F32 = jnp.float32


def dot_last(a, b):
    return lax.dot_general(a, b, (((1,), (1,)), ((), ())), preferred_element_type=F32)


def dot(a, b):
    return jnp.dot(a, b, preferred_element_type=F32)


def attention_kernel(
    layout,
    heads_per,
    earlier,
    len_ref,
    q_ref,
    g_ref,
    kr_ref,
    vr_ref,
    *rest,
):
    caches, rest = rest[: layout.caches], rest[layout.caches + earlier :]
    out_ref, dq_ref, dkr_ref, dvr_ref, *rest = rest
    dcaches, rest = rest[: layout.dcaches], rest[layout.dcaches :]
    (
        keys,
        values,
        keys_t,
        values_t,
        query,
        query_t,
        grad,
        grad_t,
        exps_even,
        exps_odd,
        weights_even,
        weights_odd,
        sgrads,
        score_even,
        score_odd,
        dprob_even,
        dprob_odd,
        fracs,
        deltas,
        dk_sum,
        dv_sum,
        tops,
        sums,
        mixture,
    ) = rest
    rows = q_ref.shape[0]
    prompt_rows = layout.prompt_rows
    total_rows = prompt_rows + rows
    half = rows // 2
    pieces = [(at, rows, 0) for at in range(0, prompt_rows, rows)]
    pieces += [(prompt_rows, half, 0), (prompt_rows + half, half, half)]
    count = len(pieces)
    factor = HD ** (-0.5)
    factor2 = factor * math.log2(math.e)
    length = len_ref[0]
    step = pl.program_id(0)
    exps = (exps_even, exps_odd)
    weights = (weights_even, weights_odd)
    scores = (score_even, score_odd)
    dprobs = (dprob_even, dprob_odd)

    @pl.when(step == 0)
    def _():
        for at, key_block, value_block in layout.load(caches):
            keys[at, :] = key_block
            values[at, :] = value_block
        for at in range(0, prompt_rows, rows):
            at = pl.ds(at, rows)
            keys_t[:, at] = keys[at, :].T
            values_t[:, at] = values[at, :].T
        at = pl.ds(prompt_rows, rows)
        keys[at, :] = kr_ref[...]
        values[at, :] = vr_ref[...]
        keys_t[:, at] = kr_ref[...].T
        values_t[:, at] = vr_ref[...].T
        dk_sum[...] = jnp.zeros_like(dk_sum)
        dv_sum[...] = jnp.zeros_like(dv_sum)
        tops[...] = jnp.full_like(tops, LOWEST)
        sums[...] = jnp.zeros_like(sums)
        for ref in (*weights, sgrads):
            ref[prompt_rows + half :, :half] = jnp.zeros((half, half), BF16)

    def blocks(piece):
        at, size, row = pieces[piece]
        for u in range(0, size, SUB):
            for r in range(0, rows - row, SUB):
                yield u, r, slice(at + u, at + u + SUB), slice(row + r, row + r + SUB)

    def stat(block_at):
        return slice(block_at.start // SUB * 8, block_at.start // SUB * 8 + 8)

    def tiled(block):
        return block.reshape(SUB // 8, 8, SUB)

    def score_products(now, piece):
        at, size, row = pieces[piece]

        def product(r):
            scores[piece % 2][:size, r - row : r - row + WIDE] = dot(
                keys[at : at + size, :], query_t[now, :, r : r + WIDE]
            )

        return [functools.partial(product, r) for r in range(row, rows, WIDE)]

    def dprob_products(before, piece):
        at, size, row = pieces[piece]

        def product(r):
            dprobs[piece % 2][:size, r - row : r - row + WIDE] = dot(
                values[at : at + size, :], grad_t[before, :, r : r + WIDE]
            )

        return [functools.partial(product, r) for r in range(row, rows, WIDE)]

    def score_chains(now, piece):
        def chain(u, r, key_at, row_at):
            block = scores[piece % 2][u : u + SUB, r : r + SUB]
            if key_at.start >= prompt_rows:
                j = lax.broadcasted_iota(jnp.int32, (SUB, SUB), 0) + key_at.start - prompt_rows
                i = lax.broadcasted_iota(jnp.int32, (SUB, SUB), 1) + row_at.start
                block = jnp.where((j <= i) & (j < length), block, -jnp.inf)
            block = tiled(block) * factor2
            top = jnp.maximum(jnp.max(block, axis=0), LOWEST)
            exp = jnp.exp2(block - top[None])
            exps[now][key_at, row_at] = exp.reshape(SUB, SUB)
            tops[stat(key_at), row_at] = top
            sums[stat(key_at), row_at] = jnp.sum(exp, axis=0)

        return [functools.partial(chain, *block) for block in blocks(piece)]

    def frac(slot, key_at, row_at):
        return tiled(exps[slot][key_at, row_at]) * fracs[slot, stat(key_at), row_at][None]

    def grad_chains(before, piece):
        def chain(u, r, key_at, row_at):
            dprob = tiled(dprobs[piece % 2][u : u + SUB, r : r + SUB])
            sgrad = frac(before, key_at, row_at) * (dprob - deltas[before, :, row_at][None])
            sgrads[key_at, row_at] = sgrad.reshape(SUB, SUB).astype(BF16)

        return [functools.partial(chain, *block) for block in blocks(piece)]

    def weight_chains(now, piece):
        def chain(u, r, key_at, row_at):
            weight = frac(now, key_at, row_at).reshape(SUB, SUB)
            weights[now][key_at, row_at] = weight.astype(BF16)

        return [functools.partial(chain, *block) for block in blocks(piece)]

    def grad_products(before, piece):
        at, size, row = pieces[piece]

        key_at = slice(at, at + size)

        def value_product():
            dv_sum[:, key_at] += dot_last(grad_t[before, :, row:], weights[before][key_at, row:])

        def key_product():
            dk_sum[:, key_at] += dot_last(query_t[before, :, row:], sgrads[key_at, row:])

        return [value_product, key_product]

    def query_products():
        def product(r):
            dquery = dot(keys_t[...], sgrads[:, r : r + WIDE])
            dq_ref[r : r + WIDE, :] = (factor * dquery).T.astype(BF16)

        return [functools.partial(product, r) for r in range(0, rows, WIDE)]

    def out_products(now, piece):
        at, size, row = pieces[piece]

        def product(r):
            term = dot(values_t[:, at : at + size], weights[now][at : at + size, r : r + WIDE])
            if piece:
                term += mixture[:, r : r + WIDE]
            mixture[:, r : r + WIDE] = term

        return [functools.partial(product, r) for r in range(row, rows, WIDE)]

    def weave(products, chains):
        count = max(len(products), len(chains))
        for i in range(count):
            for jobs in (products, chains):
                for job in jobs[i * len(jobs) // count : (i + 1) * len(jobs) // count]:
                    job()

    def run(now, with_score, with_grad):
        before = 1 - now
        for stage in range(-1, count):
            products, chains = [], []
            if stage + 1 < count:
                if with_score:
                    products += score_products(now, stage + 1)
                if with_grad:
                    products += dprob_products(before, stage + 1)
            if stage >= 1 and with_grad:
                products += grad_products(before, stage - 1)
            if stage >= 0:
                both = [score_chains(now, stage)] if with_score else []
                both += [grad_chains(before, stage)] if with_grad else []
                chains = [chain for pair in zip(*both) for chain in pair]
            weave(products, chains)
        products = []
        if with_grad:
            products += grad_products(before, count - 1) + query_products()
        chains = []
        if with_score:
            set_fracs(now)
            chains = weight_chains(now, 0)
        weave(products, chains)
        if with_score:
            for piece in range(count):
                weave(
                    out_products(now, piece),
                    weight_chains(now, piece + 1) if piece + 1 < count else [],
                )
            finish(now)

    def prepare(now):
        live_rows = lax.broadcasted_iota(jnp.int32, (rows, HD), 0) < length
        live_grad = jnp.where(live_rows, g_ref[...].astype(F32), 0.0)
        grad[now] = live_grad.astype(BF16)
        grad_t[now] = live_grad.T.astype(BF16)
        query[now] = q_ref[...]
        query_t[now] = q_ref[...].T

    def set_fracs(now):
        top = jnp.max(tops[...], axis=0, keepdims=True)
        scale = jnp.exp2(tops[...] - top)
        total = jnp.sum(scale * sums[...], axis=0, keepdims=True)
        fracs[now] = scale * (1.0 / total)

    def finish(now):
        live_lanes = lax.broadcasted_iota(jnp.int32, (HD, rows), 1) < length
        attended = jnp.where(live_lanes, mixture[...], 0.0).astype(BF16).astype(F32)
        out_ref[...] = attended.T.astype(BF16)
        delta = jnp.sum(grad_t[now].astype(F32) * attended, axis=0, keepdims=True)
        deltas[now] = jnp.broadcast_to(delta, (8, rows))

    @pl.when(step == 0)
    def _():
        prepare(0)
        run(0, True, False)

    for now in range(2):
        @pl.when((step > 0) & (step < heads_per) & (lax.rem(step, 2) == now))
        def _():
            prepare(now)
            run(now, True, True)

    @pl.when(step == heads_per)
    def _():
        run(heads_per % 2, False, True)
        layout.store(dcaches, dk_sum, dv_sum, factor)
        at = pl.ds(prompt_rows, rows)
        dkr_ref[...] = (factor * dk_sum[:, at]).T.astype(BF16)
        dvr_ref[...] = dv_sum[:, at].T.astype(BF16)


class Gathered:
    def __init__(self, members, part_rows):
        self.members, self.part_rows = members, part_rows
        self.prompt_rows = members * part_rows
        self.caches, self.dcaches = 1, members + 1

    def cache_shapes(self):
        return [(self.members, 2, self.part_rows, HD)]

    def dcache_shapes(self):
        part = (self.part_rows, HD)
        return [part] * self.members + [(self.members, *part)]

    def load(self, caches):
        for m in range(self.members):
            at = pl.ds(m * self.part_rows, self.part_rows)
            yield at, caches[0][m, 0], caches[0][m, 1]

    def store(self, dcaches, dk_sum, dv_sum, factor):
        me = lax.axis_index("resp")
        for shift in range(self.members):
            part = lax.rem(me + shift, self.members) * self.part_rows
            at = pl.ds(pl.multiple_of(part, self.part_rows), self.part_rows)
            dcaches[shift][...] = (factor * dk_sum[:, at]).T.astype(BF16)
            at = pl.ds(shift * self.part_rows, self.part_rows)
            dcaches[self.members][shift] = dv_sum[:, at].T.astype(BF16)


class Scattered(Gathered):
    def __init__(self, members, part_rows):
        super().__init__(members, part_rows)
        self.caches, self.dcaches = self.dcaches, self.caches

    def cache_shapes(self):
        return super().dcache_shapes()

    def dcache_shapes(self):
        return super().cache_shapes()

    def part(self, shift):
        return lax.rem(lax.axis_index("resp") - shift + self.members, self.members)

    def load(self, caches):
        for shift in range(self.members):
            at = pl.ds(shift * self.part_rows, self.part_rows)
            yield at, caches[shift][...], caches[self.members][self.part(shift)]

    def store(self, dcaches, dk_sum, dv_sum, factor):
        for shift in range(self.members):
            at = pl.ds(shift * self.part_rows, self.part_rows)
            dcaches[0][self.part(shift), 0] = (factor * dk_sum[:, at]).T.astype(BF16)
            dcaches[0][self.part(shift), 1] = dv_sum[:, at].T.astype(BF16)


def attend(
    layout, pair, heads_per, lengths, queries, out_grad, caches, resp_keys, resp_values, earlier
):
    rows, query_width = queries.shape
    total_rows = layout.prompt_rows + rows
    first, last = pair * heads_per, (pair + 1) * heads_per - 1
    head_block = pl.BlockSpec((rows, HD), lambda s: (0, jnp.minimum(first + s, last)))
    late_block = pl.BlockSpec((rows, HD), lambda s: (0, jnp.maximum(first + s - 1, first)))
    pair_block = pl.BlockSpec((rows, HD), lambda s: (0, pair))
    cache_blocks = [
        pl.BlockSpec(shape, lambda s, rank=len(shape): (0,) * rank)
        for shape in layout.cache_shapes()
    ]
    dcache_blocks = [
        pl.BlockSpec(shape, lambda s, rank=len(shape): (0,) * rank)
        for shape in layout.dcache_shapes()
    ]
    stats = total_rows // SUB * 8
    in_specs = [
        pl.BlockSpec(memory_space=pltpu.SMEM),
        head_block,
        head_block,
        pair_block,
        pair_block,
        *cache_blocks,
    ] + [pl.BlockSpec(memory_space=pl.ANY)] * len(earlier)
    aliases = {5 + layout.caches + i: i for i in range(len(earlier))}
    return pl.pallas_call(
        functools.partial(attention_kernel, layout, heads_per, len(earlier)),
        grid=(heads_per + 1,),
        in_specs=in_specs,
        out_specs=[head_block, late_block, pair_block, pair_block, *dcache_blocks],
        out_shape=[
            jax.ShapeDtypeStruct(queries.shape, BF16),
            jax.ShapeDtypeStruct(queries.shape, BF16),
            jax.ShapeDtypeStruct(resp_keys.shape, BF16),
            jax.ShapeDtypeStruct(resp_keys.shape, BF16),
            *[jax.ShapeDtypeStruct(shape, BF16) for shape in layout.dcache_shapes()],
        ],
        scratch_shapes=[
            pltpu.VMEM((total_rows, HD), BF16),
            pltpu.VMEM((total_rows, HD), BF16),
            pltpu.VMEM((HD, total_rows), BF16),
            pltpu.VMEM((HD, total_rows), BF16),
            pltpu.VMEM((2, rows, HD), BF16),
            pltpu.VMEM((2, HD, rows), BF16),
            pltpu.VMEM((2, rows, HD), BF16),
            pltpu.VMEM((2, HD, rows), BF16),
            pltpu.VMEM((total_rows, rows), F32),
            pltpu.VMEM((total_rows, rows), F32),
            pltpu.VMEM((total_rows, rows), BF16),
            pltpu.VMEM((total_rows, rows), BF16),
            pltpu.VMEM((total_rows, rows), BF16),
            pltpu.VMEM((rows, rows), F32),
            pltpu.VMEM((rows, rows), F32),
            pltpu.VMEM((rows, rows), F32),
            pltpu.VMEM((rows, rows), F32),
            pltpu.VMEM((2, stats, rows), F32),
            pltpu.VMEM((2, 8, rows), F32),
            pltpu.VMEM((HD, total_rows), F32),
            pltpu.VMEM((HD, total_rows), F32),
            pltpu.VMEM((stats, rows), F32),
            pltpu.VMEM((stats, rows), F32),
            pltpu.VMEM((HD, rows), F32),
        ],
        input_output_aliases=aliases,
        cost_estimate=pl.CostEstimate(
            flops=12 * heads_per * rows * total_rows * HD,
            bytes_accessed=8 * heads_per * rows * HD,
            transcendentals=heads_per * rows * total_rows,
        ),
        compiler_params=pltpu.CompilerParams(vmem_limit_bytes=60 * 1024 * 1024),
        name=f"attend_pair_{pair}",
    )(lengths, queries, out_grad, resp_keys, resp_values, *caches, *earlier)


def whole_block(shape):
    return pl.BlockSpec(shape, lambda: (0,) * len(shape))


def cut_kernel(pairs, k_ref, v_ref, *outs):
    me = lax.axis_index("tensor")
    ranks = len(outs) // pairs
    for p in range(pairs):
        for i in range(ranks):
            columns = pl.ds(pl.multiple_of(((me ^ i) * pairs + p) * HD, HD), HD)
            outs[p * ranks + i][0] = k_ref[:, columns]
            outs[p * ranks + i][1] = v_ref[:, columns]


def cut(prompt_keys, prompt_values, pairs):
    rows, columns = prompt_keys.shape
    count = columns // HD
    blocks = pl.pallas_call(
        functools.partial(cut_kernel, pairs),
        in_specs=[whole_block((rows, columns))] * 2,
        out_specs=[whole_block((2, rows, HD))] * count,
        out_shape=[jax.ShapeDtypeStruct((2, rows, HD), BF16)] * count,
        name="cut",
    )(prompt_keys, prompt_values)
    return [blocks[p * count // pairs : (p + 1) * count // pairs] for p in range(pairs)]


def place_kernel(pairs, *refs):
    *ins, dk_ref, dv_ref = refs
    me = lax.axis_index("tensor")
    ranks = len(ins) // pairs
    for p in range(pairs):
        for i in range(ranks):
            columns = pl.ds(pl.multiple_of(((me ^ i) * pairs + p) * HD, HD), HD)
            dk_ref[:, columns] = ins[p * ranks + i][0].astype(F32)
            dv_ref[:, columns] = ins[p * ranks + i][1].astype(F32)


def place(blocks, pairs, columns):
    _, rows, _ = blocks[0].shape
    shape = (rows, columns)
    return pl.pallas_call(
        functools.partial(place_kernel, pairs),
        in_specs=[whole_block(blocks[0].shape)] * len(blocks),
        out_specs=[whole_block(shape)] * 2,
        out_shape=[jax.ShapeDtypeStruct(shape, F32)] * 2,
        name="place",
    )(*blocks)


def swap(blocks):
    count = len(blocks)
    return [blocks[0]] + [
        lax.ppermute(blocks[i], "tensor", [(j, j ^ i) for j in range(count)])
        for i in range(1, count)
    ]


def send(block, members, shift):
    return lax.ppermute(block, "resp", [(m, (m + shift) % members) for m in range(members)])


def cut_rows(block, count):
    rows = block.shape[1] // count
    return [block[:, i * rows : (i + 1) * rows] for i in range(count)]


def per_device(
    members, ranks, queries, resp_keys, resp_values, prompt_keys, prompt_values, out_grad, lengths
):
    query_width = queries.shape[2]
    pair_width = resp_keys.shape[2]
    pairs = pair_width // HD
    heads_per = query_width // pair_width
    own_rows, columns = prompt_keys.shape
    queries, out_grad, resp_keys, resp_values = (
        a[0] for a in (queries, out_grad, resp_keys, resp_values)
    )
    cuts = cut(prompt_keys, prompt_values, pairs)
    kinds = [Scattered(members, ranks * own_rows)]
    kinds += [Gathered(members, ranks * own_rows) for _ in range(pairs - 1)]
    swapped = swap(cuts[0])
    key, value = (jnp.concatenate([block[i] for block in swapped], axis=0) for i in range(2))
    if pairs > 1:
        key, value, cuts[1:] = lax.optimization_barrier((key, value, cuts[1:]))
    caches = [[key] + [send(key, members, shift) for shift in range(1, members)]]
    caches[0].append(lax.all_gather(value, "resp", axis=0))
    for p in range(1, pairs):
        own = jnp.concatenate(swap(cuts[p]), axis=1)
        own, caches[0] = lax.optimization_barrier((own, caches[0]))
        caches.append([lax.all_gather(own, "resp", axis=0)])
    earlier = ()
    totals = []
    for p in range(pairs):
        results = attend(
            kinds[p],
            p,
            heads_per,
            lengths,
            queries,
            out_grad,
            caches[p],
            resp_keys,
            resp_values,
            earlier,
        )
        earlier, dcaches = results[:4], results[4:]
        if totals:
            dcaches, totals[-1] = lax.optimization_barrier((dcaches, totals[-1]))
        if isinstance(kinds[p], Scattered):
            totals.append(lax.psum_scatter(dcaches[0], "resp", scatter_dimension=0))
        else:
            arrived = [dcaches[0]] + [
                send(dcaches[shift], members, shift) for shift in range(1, members)
            ]
            dkey = sum(block.astype(F32) for block in arrived).astype(BF16)
            dvalue = lax.psum_scatter(dcaches[members], "resp", scatter_dimension=0)
            totals.append(jnp.stack([dkey, dvalue]))
    blocks = [block for total in totals for block in swap(cut_rows(total, ranks))]
    key_grad, value_grad = place(blocks, pairs, columns)
    return (*(a[None] for a in earlier), key_grad, value_grad)


def solution(mesh):
    rows = P(("group", "resp"), None, "tensor")
    prompt = P(("group", "resp", "tensor"), None)
    return jax.shard_map(
        functools.partial(per_device, mesh.shape["resp"], mesh.shape["tensor"]),
        mesh=mesh,
        in_specs=(rows, rows, rows, prompt, prompt, rows, P(("group", "resp"))),
        out_specs=(rows, rows, rows, rows, prompt, prompt),
        check_vma=False,
    )
```

```python
import functools
import math

import jax
import jax.numpy as jnp
from jax import lax
from jax.experimental import pallas as pl
from jax.experimental.pallas import tpu as pltpu
from jax.sharding import PartitionSpec as P

HD = 128
SUB = 128
WIDE = 256
LOWEST = -1e30
BF16 = jnp.bfloat16
F32 = jnp.float32


def dot(a, b):
    return jnp.dot(a, b, preferred_element_type=F32)


def attention_kernel(
    layout,
    heads_per,
    earlier,
    len_ref,
    q_ref,
    g_ref,
    kr_ref,
    vr_ref,
    *rest,
):
    caches, rest = rest[: layout.caches], rest[layout.caches + earlier :]
    out_ref, dq_ref, dkr_ref, dvr_ref, *rest = rest
    dcaches, rest = rest[: layout.dcaches], rest[layout.dcaches :]
    (
        keys,
        values,
        keys_t,
        values_t,
        query,
        query_t,
        grad,
        grad_t,
        exps_even,
        exps_odd,
        weights_even,
        weights_odd,
        sgrads,
        score_even,
        score_odd,
        dprob_even,
        dprob_odd,
        fracs,
        deltas,
        dk_sum,
        dv_sum,
        tops,
        sums,
        mixture,
        held,
    ) = rest
    rows = q_ref.shape[0]
    prompt_rows = layout.prompt_rows
    total_rows = prompt_rows + rows
    half = rows // 2
    pieces = [(at, rows, 0) for at in range(0, prompt_rows, rows)]
    pieces += [(prompt_rows, half, 0), (prompt_rows + half, half, half)]
    count = len(pieces)
    factor = HD ** (-0.5)
    factor2 = factor * math.log2(math.e)
    length = len_ref[0]
    step = pl.program_id(0)
    exps = (exps_even, exps_odd)
    weights = (weights_even, weights_odd)
    scores = (score_even, score_odd)
    dprobs = (dprob_even, dprob_odd)

    def init():
        for at, key_block, value_block in layout.load(caches):
            keys[at, :] = key_block
            values[at, :] = value_block
        for at in range(0, prompt_rows, rows):
            at = pl.ds(at, rows)
            keys_t[:, at] = keys[at, :].T
            values_t[:, at] = values[at, :].T
        at = pl.ds(prompt_rows, rows)
        keys[at, :] = kr_ref[...]
        values[at, :] = vr_ref[...]
        keys_t[:, at] = kr_ref[...].T
        values_t[:, at] = vr_ref[...].T
        dk_sum[...] = jnp.zeros_like(dk_sum)
        dv_sum[...] = jnp.zeros_like(dv_sum)
        tops[...] = jnp.full_like(tops, LOWEST)
        sums[...] = jnp.zeros_like(sums)
        for ref in (*weights, sgrads):
            ref[prompt_rows + half :, :half] = jnp.zeros((half, half), BF16)

    def blocks(piece):
        at, size, row = pieces[piece]
        for u in range(0, size, SUB):
            for r in range(0, rows - row, SUB):
                yield u, r, slice(at + u, at + u + SUB), slice(row + r, row + r + SUB)

    def stat(block_at):
        return slice(block_at.start // SUB * 8, block_at.start // SUB * 8 + 8)

    def tiled(block):
        return block.reshape(SUB // 8, 8, SUB)

    def score_products(now, piece):
        at, size, row = pieces[piece]

        def product(r):
            scores[piece % 2][:size, r - row : r - row + WIDE] = dot(
                keys[at : at + size, :], query_t[now, :, r : r + WIDE]
            )

        return [functools.partial(product, r) for r in range(row, rows, WIDE)]

    def dprob_products(before, piece):
        at, size, row = pieces[piece]

        def product(r):
            dprobs[piece % 2][:size, r - row : r - row + WIDE] = dot(
                values[at : at + size, :], grad_t[before, :, r : r + WIDE]
            )

        return [functools.partial(product, r) for r in range(row, rows, WIDE)]

    def score_chains(now, piece):
        def chain(u, r, key_at, row_at):
            block = scores[piece % 2][u : u + SUB, r : r + SUB]
            if key_at.start >= prompt_rows:
                j = lax.broadcasted_iota(jnp.int32, (SUB, SUB), 0) + key_at.start - prompt_rows
                i = lax.broadcasted_iota(jnp.int32, (SUB, SUB), 1) + row_at.start
                block = jnp.where((j <= i) & (j < length), block, -jnp.inf)
            block = tiled(block) * factor2
            top = jnp.maximum(jnp.max(block, axis=0), LOWEST)
            exp = jnp.exp2(block - top[None])
            exps[now][key_at, row_at] = exp.reshape(SUB, SUB)
            tops[stat(key_at), row_at] = top
            sums[stat(key_at), row_at] = jnp.sum(exp, axis=0)

        return [functools.partial(chain, *block) for block in blocks(piece)]

    def frac(slot, key_at, row_at):
        return tiled(exps[slot][key_at, row_at]) * fracs[slot, stat(key_at), row_at][None]

    def grad_chains(before, piece):
        def chain(u, r, key_at, row_at):
            dprob = tiled(dprobs[piece % 2][u : u + SUB, r : r + SUB])
            sgrad = frac(before, key_at, row_at) * (dprob - deltas[before, :, row_at][None])
            sgrads[key_at, row_at] = sgrad.reshape(SUB, SUB).astype(BF16)

        return [functools.partial(chain, *block) for block in blocks(piece)]

    def weight_chains(now, piece):
        def chain(u, r, key_at, row_at):
            weight = frac(now, key_at, row_at).reshape(SUB, SUB)
            weights[now][key_at, row_at] = weight.astype(BF16)

        return [functools.partial(chain, *block) for block in blocks(piece)]

    def grad_products(before, piece):
        at, size, row = pieces[piece]

        def value_product(u):
            at = slice(u, u + WIDE)
            dv_sum[at, :] += dot(weights[before][at, row:], grad[before, row:, :])

        def key_product(u):
            at = slice(u, u + WIDE)
            dk_sum[at, :] += dot(sgrads[at, row:], query[before, row:, :])

        return [
            functools.partial(product, u)
            for u in range(at, at + size, WIDE)
            for product in (value_product, key_product)
        ]

    def query_products(before):
        def product(r):
            dquery = (factor * dot(keys_t[...], sgrads[:, r : r + WIDE])).T.astype(BF16)
            if before:
                dq_ref[r : r + WIDE, HD:] = dquery
                dq_ref[r : r + WIDE, :HD] = held[r : r + WIDE, :]
            else:
                held[r : r + WIDE, :] = dquery

        return [functools.partial(product, r) for r in range(0, rows, WIDE)]

    def out_products(now, piece):
        at, size, row = pieces[piece]

        def product(r):
            term = dot(values_t[:, at : at + size], weights[now][at : at + size, r : r + WIDE])
            if piece:
                term += mixture[:, r : r + WIDE]
            mixture[:, r : r + WIDE] = term

        return [functools.partial(product, r) for r in range(row, rows, WIDE)]

    def weave(products, chains):
        count = max(len(products), len(chains))
        for i in range(count):
            for jobs in (products, chains):
                for job in jobs[i * len(jobs) // count : (i + 1) * len(jobs) // count]:
                    job()

    def run(now, with_score, with_grad):
        before = 1 - now
        for stage in range(-1, count):
            products, chains = [], []
            if stage + 1 < count:
                if with_score:
                    products += score_products(now, stage + 1)
                if with_grad:
                    products += dprob_products(before, stage + 1)
            if stage >= 1 and with_grad:
                products += grad_products(before, stage - 1)
            if stage >= 0:
                both = [score_chains(now, stage)] if with_score else []
                both += [grad_chains(before, stage)] if with_grad else []
                chains = [chain for pair in zip(*both) for chain in pair]
            weave(products, chains)
        products = []
        if with_grad:
            products += grad_products(before, count - 1) + query_products(before)
        chains = []
        if with_score:
            set_fracs(now)
            chains = weight_chains(now, 0)
        weave(products, chains)
        if with_score:
            for piece in range(count):
                weave(
                    out_products(now, piece),
                    weight_chains(now, piece + 1) if piece + 1 < count else [],
                )
            finish(now)

    def prepare(now):
        columns = slice(now * HD, (now + 1) * HD)
        live_rows = lax.broadcasted_iota(jnp.int32, (rows, HD), 0) < length
        live_grad = jnp.where(live_rows, g_ref[:, columns].astype(F32), 0.0)
        grad[now] = live_grad.astype(BF16)
        grad_t[now] = live_grad.T.astype(BF16)
        query[now] = q_ref[:, columns]
        query_t[now] = q_ref[:, columns].T

    def set_fracs(now):
        top = jnp.max(tops[...], axis=0, keepdims=True)
        scale = jnp.exp2(tops[...] - top)
        total = jnp.sum(scale * sums[...], axis=0, keepdims=True)
        fracs[now] = scale * (1.0 / total)

    def finish(now):
        live_lanes = lax.broadcasted_iota(jnp.int32, (HD, rows), 1) < length
        attended = jnp.where(live_lanes, mixture[...], 0.0).astype(BF16).astype(F32)
        out_ref[:, now * HD : (now + 1) * HD] = attended.T.astype(BF16)
        delta = jnp.sum(grad_t[now].astype(F32) * attended, axis=0, keepdims=True)
        deltas[now] = jnp.broadcast_to(delta, (8, rows))

    steps = heads_per // 2

    @pl.when(step == 0)
    def _():
        init()
        prepare(0)
        run(0, True, False)

    @pl.when((step > 0) & (step < steps))
    def _():
        prepare(0)
        run(0, True, True)

    @pl.when(step < steps)
    def _():
        prepare(1)
        run(1, True, True)

    @pl.when(step == steps)
    def _():
        run(0, False, True)
        layout.store(dcaches, dk_sum, dv_sum, factor)
        at = pl.ds(prompt_rows, rows)
        dkr_ref[...] = (factor * dk_sum[at, :]).astype(BF16)
        dvr_ref[...] = dv_sum[at, :].astype(BF16)


class Gathered:
    def __init__(self, members, part_rows):
        self.members, self.part_rows = members, part_rows
        self.prompt_rows = members * part_rows
        self.caches, self.dcaches = 1, members + 1

    def cache_shapes(self):
        return [(self.members, 2, self.part_rows, HD)]

    def dcache_shapes(self):
        part = (self.part_rows, HD)
        return [part] * self.members + [(self.members, *part)]

    def load(self, caches):
        for m in range(self.members):
            at = pl.ds(m * self.part_rows, self.part_rows)
            yield at, caches[0][m, 0], caches[0][m, 1]

    def store(self, dcaches, dk_sum, dv_sum, factor):
        me = lax.axis_index("resp")
        for shift in range(self.members):
            part = lax.rem(me + shift, self.members) * self.part_rows
            at = pl.ds(pl.multiple_of(part, self.part_rows), self.part_rows)
            dcaches[shift][...] = (factor * dk_sum[at, :]).astype(BF16)
            at = pl.ds(shift * self.part_rows, self.part_rows)
            dcaches[self.members][shift] = dv_sum[at, :].astype(BF16)


class Scattered(Gathered):
    def __init__(self, members, part_rows):
        super().__init__(members, part_rows)
        self.caches, self.dcaches = members, 1

    def cache_shapes(self):
        return [(2, self.part_rows, HD)] * self.members

    def dcache_shapes(self):
        return super().cache_shapes()

    def load(self, caches):
        for shift, ref in enumerate(caches):
            yield pl.ds(shift * self.part_rows, self.part_rows), ref[0], ref[1]

    def store(self, dcaches, dk_sum, dv_sum, factor):
        me = lax.axis_index("resp")
        for shift in range(self.members):
            part = lax.rem(me - shift + self.members, self.members)
            at = pl.ds(shift * self.part_rows, self.part_rows)
            dcaches[0][part, 0] = (factor * dk_sum[at, :]).astype(BF16)
            dcaches[0][part, 1] = dv_sum[at, :].astype(BF16)


def attend(
    layout, pair, heads_per, lengths, queries, out_grad, caches, resp_keys, resp_values, earlier
):
    rows, query_width = queries.shape
    total_rows = layout.prompt_rows + rows
    steps = heads_per // 2
    first, last = pair * steps, (pair + 1) * steps - 1
    head_block = pl.BlockSpec((rows, 2 * HD), lambda s: (0, jnp.minimum(first + s, last)))
    late_block = pl.BlockSpec((rows, 2 * HD), lambda s: (0, jnp.maximum(first + s - 1, first)))
    pair_block = pl.BlockSpec((rows, HD), lambda s: (0, pair))
    cache_blocks = [
        pl.BlockSpec(shape, lambda s, rank=len(shape): (0,) * rank)
        for shape in layout.cache_shapes()
    ]
    dcache_blocks = [
        pl.BlockSpec(shape, lambda s, rank=len(shape): (0,) * rank)
        for shape in layout.dcache_shapes()
    ]
    stats = total_rows // SUB * 8
    in_specs = [
        pl.BlockSpec(memory_space=pltpu.SMEM),
        head_block,
        head_block,
        pair_block,
        pair_block,
        *cache_blocks,
    ] + [pl.BlockSpec(memory_space=pl.ANY)] * len(earlier)
    aliases = {5 + layout.caches + i: i for i in range(len(earlier))}
    return pl.pallas_call(
        functools.partial(attention_kernel, layout, heads_per, len(earlier)),
        grid=(steps + 1,),
        in_specs=in_specs,
        out_specs=[head_block, late_block, pair_block, pair_block, *dcache_blocks],
        out_shape=[
            jax.ShapeDtypeStruct(queries.shape, BF16),
            jax.ShapeDtypeStruct(queries.shape, BF16),
            jax.ShapeDtypeStruct(resp_keys.shape, BF16),
            jax.ShapeDtypeStruct(resp_keys.shape, BF16),
            *[jax.ShapeDtypeStruct(shape, BF16) for shape in layout.dcache_shapes()],
        ],
        scratch_shapes=[
            pltpu.VMEM((total_rows, HD), BF16),
            pltpu.VMEM((total_rows, HD), BF16),
            pltpu.VMEM((HD, total_rows), BF16),
            pltpu.VMEM((HD, total_rows), BF16),
            pltpu.VMEM((2, rows, HD), BF16),
            pltpu.VMEM((2, HD, rows), BF16),
            pltpu.VMEM((2, rows, HD), BF16),
            pltpu.VMEM((2, HD, rows), BF16),
            pltpu.VMEM((total_rows, rows), F32),
            pltpu.VMEM((total_rows, rows), F32),
            pltpu.VMEM((total_rows, rows), BF16),
            pltpu.VMEM((total_rows, rows), BF16),
            pltpu.VMEM((total_rows, rows), BF16),
            pltpu.VMEM((rows, rows), F32),
            pltpu.VMEM((rows, rows), F32),
            pltpu.VMEM((rows, rows), F32),
            pltpu.VMEM((rows, rows), F32),
            pltpu.VMEM((2, stats, rows), F32),
            pltpu.VMEM((2, 8, rows), F32),
            pltpu.VMEM((total_rows, HD), F32),
            pltpu.VMEM((total_rows, HD), F32),
            pltpu.VMEM((stats, rows), F32),
            pltpu.VMEM((stats, rows), F32),
            pltpu.VMEM((HD, rows), F32),
            pltpu.VMEM((rows, HD), BF16),
        ],
        input_output_aliases=aliases,
        cost_estimate=pl.CostEstimate(
            flops=12 * heads_per * rows * total_rows * HD,
            bytes_accessed=8 * heads_per * rows * HD,
            transcendentals=heads_per * rows * total_rows,
        ),
        compiler_params=pltpu.CompilerParams(vmem_limit_bytes=60 * 1024 * 1024),
        name=f"attend_pair_{pair}",
    )(lengths, queries, out_grad, resp_keys, resp_values, *caches, *earlier)


def whole_block(shape):
    return pl.BlockSpec(shape, lambda: (0,) * len(shape))


def cut_kernel(pairs, k_ref, v_ref, *outs):
    me = lax.axis_index("tensor")
    ranks = len(outs) // pairs
    for p in range(pairs):
        for i in range(ranks):
            columns = pl.ds(pl.multiple_of(((me ^ i) * pairs + p) * HD, HD), HD)
            outs[p * ranks + i][0] = k_ref[:, columns]
            outs[p * ranks + i][1] = v_ref[:, columns]


def cut(prompt_keys, prompt_values, pairs):
    rows, columns = prompt_keys.shape
    count = columns // HD
    blocks = pl.pallas_call(
        functools.partial(cut_kernel, pairs),
        in_specs=[whole_block((rows, columns))] * 2,
        out_specs=[whole_block((2, rows, HD))] * count,
        out_shape=[jax.ShapeDtypeStruct((2, rows, HD), BF16)] * count,
        name="cut",
    )(prompt_keys, prompt_values)
    return [blocks[p * count // pairs : (p + 1) * count // pairs] for p in range(pairs)]


def place_kernel(pairs, *refs):
    *ins, dk_ref, dv_ref = refs
    me = lax.axis_index("tensor")
    ranks = len(ins) // pairs
    for p in range(pairs):
        for i in range(ranks):
            columns = pl.ds(pl.multiple_of(((me ^ i) * pairs + p) * HD, HD), HD)
            dk_ref[:, columns] = ins[p * ranks + i][0].astype(F32)
            dv_ref[:, columns] = ins[p * ranks + i][1].astype(F32)


def place(blocks, pairs, columns):
    _, rows, _ = blocks[0].shape
    shape = (rows, columns)
    return pl.pallas_call(
        functools.partial(place_kernel, pairs),
        in_specs=[whole_block(blocks[0].shape)] * len(blocks),
        out_specs=[whole_block(shape)] * 2,
        out_shape=[jax.ShapeDtypeStruct(shape, F32)] * 2,
        name="place",
    )(*blocks)


def swap(blocks):
    count = len(blocks)
    return [blocks[0]] + [
        lax.ppermute(blocks[i], "tensor", [(j, j ^ i) for j in range(count)])
        for i in range(1, count)
    ]


def send(block, members, shift):
    return lax.ppermute(block, "resp", [(m, (m + shift) % members) for m in range(members)])


def cut_rows(block, count):
    rows = block.shape[1] // count
    return [block[:, i * rows : (i + 1) * rows] for i in range(count)]


def per_device(
    members, ranks, queries, resp_keys, resp_values, prompt_keys, prompt_values, out_grad, lengths
):
    query_width = queries.shape[2]
    pair_width = resp_keys.shape[2]
    pairs = pair_width // HD
    heads_per = query_width // pair_width
    own_rows, columns = prompt_keys.shape
    queries, out_grad, resp_keys, resp_values = (
        a[0] for a in (queries, out_grad, resp_keys, resp_values)
    )
    cuts = cut(prompt_keys, prompt_values, pairs)
    kinds = [Scattered(members, ranks * own_rows)]
    kinds += [Gathered(members, ranks * own_rows) for _ in range(pairs - 1)]
    own = jnp.concatenate(swap(cuts[0]), axis=1)
    if pairs > 1:
        own, cuts[1:] = lax.optimization_barrier((own, cuts[1:]))
    caches = [[own] + [send(own, members, shift) for shift in range(1, members)]]
    for p in range(1, pairs):
        own = jnp.concatenate(swap(cuts[p]), axis=1)
        own, caches[0] = lax.optimization_barrier((own, caches[0]))
        caches.append([lax.all_gather(own, "resp", axis=0)])
    earlier = ()
    totals = []
    for p in range(pairs):
        results = attend(
            kinds[p],
            p,
            heads_per,
            lengths,
            queries,
            out_grad,
            caches[p],
            resp_keys,
            resp_values,
            earlier,
        )
        earlier, dcaches = results[:4], results[4:]
        if totals:
            dcaches, totals[-1] = lax.optimization_barrier((dcaches, totals[-1]))
        if isinstance(kinds[p], Scattered):
            totals.append(lax.psum_scatter(dcaches[0], "resp", scatter_dimension=0))
        else:
            arrived = [dcaches[0]] + [
                send(dcaches[shift], members, shift) for shift in range(1, members)
            ]
            dkey = sum(block.astype(F32) for block in arrived).astype(BF16)
            dvalue = lax.psum_scatter(dcaches[members], "resp", scatter_dimension=0)
            totals.append(jnp.stack([dkey, dvalue]))
    blocks = [block for total in totals for block in swap(cut_rows(total, ranks))]
    key_grad, value_grad = place(blocks, pairs, columns)
    return (*(a[None] for a in earlier), key_grad, value_grad)


def solution(mesh):
    rows = P(("group", "resp"), None, "tensor")
    prompt = P(("group", "resp", "tensor"), None)
    return jax.shard_map(
        functools.partial(per_device, mesh.shape["resp"], mesh.shape["tensor"]),
        mesh=mesh,
        in_specs=(rows, rows, rows, prompt, prompt, rows, P(("group", "resp"))),
        out_specs=(rows, rows, rows, rows, prompt, prompt),
        check_vma=False,
    )
```

```python
import functools
import math

import jax
import jax.numpy as jnp
from jax import lax
from jax.experimental import pallas as pl
from jax.experimental.pallas import tpu as pltpu
from jax.sharding import PartitionSpec as P

HD = 128
SUB = 128
WIDE = 256
LOWEST = -1e30
BF16 = jnp.bfloat16
F32 = jnp.float32


def dot(a, b):
    return jnp.dot(a, b, preferred_element_type=F32)


def attention_kernel(
    layout,
    heads_per,
    earlier,
    len_ref,
    q_ref,
    g_ref,
    kr_ref,
    vr_ref,
    *rest,
):
    caches, rest = rest[: layout.caches], rest[layout.caches + earlier :]
    out_ref, dq_ref, dkr_ref, dvr_ref, *rest = rest
    dcaches, rest = rest[: layout.dcaches], rest[layout.dcaches :]
    (
        keys,
        values,
        keys_t,
        values_t,
        query,
        query_t,
        grad,
        grad_t,
        exps_even,
        exps_odd,
        weights_even,
        weights_odd,
        sgrads,
        fracs,
        deltas,
        dk_sum,
        dv_sum,
        tops,
        sums,
        mixture,
        held,
    ) = rest
    rows = q_ref.shape[0]
    prompt_rows = layout.prompt_rows
    total_rows = prompt_rows + rows
    half = rows // 2
    pieces = [(at, rows, 0) for at in range(0, prompt_rows, rows)]
    pieces += [(prompt_rows, half, 0), (prompt_rows + half, half, half)]
    count = len(pieces)
    factor = HD ** (-0.5)
    factor2 = factor * math.log2(math.e)
    length = len_ref[0]
    step = pl.program_id(0)
    exps = (exps_even, exps_odd)
    weights = (weights_even, weights_odd)

    def init():
        for at, key_block, value_block in layout.load(caches):
            keys[at, :] = key_block
            values[at, :] = value_block
        for at in range(0, prompt_rows, rows):
            at = pl.ds(at, rows)
            keys_t[:, at] = keys[at, :].T
            values_t[:, at] = values[at, :].T
        at = pl.ds(prompt_rows, rows)
        keys[at, :] = kr_ref[...]
        values[at, :] = vr_ref[...]
        keys_t[:, at] = kr_ref[...].T
        values_t[:, at] = vr_ref[...].T
        dk_sum[...] = jnp.zeros_like(dk_sum)
        dv_sum[...] = jnp.zeros_like(dv_sum)
        tops[...] = jnp.full_like(tops, LOWEST)
        sums[...] = jnp.zeros_like(sums)
        for ref in (*weights, sgrads):
            ref[prompt_rows + half :, :half] = jnp.zeros((half, half), BF16)

    def blocks(piece):
        at, size, row = pieces[piece]
        for u in range(0, size, SUB):
            for r in range(0, rows - row, SUB):
                yield u, r, slice(at + u, at + u + SUB), slice(row + r, row + r + SUB)

    def stat(block_at):
        return slice(block_at.start // SUB * 8, block_at.start // SUB * 8 + 8)

    def tiled(block):
        return block.reshape(SUB // 8, 8, SUB)

    def units(piece):
        at, size, row = pieces[piece]
        return [(u, r) for r in range(row, rows, WIDE) for u in range(at, at + size, WIDE)]

    def inner(u, r):
        for du in range(0, WIDE, SUB):
            for dr in range(0, WIDE, SUB):
                block = (slice(du, du + SUB), slice(dr, dr + SUB))
                yield block, slice(u + du, u + du + SUB), slice(r + dr, r + dr + SUB)

    def score_chains(now, piece):
        def chain(u, r):
            score = dot(keys[u : u + WIDE, :], query_t[now, :, r : r + WIDE])
            for at, key_at, row_at in inner(u, r):
                block = score[at]
                if key_at.start >= prompt_rows:
                    j = lax.broadcasted_iota(jnp.int32, (SUB, SUB), 0) + key_at.start - prompt_rows
                    i = lax.broadcasted_iota(jnp.int32, (SUB, SUB), 1) + row_at.start
                    block = jnp.where((j <= i) & (j < length), block, -jnp.inf)
                block = tiled(block) * factor2
                top = jnp.maximum(jnp.max(block, axis=0), LOWEST)
                exp = jnp.exp2(block - top[None])
                exps[now][key_at, row_at] = exp.reshape(SUB, SUB)
                tops[stat(key_at), row_at] = top
                sums[stat(key_at), row_at] = jnp.sum(exp, axis=0)

        return [functools.partial(chain, *unit) for unit in units(piece)]

    def frac(slot, key_at, row_at):
        return tiled(exps[slot][key_at, row_at]) * fracs[slot, stat(key_at), row_at][None]

    def grad_chains(before, piece):
        def chain(u, r):
            dprob = dot(values[u : u + WIDE, :], grad_t[before, :, r : r + WIDE])
            for at, key_at, row_at in inner(u, r):
                sgrad = tiled(dprob[at]) - deltas[before, :, row_at][None]
                sgrad = frac(before, key_at, row_at) * sgrad
                sgrads[key_at, row_at] = sgrad.reshape(SUB, SUB).astype(BF16)

        return [functools.partial(chain, *unit) for unit in units(piece)]

    def weight_chains(now, piece):
        def chain(u, r, key_at, row_at):
            weight = frac(now, key_at, row_at).reshape(SUB, SUB)
            weights[now][key_at, row_at] = weight.astype(BF16)

        return [functools.partial(chain, *block) for block in blocks(piece)]

    def grad_products(before, piece):
        at, size, row = pieces[piece]

        def value_product(u):
            at = slice(u, u + WIDE)
            dv_sum[at, :] += dot(weights[before][at, row:], grad[before, row:, :])

        def key_product(u):
            at = slice(u, u + WIDE)
            dk_sum[at, :] += dot(sgrads[at, row:], query[before, row:, :])

        return [
            functools.partial(product, u)
            for u in range(at, at + size, WIDE)
            for product in (value_product, key_product)
        ]

    def query_products(before):
        def product(r):
            dquery = (factor * dot(keys_t[...], sgrads[:, r : r + WIDE])).T.astype(BF16)
            if before:
                dq_ref[r : r + WIDE, HD:] = dquery
                dq_ref[r : r + WIDE, :HD] = held[r : r + WIDE, :]
            else:
                held[r : r + WIDE, :] = dquery

        return [functools.partial(product, r) for r in range(0, rows, WIDE)]

    def out_products(now, piece):
        at, size, row = pieces[piece]

        def product(r):
            term = dot(values_t[:, at : at + size], weights[now][at : at + size, r : r + WIDE])
            if piece:
                term += mixture[:, r : r + WIDE]
            mixture[:, r : r + WIDE] = term

        return [functools.partial(product, r) for r in range(row, rows, WIDE)]

    def weave(products, chains):
        count = max(len(products), len(chains))
        for i in range(count):
            for jobs in (products, chains):
                for job in jobs[i * len(jobs) // count : (i + 1) * len(jobs) // count]:
                    job()

    def run(now, with_score, with_grad):
        before = 1 - now
        for stage in range(count):
            products, chains = [], []
            if stage >= 1 and with_grad:
                products += grad_products(before, stage - 1)
            both = [score_chains(now, stage)] if with_score else []
            both += [grad_chains(before, stage)] if with_grad else []
            chains = [chain for pair in zip(*both) for chain in pair]
            weave(products, chains)
        products = []
        if with_grad:
            products += grad_products(before, count - 1) + query_products(before)
        chains = []
        if with_score:
            set_fracs(now)
            chains = weight_chains(now, 0)
        weave(products, chains)
        if with_score:
            for piece in range(count):
                weave(
                    out_products(now, piece),
                    weight_chains(now, piece + 1) if piece + 1 < count else [],
                )
            finish(now)

    def prepare(now):
        columns = slice(now * HD, (now + 1) * HD)
        live_rows = lax.broadcasted_iota(jnp.int32, (rows, HD), 0) < length
        live_grad = jnp.where(live_rows, g_ref[:, columns].astype(F32), 0.0)
        grad[now] = live_grad.astype(BF16)
        grad_t[now] = live_grad.T.astype(BF16)
        query[now] = q_ref[:, columns]
        query_t[now] = q_ref[:, columns].T

    def set_fracs(now):
        top = jnp.max(tops[...], axis=0, keepdims=True)
        scale = jnp.exp2(tops[...] - top)
        total = jnp.sum(scale * sums[...], axis=0, keepdims=True)
        fracs[now] = scale * (1.0 / total)

    def finish(now):
        live_lanes = lax.broadcasted_iota(jnp.int32, (HD, rows), 1) < length
        attended = jnp.where(live_lanes, mixture[...], 0.0).astype(BF16).astype(F32)
        out_ref[:, now * HD : (now + 1) * HD] = attended.T.astype(BF16)
        delta = jnp.sum(grad_t[now].astype(F32) * attended, axis=0, keepdims=True)
        deltas[now] = jnp.broadcast_to(delta, (8, rows))

    steps = heads_per // 2

    @pl.when(step == 0)
    def _():
        init()
        prepare(0)
        run(0, True, False)

    @pl.when((step > 0) & (step < steps))
    def _():
        prepare(0)
        run(0, True, True)

    @pl.when(step < steps)
    def _():
        prepare(1)
        run(1, True, True)

    @pl.when(step == steps)
    def _():
        run(0, False, True)
        layout.store(dcaches, dk_sum, dv_sum, factor)
        at = pl.ds(prompt_rows, rows)
        dkr_ref[...] = (factor * dk_sum[at, :]).astype(BF16)
        dvr_ref[...] = dv_sum[at, :].astype(BF16)


class Gathered:
    def __init__(self, members, part_rows):
        self.members, self.part_rows = members, part_rows
        self.prompt_rows = members * part_rows
        self.share = part_rows // 2
        self.caches, self.dcaches = 1, members + 1

    def cache_shapes(self):
        return [(self.members, 2, self.part_rows, HD)]

    def dcache_shapes(self):
        shape = (self.part_rows + self.share, HD)
        return [shape] * self.members + [(self.members, self.part_rows - self.share, HD)]

    def load(self, caches):
        for m in range(self.members):
            at = pl.ds(m * self.part_rows, self.part_rows)
            yield at, caches[0][m, 0], caches[0][m, 1]

    def store(self, dcaches, dk_sum, dv_sum, factor):
        me = lax.axis_index("resp")
        for shift in range(self.members):
            part = pl.multiple_of(lax.rem(me + shift, self.members) * self.part_rows, self.part_rows)
            key_at, value_at = pl.ds(part, self.part_rows), pl.ds(part, self.share)
            dcaches[shift][: self.part_rows, :] = (factor * dk_sum[key_at, :]).astype(BF16)
            dcaches[shift][self.part_rows :, :] = dv_sum[value_at, :].astype(BF16)
            at = pl.ds(shift * self.part_rows + self.share, self.part_rows - self.share)
            dcaches[self.members][shift] = dv_sum[at, :].astype(BF16)


class Scattered(Gathered):
    def __init__(self, members, part_rows):
        super().__init__(members, part_rows)
        self.caches, self.dcaches = members, 1

    def cache_shapes(self):
        return [(2, self.part_rows, HD)] * self.members

    def dcache_shapes(self):
        return super().cache_shapes()

    def load(self, caches):
        for shift, ref in enumerate(caches):
            yield pl.ds(shift * self.part_rows, self.part_rows), ref[0], ref[1]

    def store(self, dcaches, dk_sum, dv_sum, factor):
        me = lax.axis_index("resp")
        for shift in range(self.members):
            part = lax.rem(me - shift + self.members, self.members)
            at = pl.ds(shift * self.part_rows, self.part_rows)
            dcaches[0][part, 0] = (factor * dk_sum[at, :]).astype(BF16)
            dcaches[0][part, 1] = dv_sum[at, :].astype(BF16)


def attend(
    layout, pair, heads_per, lengths, queries, out_grad, caches, resp_keys, resp_values, earlier
):
    rows, query_width = queries.shape
    total_rows = layout.prompt_rows + rows
    steps = heads_per // 2
    first, last = pair * steps, (pair + 1) * steps - 1
    head_block = pl.BlockSpec((rows, 2 * HD), lambda s: (0, jnp.minimum(first + s, last)))
    late_block = pl.BlockSpec((rows, 2 * HD), lambda s: (0, jnp.maximum(first + s - 1, first)))
    pair_block = pl.BlockSpec((rows, HD), lambda s: (0, pair))
    cache_blocks = [
        pl.BlockSpec(shape, lambda s, rank=len(shape): (0,) * rank)
        for shape in layout.cache_shapes()
    ]
    dcache_blocks = [
        pl.BlockSpec(shape, lambda s, rank=len(shape): (0,) * rank)
        for shape in layout.dcache_shapes()
    ]
    stats = total_rows // SUB * 8
    in_specs = [
        pl.BlockSpec(memory_space=pltpu.SMEM),
        head_block,
        head_block,
        pair_block,
        pair_block,
        *cache_blocks,
    ] + [pl.BlockSpec(memory_space=pl.ANY)] * len(earlier)
    aliases = {5 + layout.caches + i: i for i in range(len(earlier))}
    return pl.pallas_call(
        functools.partial(attention_kernel, layout, heads_per, len(earlier)),
        grid=(steps + 1,),
        in_specs=in_specs,
        out_specs=[head_block, late_block, pair_block, pair_block, *dcache_blocks],
        out_shape=[
            jax.ShapeDtypeStruct(queries.shape, BF16),
            jax.ShapeDtypeStruct(queries.shape, BF16),
            jax.ShapeDtypeStruct(resp_keys.shape, BF16),
            jax.ShapeDtypeStruct(resp_keys.shape, BF16),
            *[jax.ShapeDtypeStruct(shape, BF16) for shape in layout.dcache_shapes()],
        ],
        scratch_shapes=[
            pltpu.VMEM((total_rows, HD), BF16),
            pltpu.VMEM((total_rows, HD), BF16),
            pltpu.VMEM((HD, total_rows), BF16),
            pltpu.VMEM((HD, total_rows), BF16),
            pltpu.VMEM((2, rows, HD), BF16),
            pltpu.VMEM((2, HD, rows), BF16),
            pltpu.VMEM((2, rows, HD), BF16),
            pltpu.VMEM((2, HD, rows), BF16),
            pltpu.VMEM((total_rows, rows), F32),
            pltpu.VMEM((total_rows, rows), F32),
            pltpu.VMEM((total_rows, rows), BF16),
            pltpu.VMEM((total_rows, rows), BF16),
            pltpu.VMEM((total_rows, rows), BF16),
            pltpu.VMEM((2, stats, rows), F32),
            pltpu.VMEM((2, 8, rows), F32),
            pltpu.VMEM((total_rows, HD), F32),
            pltpu.VMEM((total_rows, HD), F32),
            pltpu.VMEM((stats, rows), F32),
            pltpu.VMEM((stats, rows), F32),
            pltpu.VMEM((HD, rows), F32),
            pltpu.VMEM((rows, HD), BF16),
        ],
        input_output_aliases=aliases,
        cost_estimate=pl.CostEstimate(
            flops=12 * heads_per * rows * total_rows * HD,
            bytes_accessed=8 * heads_per * rows * HD,
            transcendentals=heads_per * rows * total_rows,
        ),
        compiler_params=pltpu.CompilerParams(vmem_limit_bytes=60 * 1024 * 1024),
        name=f"attend_pair_{pair}",
    )(lengths, queries, out_grad, resp_keys, resp_values, *caches, *earlier)


def whole_block(shape):
    return pl.BlockSpec(shape, lambda: (0,) * len(shape))


def cut_kernel(pairs, k_ref, v_ref, *outs):
    me = lax.axis_index("tensor")
    ranks = len(outs) // pairs
    for p in range(pairs):
        for i in range(ranks):
            columns = pl.ds(pl.multiple_of(((me ^ i) * pairs + p) * HD, HD), HD)
            outs[p * ranks + i][0] = k_ref[:, columns]
            outs[p * ranks + i][1] = v_ref[:, columns]


def cut(prompt_keys, prompt_values, pairs):
    rows, columns = prompt_keys.shape
    count = columns // HD
    blocks = pl.pallas_call(
        functools.partial(cut_kernel, pairs),
        in_specs=[whole_block((rows, columns))] * 2,
        out_specs=[whole_block((2, rows, HD))] * count,
        out_shape=[jax.ShapeDtypeStruct((2, rows, HD), BF16)] * count,
        name="cut",
    )(prompt_keys, prompt_values)
    return [blocks[p * count // pairs : (p + 1) * count // pairs] for p in range(pairs)]


def place_kernel(pairs, *refs):
    *ins, dk_ref, dv_ref = refs
    me = lax.axis_index("tensor")
    ranks = len(ins) // pairs
    for p in range(pairs):
        for i in range(ranks):
            columns = pl.ds(pl.multiple_of(((me ^ i) * pairs + p) * HD, HD), HD)
            dk_ref[:, columns] = ins[p * ranks + i][0].astype(F32)
            dv_ref[:, columns] = ins[p * ranks + i][1].astype(F32)


def place(blocks, pairs, columns):
    _, rows, _ = blocks[0].shape
    shape = (rows, columns)
    return pl.pallas_call(
        functools.partial(place_kernel, pairs),
        in_specs=[whole_block(blocks[0].shape)] * len(blocks),
        out_specs=[whole_block(shape)] * 2,
        out_shape=[jax.ShapeDtypeStruct(shape, F32)] * 2,
        name="place",
    )(*blocks)


def swap(blocks):
    count = len(blocks)
    return [blocks[0]] + [
        lax.ppermute(blocks[i], "tensor", [(j, j ^ i) for j in range(count)])
        for i in range(1, count)
    ]


def send(block, members, shift):
    return lax.ppermute(block, "resp", [(m, (m + shift) % members) for m in range(members)])


def cut_rows(block, count):
    rows = block.shape[1] // count
    return [block[:, i * rows : (i + 1) * rows] for i in range(count)]


def per_device(
    members, ranks, queries, resp_keys, resp_values, prompt_keys, prompt_values, out_grad, lengths
):
    query_width = queries.shape[2]
    pair_width = resp_keys.shape[2]
    pairs = pair_width // HD
    heads_per = query_width // pair_width
    own_rows, columns = prompt_keys.shape
    queries, out_grad, resp_keys, resp_values = (
        a[0] for a in (queries, out_grad, resp_keys, resp_values)
    )
    cuts = cut(prompt_keys, prompt_values, pairs)
    kinds = [Scattered(members, ranks * own_rows)]
    kinds += [Gathered(members, ranks * own_rows) for _ in range(pairs - 1)]
    own = jnp.concatenate(swap(cuts[0]), axis=1)
    if pairs > 1:
        own, cuts[1:] = lax.optimization_barrier((own, cuts[1:]))
    caches = [[own] + [send(own, members, shift) for shift in range(1, members)]]
    for p in range(1, pairs):
        own = jnp.concatenate(swap(cuts[p]), axis=1)
        own, caches[0] = lax.optimization_barrier((own, caches[0]))
        caches.append([lax.all_gather(own, "resp", axis=0)])
    earlier = ()
    totals = []
    for p in range(pairs):
        results = attend(
            kinds[p],
            p,
            heads_per,
            lengths,
            queries,
            out_grad,
            caches[p],
            resp_keys,
            resp_values,
            earlier,
        )
        earlier, dcaches = results[:4], results[4:]
        if totals:
            dcaches, totals[-1] = lax.optimization_barrier((dcaches, totals[-1]))
        if isinstance(kinds[p], Scattered):
            totals.append(lax.psum_scatter(dcaches[0], "resp", scatter_dimension=0))
        else:
            arrived = [dcaches[0]] + [
                send(dcaches[shift], members, shift) for shift in range(1, members)
            ]
            both = sum(block.astype(F32) for block in arrived).astype(BF16)
            rest = lax.psum_scatter(dcaches[members], "resp", scatter_dimension=0)
            both = jnp.concatenate([both, rest], axis=0)
            totals.append(both.reshape(2, ranks * own_rows, HD))
    blocks = [block for total in totals for block in swap(cut_rows(total, ranks))]
    key_grad, value_grad = place(blocks, pairs, columns)
    return (*(a[None] for a in earlier), key_grad, value_grad)


def solution(mesh):
    rows = P(("group", "resp"), None, "tensor")
    prompt = P(("group", "resp", "tensor"), None)
    return jax.shard_map(
        functools.partial(per_device, mesh.shape["resp"], mesh.shape["tensor"]),
        mesh=mesh,
        in_specs=(rows, rows, rows, prompt, prompt, rows, P(("group", "resp"))),
        out_specs=(rows, rows, rows, rows, prompt, prompt),
        check_vma=False,
    )
```

```python
import functools
import math

import jax
import jax.numpy as jnp
from jax import lax
from jax.experimental import pallas as pl
from jax.experimental.pallas import tpu as pltpu
from jax.sharding import PartitionSpec as P

HD = 128
SUB = 128
WIDE = 256
LOWEST = -1e30
BF16 = jnp.bfloat16
F32 = jnp.float32


def dot(a, b):
    return jnp.dot(a, b, preferred_element_type=F32)


def attention_kernel(
    layout,
    heads_per,
    earlier,
    len_ref,
    q_ref,
    g_ref,
    kr_ref,
    vr_ref,
    *rest,
):
    caches, rest = rest[: layout.caches], rest[layout.caches + earlier :]
    out_ref, dq_ref, dkr_ref, dvr_ref, *rest = rest
    dcaches, rest = rest[: layout.dcaches], rest[layout.dcaches :]
    (
        keys,
        values,
        keys_t,
        values_t,
        query,
        query_t,
        grad,
        grad_t,
        exps_even,
        exps_odd,
        weights_even,
        weights_odd,
        sgrads,
        fracs,
        deltas,
        dk_sum,
        dv_sum,
        tops,
        sums,
        mixture,
        held,
    ) = rest
    rows = q_ref.shape[0]
    prompt_rows = layout.prompt_rows
    total_rows = prompt_rows + rows
    half = rows // 2
    pieces = [(at, rows, 0) for at in range(0, prompt_rows, rows)]
    pieces += [(prompt_rows, half, 0), (prompt_rows + half, half, half)]
    count = len(pieces)
    factor = HD ** (-0.5)
    factor2 = factor * math.log2(math.e)
    length = len_ref[0]
    step = pl.program_id(0)
    exps = (exps_even, exps_odd)
    weights = (weights_even, weights_odd)

    def init():
        for at, key_block, value_block in layout.load(caches):
            keys[at, :] = key_block
            values[at, :] = value_block
        for at in range(0, prompt_rows, rows):
            at = pl.ds(at, rows)
            keys_t[:, at] = keys[at, :].T
            values_t[:, at] = values[at, :].T
        at = pl.ds(prompt_rows, rows)
        keys[at, :] = kr_ref[...]
        values[at, :] = vr_ref[...]
        keys_t[:, at] = kr_ref[...].T
        values_t[:, at] = vr_ref[...].T
        dk_sum[...] = jnp.zeros_like(dk_sum)
        dv_sum[...] = jnp.zeros_like(dv_sum)
        tops[...] = jnp.full_like(tops, LOWEST)
        sums[...] = jnp.zeros_like(sums)
        for ref in (*weights, sgrads):
            ref[prompt_rows + half :, :half] = jnp.zeros((half, half), BF16)

    def blocks(piece):
        at, size, row = pieces[piece]
        for u in range(0, size, SUB):
            for r in range(0, rows - row, SUB):
                yield u, r, slice(at + u, at + u + SUB), slice(row + r, row + r + SUB)

    def stat(block_at):
        return slice(block_at.start // SUB * 8, block_at.start // SUB * 8 + 8)

    def tiled(block):
        return block.reshape(SUB // 8, 8, SUB)

    def units(piece):
        at, size, row = pieces[piece]
        return [(at, size, r) for r in range(row, rows, WIDE)]

    def inner(u, size, r):
        for du in range(0, size, SUB):
            for dr in range(0, WIDE, SUB):
                block = (slice(du, du + SUB), slice(dr, dr + SUB))
                yield block, slice(u + du, u + du + SUB), slice(r + dr, r + dr + SUB)

    def score_chains(now, piece):
        def chain(u, size, r):
            score = dot(keys[u : u + size, :], query_t[now, :, r : r + WIDE])
            for at, key_at, row_at in inner(u, size, r):
                block = score[at]
                if key_at.start >= prompt_rows:
                    j = lax.broadcasted_iota(jnp.int32, (SUB, SUB), 0) + key_at.start - prompt_rows
                    i = lax.broadcasted_iota(jnp.int32, (SUB, SUB), 1) + row_at.start
                    block = jnp.where((j <= i) & (j < length), block, -jnp.inf)
                block = tiled(block) * factor2
                top = jnp.maximum(jnp.max(block, axis=0), LOWEST)
                exp = jnp.exp2(block - top[None])
                exps[now][key_at, row_at] = exp.reshape(SUB, SUB)
                tops[stat(key_at), row_at] = top
                sums[stat(key_at), row_at] = jnp.sum(exp, axis=0)

        return [functools.partial(chain, *unit) for unit in units(piece)]

    def frac(slot, key_at, row_at):
        return tiled(exps[slot][key_at, row_at]) * fracs[slot, stat(key_at), row_at][None]

    def grad_chains(before, piece):
        def chain(u, size, r):
            dprob = dot(values[u : u + size, :], grad_t[before, :, r : r + WIDE])
            for at, key_at, row_at in inner(u, size, r):
                sgrad = tiled(dprob[at]) - deltas[before, :, row_at][None]
                sgrad = frac(before, key_at, row_at) * sgrad
                sgrads[key_at, row_at] = sgrad.reshape(SUB, SUB).astype(BF16)

        return [functools.partial(chain, *unit) for unit in units(piece)]

    def weight_chains(now, piece):
        def chain(u, r, key_at, row_at):
            weight = frac(now, key_at, row_at).reshape(SUB, SUB)
            weights[now][key_at, row_at] = weight.astype(BF16)

        return [functools.partial(chain, *block) for block in blocks(piece)]

    def grad_products(before, piece):
        at, size, row = pieces[piece]

        def value_product(u):
            at = slice(u, u + WIDE)
            dv_sum[at, :] += dot(weights[before][at, row:], grad[before, row:, :])

        def key_product(u):
            at = slice(u, u + WIDE)
            dk_sum[at, :] += dot(sgrads[at, row:], query[before, row:, :])

        return [
            functools.partial(product, u)
            for u in range(at, at + size, WIDE)
            for product in (value_product, key_product)
        ]

    def query_products(before):
        def product(r):
            dquery = (factor * dot(keys_t[...], sgrads[:, r : r + WIDE])).T.astype(BF16)
            if before:
                dq_ref[r : r + WIDE, HD:] = dquery
                dq_ref[r : r + WIDE, :HD] = held[r : r + WIDE, :]
            else:
                held[r : r + WIDE, :] = dquery

        return [functools.partial(product, r) for r in range(0, rows, WIDE)]

    def out_products(now, piece):
        at, size, row = pieces[piece]

        def product(r):
            term = dot(values_t[:, at : at + size], weights[now][at : at + size, r : r + WIDE])
            if piece:
                term += mixture[:, r : r + WIDE]
            mixture[:, r : r + WIDE] = term

        return [functools.partial(product, r) for r in range(row, rows, WIDE)]

    def weave(products, chains):
        count = max(len(products), len(chains))
        for i in range(count):
            for jobs in (products, chains):
                for job in jobs[i * len(jobs) // count : (i + 1) * len(jobs) // count]:
                    job()

    def run(now, with_score, with_grad):
        before = 1 - now
        for stage in range(count):
            products, chains = [], []
            if stage >= 1 and with_grad:
                products += grad_products(before, stage - 1)
            both = [score_chains(now, stage)] if with_score else []
            both += [grad_chains(before, stage)] if with_grad else []
            chains = [chain for pair in zip(*both) for chain in pair]
            weave(products, chains)
        products = []
        if with_grad:
            products += grad_products(before, count - 1) + query_products(before)
        chains = []
        if with_score:
            set_fracs(now)
            chains = weight_chains(now, 0)
        weave(products, chains)
        if with_score:
            for piece in range(count):
                weave(
                    out_products(now, piece),
                    weight_chains(now, piece + 1) if piece + 1 < count else [],
                )
            finish(now)

    def prepare(now):
        columns = slice(now * HD, (now + 1) * HD)
        live_rows = lax.broadcasted_iota(jnp.int32, (rows, HD), 0) < length
        live_grad = jnp.where(live_rows, g_ref[:, columns].astype(F32), 0.0)
        grad[now] = live_grad.astype(BF16)
        grad_t[now] = live_grad.T.astype(BF16)
        query[now] = q_ref[:, columns]
        query_t[now] = q_ref[:, columns].T

    def set_fracs(now):
        top = jnp.max(tops[...], axis=0, keepdims=True)
        scale = jnp.exp2(tops[...] - top)
        total = jnp.sum(scale * sums[...], axis=0, keepdims=True)
        fracs[now] = scale * (1.0 / total)

    def finish(now):
        live_lanes = lax.broadcasted_iota(jnp.int32, (HD, rows), 1) < length
        attended = jnp.where(live_lanes, mixture[...], 0.0).astype(BF16).astype(F32)
        out_ref[:, now * HD : (now + 1) * HD] = attended.T.astype(BF16)
        delta = jnp.sum(grad_t[now].astype(F32) * attended, axis=0, keepdims=True)
        deltas[now] = jnp.broadcast_to(delta, (8, rows))

    steps = heads_per // 2

    @pl.when(step == 0)
    def _():
        init()
        prepare(0)
        run(0, True, False)

    @pl.when((step > 0) & (step < steps))
    def _():
        prepare(0)
        run(0, True, True)

    @pl.when(step < steps)
    def _():
        prepare(1)
        run(1, True, True)

    @pl.when(step == steps)
    def _():
        run(0, False, True)
        layout.store(dcaches, dk_sum, dv_sum, factor)
        at = pl.ds(prompt_rows, rows)
        dkr_ref[...] = (factor * dk_sum[at, :]).astype(BF16)
        dvr_ref[...] = dv_sum[at, :].astype(BF16)


class Gathered:
    def __init__(self, members, part_rows):
        self.members, self.part_rows = members, part_rows
        self.prompt_rows = members * part_rows
        self.share = part_rows // 2
        self.caches, self.dcaches = 1, members + 1

    def cache_shapes(self):
        return [(self.members, 2, self.part_rows, HD)]

    def dcache_shapes(self):
        shape = (self.part_rows + self.share, HD)
        return [shape] * self.members + [(self.members, self.part_rows - self.share, HD)]

    def load(self, caches):
        for m in range(self.members):
            at = pl.ds(m * self.part_rows, self.part_rows)
            yield at, caches[0][m, 0], caches[0][m, 1]

    def store(self, dcaches, dk_sum, dv_sum, factor):
        me = lax.axis_index("resp")
        for shift in range(self.members):
            part = pl.multiple_of(lax.rem(me + shift, self.members) * self.part_rows, self.part_rows)
            key_at, value_at = pl.ds(part, self.part_rows), pl.ds(part, self.share)
            dcaches[shift][: self.part_rows, :] = (factor * dk_sum[key_at, :]).astype(BF16)
            dcaches[shift][self.part_rows :, :] = dv_sum[value_at, :].astype(BF16)
            at = pl.ds(shift * self.part_rows + self.share, self.part_rows - self.share)
            dcaches[self.members][shift] = dv_sum[at, :].astype(BF16)


class Scattered(Gathered):
    def __init__(self, members, part_rows):
        super().__init__(members, part_rows)
        self.caches, self.dcaches = members, 1

    def cache_shapes(self):
        return [(2, self.part_rows, HD)] * self.members

    def dcache_shapes(self):
        return super().cache_shapes()

    def load(self, caches):
        for shift, ref in enumerate(caches):
            yield pl.ds(shift * self.part_rows, self.part_rows), ref[0], ref[1]

    def store(self, dcaches, dk_sum, dv_sum, factor):
        me = lax.axis_index("resp")
        for shift in range(self.members):
            part = lax.rem(me - shift + self.members, self.members)
            at = pl.ds(shift * self.part_rows, self.part_rows)
            dcaches[0][part, 0] = (factor * dk_sum[at, :]).astype(BF16)
            dcaches[0][part, 1] = dv_sum[at, :].astype(BF16)


def attend(
    layout, pair, heads_per, lengths, queries, out_grad, caches, resp_keys, resp_values, earlier
):
    rows, query_width = queries.shape
    total_rows = layout.prompt_rows + rows
    steps = heads_per // 2
    first, last = pair * steps, (pair + 1) * steps - 1
    head_block = pl.BlockSpec((rows, 2 * HD), lambda s: (0, jnp.minimum(first + s, last)))
    late_block = pl.BlockSpec((rows, 2 * HD), lambda s: (0, jnp.maximum(first + s - 1, first)))
    pair_block = pl.BlockSpec((rows, HD), lambda s: (0, pair))
    cache_blocks = [
        pl.BlockSpec(shape, lambda s, rank=len(shape): (0,) * rank)
        for shape in layout.cache_shapes()
    ]
    dcache_blocks = [
        pl.BlockSpec(shape, lambda s, rank=len(shape): (0,) * rank)
        for shape in layout.dcache_shapes()
    ]
    stats = total_rows // SUB * 8
    in_specs = [
        pl.BlockSpec(memory_space=pltpu.SMEM),
        head_block,
        head_block,
        pair_block,
        pair_block,
        *cache_blocks,
    ] + [pl.BlockSpec(memory_space=pl.ANY)] * len(earlier)
    aliases = {5 + layout.caches + i: i for i in range(len(earlier))}
    return pl.pallas_call(
        functools.partial(attention_kernel, layout, heads_per, len(earlier)),
        grid=(steps + 1,),
        in_specs=in_specs,
        out_specs=[head_block, late_block, pair_block, pair_block, *dcache_blocks],
        out_shape=[
            jax.ShapeDtypeStruct(queries.shape, BF16),
            jax.ShapeDtypeStruct(queries.shape, BF16),
            jax.ShapeDtypeStruct(resp_keys.shape, BF16),
            jax.ShapeDtypeStruct(resp_keys.shape, BF16),
            *[jax.ShapeDtypeStruct(shape, BF16) for shape in layout.dcache_shapes()],
        ],
        scratch_shapes=[
            pltpu.VMEM((total_rows, HD), BF16),
            pltpu.VMEM((total_rows, HD), BF16),
            pltpu.VMEM((HD, total_rows), BF16),
            pltpu.VMEM((HD, total_rows), BF16),
            pltpu.VMEM((2, rows, HD), BF16),
            pltpu.VMEM((2, HD, rows), BF16),
            pltpu.VMEM((2, rows, HD), BF16),
            pltpu.VMEM((2, HD, rows), BF16),
            pltpu.VMEM((total_rows, rows), F32),
            pltpu.VMEM((total_rows, rows), F32),
            pltpu.VMEM((total_rows, rows), BF16),
            pltpu.VMEM((total_rows, rows), BF16),
            pltpu.VMEM((total_rows, rows), BF16),
            pltpu.VMEM((2, stats, rows), F32),
            pltpu.VMEM((2, 8, rows), F32),
            pltpu.VMEM((total_rows, HD), F32),
            pltpu.VMEM((total_rows, HD), F32),
            pltpu.VMEM((stats, rows), F32),
            pltpu.VMEM((stats, rows), F32),
            pltpu.VMEM((HD, rows), F32),
            pltpu.VMEM((rows, HD), BF16),
        ],
        input_output_aliases=aliases,
        cost_estimate=pl.CostEstimate(
            flops=12 * heads_per * rows * total_rows * HD,
            bytes_accessed=8 * heads_per * rows * HD,
            transcendentals=heads_per * rows * total_rows,
        ),
        compiler_params=pltpu.CompilerParams(vmem_limit_bytes=60 * 1024 * 1024),
        name=f"attend_pair_{pair}",
    )(lengths, queries, out_grad, resp_keys, resp_values, *caches, *earlier)


def whole_block(shape):
    return pl.BlockSpec(shape, lambda: (0,) * len(shape))


def cut_kernel(pairs, k_ref, v_ref, *outs):
    me = lax.axis_index("tensor")
    ranks = len(outs) // pairs
    for p in range(pairs):
        for i in range(ranks):
            columns = pl.ds(pl.multiple_of(((me ^ i) * pairs + p) * HD, HD), HD)
            outs[p * ranks + i][0] = k_ref[:, columns]
            outs[p * ranks + i][1] = v_ref[:, columns]


def cut(prompt_keys, prompt_values, pairs):
    rows, columns = prompt_keys.shape
    count = columns // HD
    blocks = pl.pallas_call(
        functools.partial(cut_kernel, pairs),
        in_specs=[whole_block((rows, columns))] * 2,
        out_specs=[whole_block((2, rows, HD))] * count,
        out_shape=[jax.ShapeDtypeStruct((2, rows, HD), BF16)] * count,
        name="cut",
    )(prompt_keys, prompt_values)
    return [blocks[p * count // pairs : (p + 1) * count // pairs] for p in range(pairs)]


def place_kernel(pairs, *refs):
    *ins, dk_ref, dv_ref = refs
    me = lax.axis_index("tensor")
    ranks = len(ins) // pairs
    for p in range(pairs):
        for i in range(ranks):
            columns = pl.ds(pl.multiple_of(((me ^ i) * pairs + p) * HD, HD), HD)
            dk_ref[:, columns] = ins[p * ranks + i][0].astype(F32)
            dv_ref[:, columns] = ins[p * ranks + i][1].astype(F32)


def place(blocks, pairs, columns):
    _, rows, _ = blocks[0].shape
    shape = (rows, columns)
    return pl.pallas_call(
        functools.partial(place_kernel, pairs),
        in_specs=[whole_block(blocks[0].shape)] * len(blocks),
        out_specs=[whole_block(shape)] * 2,
        out_shape=[jax.ShapeDtypeStruct(shape, F32)] * 2,
        name="place",
    )(*blocks)


def swap(blocks):
    count = len(blocks)
    return [blocks[0]] + [
        lax.ppermute(blocks[i], "tensor", [(j, j ^ i) for j in range(count)])
        for i in range(1, count)
    ]


def send(block, members, shift):
    return lax.ppermute(block, "resp", [(m, (m + shift) % members) for m in range(members)])


def cut_rows(block, count):
    rows = block.shape[1] // count
    return [block[:, i * rows : (i + 1) * rows] for i in range(count)]


def per_device(
    members, ranks, queries, resp_keys, resp_values, prompt_keys, prompt_values, out_grad, lengths
):
    query_width = queries.shape[2]
    pair_width = resp_keys.shape[2]
    pairs = pair_width // HD
    heads_per = query_width // pair_width
    own_rows, columns = prompt_keys.shape
    queries, out_grad, resp_keys, resp_values = (
        a[0] for a in (queries, out_grad, resp_keys, resp_values)
    )
    cuts = cut(prompt_keys, prompt_values, pairs)
    kinds = [Scattered(members, ranks * own_rows)]
    kinds += [Gathered(members, ranks * own_rows) for _ in range(pairs - 1)]
    own = jnp.concatenate(swap(cuts[0]), axis=1)
    if pairs > 1:
        own, cuts[1:] = lax.optimization_barrier((own, cuts[1:]))
    caches = [[own] + [send(own, members, shift) for shift in range(1, members)]]
    for p in range(1, pairs):
        own = jnp.concatenate(swap(cuts[p]), axis=1)
        own, caches[0] = lax.optimization_barrier((own, caches[0]))
        caches.append([lax.all_gather(own, "resp", axis=0)])
    earlier = ()
    totals = []
    for p in range(pairs):
        results = attend(
            kinds[p],
            p,
            heads_per,
            lengths,
            queries,
            out_grad,
            caches[p],
            resp_keys,
            resp_values,
            earlier,
        )
        earlier, dcaches = results[:4], results[4:]
        if totals:
            dcaches, totals[-1] = lax.optimization_barrier((dcaches, totals[-1]))
        if isinstance(kinds[p], Scattered):
            totals.append(lax.psum_scatter(dcaches[0], "resp", scatter_dimension=0))
        else:
            arrived = [dcaches[0]] + [
                send(dcaches[shift], members, shift) for shift in range(1, members)
            ]
            both = sum(block.astype(F32) for block in arrived).astype(BF16)
            rest = lax.psum_scatter(dcaches[members], "resp", scatter_dimension=0)
            parts = ranks * own_rows
            keys, both = both[:parts], both[parts:]
            split = both.shape[0] // own_rows
            values = [both[i * own_rows : (i + 1) * own_rows] for i in range(split)]
            values += [rest[i * own_rows : (i + 1) * own_rows] for i in range(ranks - split)]
            pieces = [keys[i * own_rows : (i + 1) * own_rows] for i in range(ranks)]
            totals.append([jnp.stack(both) for both in zip(pieces, values)])
    blocks = []
    for total in totals:
        blocks += swap(total if isinstance(total, list) else cut_rows(total, ranks))
    key_grad, value_grad = place(blocks, pairs, columns)
    return (*(a[None] for a in earlier), key_grad, value_grad)


def solution(mesh):
    rows = P(("group", "resp"), None, "tensor")
    prompt = P(("group", "resp", "tensor"), None)
    return jax.shard_map(
        functools.partial(per_device, mesh.shape["resp"], mesh.shape["tensor"]),
        mesh=mesh,
        in_specs=(rows, rows, rows, prompt, prompt, rows, P(("group", "resp"))),
        out_specs=(rows, rows, rows, rows, prompt, prompt),
        check_vma=False,
    )
```

```python
import functools
import math

import jax
import jax.numpy as jnp
from jax import lax
from jax.experimental import pallas as pl
from jax.experimental.pallas import tpu as pltpu
from jax.sharding import PartitionSpec as P

HD = 128
SUB = 128
WIDE = 256
LOWEST = -1e30
BF16 = jnp.bfloat16
F32 = jnp.float32


def dot(a, b):
    return jnp.dot(a, b, preferred_element_type=F32)


def attention_kernel(
    layout,
    heads_per,
    earlier,
    len_ref,
    q_ref,
    g_ref,
    kr_ref,
    vr_ref,
    *rest,
):
    caches, rest = rest[: layout.caches], rest[layout.caches + earlier :]
    out_ref, dq_ref, dkr_ref, dvr_ref, *rest = rest
    dcaches, rest = rest[: layout.dcaches], rest[layout.dcaches :]
    (
        keys,
        values,
        keys_t,
        values_t,
        query,
        query_t,
        grad,
        grad_t,
        exps_even,
        exps_odd,
        weights_even,
        weights_odd,
        sgrads,
        fracs,
        deltas,
        dk_sum,
        dv_sum,
        tops,
        sums,
        mixture,
        held,
    ) = rest
    rows = q_ref.shape[0]
    prompt_rows = layout.prompt_rows
    total_rows = prompt_rows + rows
    half = rows // 2
    pieces = [(at, rows, 0) for at in range(0, prompt_rows, rows)]
    pieces += [(prompt_rows, half, 0), (prompt_rows + half, half, half)]
    count = len(pieces)
    factor = HD ** (-0.5)
    factor2 = factor * math.log2(math.e)
    length = len_ref[0]
    step = pl.program_id(0)
    exps = (exps_even, exps_odd)
    weights = (weights_even, weights_odd)

    def init():
        for at, key_block, value_block in layout.load(caches):
            keys[at, :] = key_block
            values[at, :] = value_block
        for at in range(0, prompt_rows, rows):
            at = pl.ds(at, rows)
            keys_t[:, at] = keys[at, :].T
            values_t[:, at] = values[at, :].T
        at = pl.ds(prompt_rows, rows)
        keys[at, :] = kr_ref[...]
        values[at, :] = vr_ref[...]
        keys_t[:, at] = kr_ref[...].T
        values_t[:, at] = vr_ref[...].T
        dk_sum[...] = jnp.zeros_like(dk_sum)
        dv_sum[...] = jnp.zeros_like(dv_sum)
        tops[...] = jnp.full_like(tops, LOWEST)
        sums[...] = jnp.zeros_like(sums)
        for ref in (*weights, sgrads):
            ref[prompt_rows + half :, :half] = jnp.zeros((half, half), BF16)

    def blocks(piece):
        at, size, row = pieces[piece]
        for u in range(0, size, SUB):
            for r in range(0, rows - row, SUB):
                yield u, r, slice(at + u, at + u + SUB), slice(row + r, row + r + SUB)

    def stat(block_at):
        return slice(block_at.start // SUB * 8, block_at.start // SUB * 8 + 8)

    def tiled(block):
        return block.reshape(SUB // 8, 8, SUB)

    def units(piece):
        at, size, row = pieces[piece]
        return [(u, r) for r in range(row, rows, WIDE) for u in range(at, at + size, WIDE)]

    def inner(u, r):
        for du in range(0, WIDE, SUB):
            for dr in range(0, WIDE, SUB):
                block = (slice(du, du + SUB), slice(dr, dr + SUB))
                yield block, slice(u + du, u + du + SUB), slice(r + dr, r + dr + SUB)

    def score_chains(now, piece):
        def chain(u, r):
            score = dot(keys[u : u + WIDE, :], query_t[now, :, r : r + WIDE])
            for at, key_at, row_at in inner(u, r):
                block = score[at]
                if key_at.start >= prompt_rows:
                    j = lax.broadcasted_iota(jnp.int32, (SUB, SUB), 0) + key_at.start - prompt_rows
                    i = lax.broadcasted_iota(jnp.int32, (SUB, SUB), 1) + row_at.start
                    block = jnp.where((j <= i) & (j < length), block, -jnp.inf)
                block = tiled(block) * factor2
                top = jnp.maximum(jnp.max(block, axis=0), LOWEST)
                exp = jnp.exp2(block - top[None])
                exps[now][key_at, row_at] = exp.reshape(SUB, SUB)
                tops[stat(key_at), row_at] = top
                sums[stat(key_at), row_at] = jnp.sum(exp, axis=0)

        return [functools.partial(chain, *unit) for unit in units(piece)]

    def frac(slot, key_at, row_at):
        return tiled(exps[slot][key_at, row_at]) * fracs[slot, stat(key_at), row_at][None]

    def grad_chains(before, piece):
        def chain(u, r):
            dprob = dot(values[u : u + WIDE, :], grad_t[before, :, r : r + WIDE])
            for at, key_at, row_at in inner(u, r):
                sgrad = tiled(dprob[at]) - deltas[before, :, row_at][None]
                sgrad = frac(before, key_at, row_at) * sgrad
                sgrads[key_at, row_at] = sgrad.reshape(SUB, SUB).astype(BF16)

        return [functools.partial(chain, *unit) for unit in units(piece)]

    def weight_chains(now, piece):
        def chain(u, r, key_at, row_at):
            weight = frac(now, key_at, row_at).reshape(SUB, SUB)
            weights[now][key_at, row_at] = weight.astype(BF16)

        return [functools.partial(chain, *block) for block in blocks(piece)]

    def grad_products(before, piece):
        at, size, row = pieces[piece]

        key_at = slice(at, at + size)

        def value_product():
            dv_sum[key_at, :] += dot(weights[before][key_at, row:], grad[before, row:, :])

        def key_product():
            dk_sum[key_at, :] += dot(sgrads[key_at, row:], query[before, row:, :])

        return [value_product, key_product]

    def query_products(before):
        def product(r):
            dquery = (factor * dot(keys_t[...], sgrads[:, r : r + WIDE])).T.astype(BF16)
            if before:
                dq_ref[r : r + WIDE, HD:] = dquery
                dq_ref[r : r + WIDE, :HD] = held[r : r + WIDE, :]
            else:
                held[r : r + WIDE, :] = dquery

        return [functools.partial(product, r) for r in range(0, rows, WIDE)]

    def out_products(now, piece):
        at, size, row = pieces[piece]

        def product(r):
            term = dot(values_t[:, at : at + size], weights[now][at : at + size, r : r + WIDE])
            if piece:
                term += mixture[:, r : r + WIDE]
            mixture[:, r : r + WIDE] = term

        return [functools.partial(product, r) for r in range(row, rows, WIDE)]

    def weave(products, chains):
        count = max(len(products), len(chains))
        for i in range(count):
            for jobs in (products, chains):
                for job in jobs[i * len(jobs) // count : (i + 1) * len(jobs) // count]:
                    job()

    def run(now, with_score, with_grad):
        before = 1 - now
        for stage in range(count):
            products, chains = [], []
            if stage >= 1 and with_grad:
                products += grad_products(before, stage - 1)
            both = [score_chains(now, stage)] if with_score else []
            both += [grad_chains(before, stage)] if with_grad else []
            chains = [chain for pair in zip(*both) for chain in pair]
            weave(products, chains)
        products = []
        if with_grad:
            products += grad_products(before, count - 1) + query_products(before)
        chains = []
        if with_score:
            set_fracs(now)
            chains = weight_chains(now, 0)
        weave(products, chains)
        if with_score:
            for piece in range(count):
                weave(
                    out_products(now, piece),
                    weight_chains(now, piece + 1) if piece + 1 < count else [],
                )
            finish(now)

    def prepare(now):
        columns = slice(now * HD, (now + 1) * HD)
        live_rows = lax.broadcasted_iota(jnp.int32, (rows, HD), 0) < length
        live_grad = jnp.where(live_rows, g_ref[:, columns].astype(F32), 0.0)
        grad[now] = live_grad.astype(BF16)
        grad_t[now] = live_grad.T.astype(BF16)
        query[now] = q_ref[:, columns]
        query_t[now] = q_ref[:, columns].T

    def set_fracs(now):
        top = jnp.max(tops[...], axis=0, keepdims=True)
        scale = jnp.exp2(tops[...] - top)
        total = jnp.sum(scale * sums[...], axis=0, keepdims=True)
        fracs[now] = scale * (1.0 / total)

    def finish(now):
        live_lanes = lax.broadcasted_iota(jnp.int32, (HD, rows), 1) < length
        attended = jnp.where(live_lanes, mixture[...], 0.0).astype(BF16).astype(F32)
        out_ref[:, now * HD : (now + 1) * HD] = attended.T.astype(BF16)
        delta = jnp.sum(grad_t[now].astype(F32) * attended, axis=0, keepdims=True)
        deltas[now] = jnp.broadcast_to(delta, (8, rows))

    steps = heads_per // 2

    @pl.when(step == 0)
    def _():
        init()
        prepare(0)
        run(0, True, False)

    @pl.when((step > 0) & (step < steps))
    def _():
        prepare(0)
        run(0, True, True)

    @pl.when(step < steps)
    def _():
        prepare(1)
        run(1, True, True)

    @pl.when(step == steps)
    def _():
        run(0, False, True)
        layout.store(dcaches, dk_sum, dv_sum, factor)
        at = pl.ds(prompt_rows, rows)
        dkr_ref[...] = (factor * dk_sum[at, :]).astype(BF16)
        dvr_ref[...] = dv_sum[at, :].astype(BF16)


class Gathered:
    def __init__(self, members, part_rows):
        self.members, self.part_rows = members, part_rows
        self.prompt_rows = members * part_rows
        self.share = part_rows // 2
        self.caches, self.dcaches = 1, members + 1

    def cache_shapes(self):
        return [(self.members, 2, self.part_rows, HD)]

    def dcache_shapes(self):
        shape = (self.part_rows + self.share, HD)
        return [shape] * self.members + [(self.members, self.part_rows - self.share, HD)]

    def load(self, caches):
        for m in range(self.members):
            at = pl.ds(m * self.part_rows, self.part_rows)
            yield at, caches[0][m, 0], caches[0][m, 1]

    def store(self, dcaches, dk_sum, dv_sum, factor):
        me = lax.axis_index("resp")
        for shift in range(self.members):
            part = pl.multiple_of(lax.rem(me + shift, self.members) * self.part_rows, self.part_rows)
            key_at, value_at = pl.ds(part, self.part_rows), pl.ds(part, self.share)
            dcaches[shift][: self.part_rows, :] = (factor * dk_sum[key_at, :]).astype(BF16)
            dcaches[shift][self.part_rows :, :] = dv_sum[value_at, :].astype(BF16)
            at = pl.ds(shift * self.part_rows + self.share, self.part_rows - self.share)
            dcaches[self.members][shift] = dv_sum[at, :].astype(BF16)


class Scattered(Gathered):
    def __init__(self, members, part_rows):
        super().__init__(members, part_rows)
        self.caches, self.dcaches = members, 1

    def cache_shapes(self):
        return [(2, self.part_rows, HD)] * self.members

    def dcache_shapes(self):
        return super().cache_shapes()

    def load(self, caches):
        for shift, ref in enumerate(caches):
            yield pl.ds(shift * self.part_rows, self.part_rows), ref[0], ref[1]

    def store(self, dcaches, dk_sum, dv_sum, factor):
        me = lax.axis_index("resp")
        for shift in range(self.members):
            part = lax.rem(me - shift + self.members, self.members)
            at = pl.ds(shift * self.part_rows, self.part_rows)
            dcaches[0][part, 0] = (factor * dk_sum[at, :]).astype(BF16)
            dcaches[0][part, 1] = dv_sum[at, :].astype(BF16)


def attend(
    layout, pair, heads_per, lengths, queries, out_grad, caches, resp_keys, resp_values, earlier
):
    rows, query_width = queries.shape
    total_rows = layout.prompt_rows + rows
    steps = heads_per // 2
    first, last = pair * steps, (pair + 1) * steps - 1
    head_block = pl.BlockSpec((rows, 2 * HD), lambda s: (0, jnp.minimum(first + s, last)))
    late_block = pl.BlockSpec((rows, 2 * HD), lambda s: (0, jnp.maximum(first + s - 1, first)))
    pair_block = pl.BlockSpec((rows, HD), lambda s: (0, pair))
    cache_blocks = [
        pl.BlockSpec(shape, lambda s, rank=len(shape): (0,) * rank)
        for shape in layout.cache_shapes()
    ]
    dcache_blocks = [
        pl.BlockSpec(shape, lambda s, rank=len(shape): (0,) * rank)
        for shape in layout.dcache_shapes()
    ]
    stats = total_rows // SUB * 8
    in_specs = [
        pl.BlockSpec(memory_space=pltpu.SMEM),
        head_block,
        head_block,
        pair_block,
        pair_block,
        *cache_blocks,
    ] + [pl.BlockSpec(memory_space=pl.ANY)] * len(earlier)
    aliases = {5 + layout.caches + i: i for i in range(len(earlier))}
    return pl.pallas_call(
        functools.partial(attention_kernel, layout, heads_per, len(earlier)),
        grid=(steps + 1,),
        in_specs=in_specs,
        out_specs=[head_block, late_block, pair_block, pair_block, *dcache_blocks],
        out_shape=[
            jax.ShapeDtypeStruct(queries.shape, BF16),
            jax.ShapeDtypeStruct(queries.shape, BF16),
            jax.ShapeDtypeStruct(resp_keys.shape, BF16),
            jax.ShapeDtypeStruct(resp_keys.shape, BF16),
            *[jax.ShapeDtypeStruct(shape, BF16) for shape in layout.dcache_shapes()],
        ],
        scratch_shapes=[
            pltpu.VMEM((total_rows, HD), BF16),
            pltpu.VMEM((total_rows, HD), BF16),
            pltpu.VMEM((HD, total_rows), BF16),
            pltpu.VMEM((HD, total_rows), BF16),
            pltpu.VMEM((2, rows, HD), BF16),
            pltpu.VMEM((2, HD, rows), BF16),
            pltpu.VMEM((2, rows, HD), BF16),
            pltpu.VMEM((2, HD, rows), BF16),
            pltpu.VMEM((total_rows, rows), F32),
            pltpu.VMEM((total_rows, rows), F32),
            pltpu.VMEM((total_rows, rows), BF16),
            pltpu.VMEM((total_rows, rows), BF16),
            pltpu.VMEM((total_rows, rows), BF16),
            pltpu.VMEM((2, stats, rows), F32),
            pltpu.VMEM((2, 8, rows), F32),
            pltpu.VMEM((total_rows, HD), F32),
            pltpu.VMEM((total_rows, HD), F32),
            pltpu.VMEM((stats, rows), F32),
            pltpu.VMEM((stats, rows), F32),
            pltpu.VMEM((HD, rows), F32),
            pltpu.VMEM((rows, HD), BF16),
        ],
        input_output_aliases=aliases,
        cost_estimate=pl.CostEstimate(
            flops=12 * heads_per * rows * total_rows * HD,
            bytes_accessed=8 * heads_per * rows * HD,
            transcendentals=heads_per * rows * total_rows,
        ),
        compiler_params=pltpu.CompilerParams(vmem_limit_bytes=60 * 1024 * 1024),
        name=f"attend_pair_{pair}",
    )(lengths, queries, out_grad, resp_keys, resp_values, *caches, *earlier)


def whole_block(shape):
    return pl.BlockSpec(shape, lambda: (0,) * len(shape))


def cut_kernel(pairs, k_ref, v_ref, *outs):
    me = lax.axis_index("tensor")
    ranks = len(outs) // pairs
    for p in range(pairs):
        for i in range(ranks):
            columns = pl.ds(pl.multiple_of(((me ^ i) * pairs + p) * HD, HD), HD)
            outs[p * ranks + i][0] = k_ref[:, columns]
            outs[p * ranks + i][1] = v_ref[:, columns]


def cut(prompt_keys, prompt_values, pairs):
    rows, columns = prompt_keys.shape
    count = columns // HD
    blocks = pl.pallas_call(
        functools.partial(cut_kernel, pairs),
        in_specs=[whole_block((rows, columns))] * 2,
        out_specs=[whole_block((2, rows, HD))] * count,
        out_shape=[jax.ShapeDtypeStruct((2, rows, HD), BF16)] * count,
        name="cut",
    )(prompt_keys, prompt_values)
    return [blocks[p * count // pairs : (p + 1) * count // pairs] for p in range(pairs)]


def place_kernel(pairs, *refs):
    *ins, dk_ref, dv_ref = refs
    me = lax.axis_index("tensor")
    ranks = len(ins) // pairs
    for p in range(pairs):
        for i in range(ranks):
            columns = pl.ds(pl.multiple_of(((me ^ i) * pairs + p) * HD, HD), HD)
            dk_ref[:, columns] = ins[p * ranks + i][0].astype(F32)
            dv_ref[:, columns] = ins[p * ranks + i][1].astype(F32)


def place(blocks, pairs, columns):
    _, rows, _ = blocks[0].shape
    shape = (rows, columns)
    return pl.pallas_call(
        functools.partial(place_kernel, pairs),
        in_specs=[whole_block(blocks[0].shape)] * len(blocks),
        out_specs=[whole_block(shape)] * 2,
        out_shape=[jax.ShapeDtypeStruct(shape, F32)] * 2,
        name="place",
    )(*blocks)


def swap(blocks):
    count = len(blocks)
    return [blocks[0]] + [
        lax.ppermute(blocks[i], "tensor", [(j, j ^ i) for j in range(count)])
        for i in range(1, count)
    ]


def send(block, members, shift):
    return lax.ppermute(block, "resp", [(m, (m + shift) % members) for m in range(members)])


def cut_rows(block, count):
    rows = block.shape[1] // count
    return [block[:, i * rows : (i + 1) * rows] for i in range(count)]


def per_device(
    members, ranks, queries, resp_keys, resp_values, prompt_keys, prompt_values, out_grad, lengths
):
    query_width = queries.shape[2]
    pair_width = resp_keys.shape[2]
    pairs = pair_width // HD
    heads_per = query_width // pair_width
    own_rows, columns = prompt_keys.shape
    queries, out_grad, resp_keys, resp_values = (
        a[0] for a in (queries, out_grad, resp_keys, resp_values)
    )
    cuts = cut(prompt_keys, prompt_values, pairs)
    kinds = [Scattered(members, ranks * own_rows)]
    kinds += [Gathered(members, ranks * own_rows) for _ in range(pairs - 1)]
    own = jnp.concatenate(swap(cuts[0]), axis=1)
    if pairs > 1:
        own, cuts[1:] = lax.optimization_barrier((own, cuts[1:]))
    caches = [[own] + [send(own, members, shift) for shift in range(1, members)]]
    for p in range(1, pairs):
        own = jnp.concatenate(swap(cuts[p]), axis=1)
        own, caches[0] = lax.optimization_barrier((own, caches[0]))
        caches.append([lax.all_gather(own, "resp", axis=0)])
    earlier = ()
    totals = []
    for p in range(pairs):
        results = attend(
            kinds[p],
            p,
            heads_per,
            lengths,
            queries,
            out_grad,
            caches[p],
            resp_keys,
            resp_values,
            earlier,
        )
        earlier, dcaches = results[:4], results[4:]
        if totals:
            dcaches, totals[-1] = lax.optimization_barrier((dcaches, totals[-1]))
        if isinstance(kinds[p], Scattered):
            totals.append(lax.psum_scatter(dcaches[0], "resp", scatter_dimension=0))
        else:
            arrived = [dcaches[0]] + [
                send(dcaches[shift], members, shift) for shift in range(1, members)
            ]
            both = sum(block.astype(F32) for block in arrived).astype(BF16)
            rest = lax.psum_scatter(dcaches[members], "resp", scatter_dimension=0)
            parts = ranks * own_rows
            keys, both = both[:parts], both[parts:]
            split = both.shape[0] // own_rows
            values = [both[i * own_rows : (i + 1) * own_rows] for i in range(split)]
            values += [rest[i * own_rows : (i + 1) * own_rows] for i in range(ranks - split)]
            pieces = [keys[i * own_rows : (i + 1) * own_rows] for i in range(ranks)]
            totals.append([jnp.stack(both) for both in zip(pieces, values)])
    blocks = []
    for total in totals:
        blocks += swap(total if isinstance(total, list) else cut_rows(total, ranks))
    key_grad, value_grad = place(blocks, pairs, columns)
    return (*(a[None] for a in earlier), key_grad, value_grad)


def solution(mesh):
    rows = P(("group", "resp"), None, "tensor")
    prompt = P(("group", "resp", "tensor"), None)
    return jax.shard_map(
        functools.partial(per_device, mesh.shape["resp"], mesh.shape["tensor"]),
        mesh=mesh,
        in_specs=(rows, rows, rows, prompt, prompt, rows, P(("group", "resp"))),
        out_specs=(rows, rows, rows, rows, prompt, prompt),
        check_vma=False,
    )
```
